32 devices in a mesh: dp: 16 (over z, y, core), tensor: 2 (over x).
Axes of the slice: x: 2, y: 2, z: 4, core: 2. Of those that a mesh axis runs over, the one named last changes fastest.
Arguments:
- tokens: bfloat16 [25088, 512], P(('dp', 'tensor')), may hold values from -6 to 6
- cotangent: bfloat16 [25088, 512], P(('dp', 'tensor')), may hold values from -6 to 6
- image_counts: int32 [16], replicated, may hold values from 2 to 8, as said below
- w_in: float32 [512, 1536], P(None, 'tensor'), may hold values from -0.25 to 0.25
- m_in: float32 [512, 1536], P(None, 'tensor'), may hold values from -448 to 448
- v_in: float32 [512, 1536], P(None, 'tensor'), may hold values from 2007.04 to 8028.16
- w_out: float32 [512, 512], P('tensor'), may hold values from -1.5 to 1.5
- m_out: float32 [512, 512], P('tensor'), may hold values from -168 to 168
- v_out: float32 [512, 512], P('tensor'), may hold values from 282.24 to 1128.96
- w_up: float32 [512, 2048], P(None, 'tensor'), may hold values from -0.25 to 0.25
- m_up: float32 [512, 2048], P(None, 'tensor'), may hold values from -336 to 336
- v_up: float32 [512, 2048], P(None, 'tensor'), may hold values from 1128.96 to 4515.84
- w_down: float32 [2048, 512], P('tensor'), may hold values from -0.125 to 0.125
- m_down: float32 [2048, 512], P('tensor'), may hold values from -672 to 672
- v_down: float32 [2048, 512], P('tensor'), may hold values from 4515.84 to 18063.36
- kernel: float32 [9, 512], P(None, 'tensor'), may hold values from -12 to 12
- m_kernel: float32 [9, 512], P(None, 'tensor'), may hold values from -224 to 224
- v_kernel: float32 [9, 512], P(None, 'tensor'), may hold values from 501.76 to 2007.04
- up_bias: float32 [2048], P('tensor'), may hold values from -1.5 to 1.5
- m_bias: float32 [2048], P('tensor'), may hold values from -336 to 336
- v_bias: float32 [2048], P('tensor'), may hold values from 1128.96 to 4515.84
- vectors: float32 [7, 512], replicated, may hold values from -0.9 to 1.45
- m_vectors: float32 [7, 512], P(None, 'tensor'), may hold values from -784 to 784
- v_vectors: float32 [7, 512], P(None, 'tensor'), may hold values from 6146.56 to 24586.24
Outputs:
- output: bfloat16 [25088, 512], P(('dp', 'tensor'))
- grad_in: float32 [25088, 512], P(('dp', 'tensor'))
- new_w_in: float32 [512, 1536], P(None, 'tensor')
- new_m_in: float32 [512, 1536], P(None, 'tensor')
- new_v_in: float32 [512, 1536], P(None, 'tensor')
- copy_w_in: bfloat16 [512, 1536], P(None, 'tensor')
- new_w_out: float32 [512, 512], P('tensor')
- new_m_out: float32 [512, 512], P('tensor')
- new_v_out: float32 [512, 512], P('tensor')
- copy_w_out: bfloat16 [512, 512], P('tensor')
- new_w_up: float32 [512, 2048], P(None, 'tensor')
- new_m_up: float32 [512, 2048], P(None, 'tensor')
- new_v_up: float32 [512, 2048], P(None, 'tensor')
- copy_w_up: bfloat16 [512, 2048], P(None, 'tensor')
- new_w_down: float32 [2048, 512], P('tensor')
- new_m_down: float32 [2048, 512], P('tensor')
- new_v_down: float32 [2048, 512], P('tensor')
- copy_w_down: bfloat16 [2048, 512], P('tensor')
- new_kernel: float32 [9, 512], P(None, 'tensor')
- new_m_kernel: float32 [9, 512], P(None, 'tensor')
- new_v_kernel: float32 [9, 512], P(None, 'tensor')
- new_up_bias: float32 [2048], P('tensor')
- new_m_bias: float32 [2048], P('tensor')
- new_v_bias: float32 [2048], P('tensor')
- new_vectors: float32 [7, 512], P(None, 'tensor')
- new_m_vectors: float32 [7, 512], P(None, 'tensor')
- new_v_vectors: float32 [7, 512], P(None, 'tensor')
The draws below stay inside these ranges and needn't reach their ends.
Inputs may be any that keep to these rules, and one draw needn't show every extreme that they name: image_counts[i] images of dp group i are live, in its first slots; some group has all 8 slots live and some group the fewest.
All inputs are finite; a program needn't handle non-finite values.
Results may differ from the reference program's by a relative error of at most 0.01145.
The reference program's roundings to bfloat16 on the way count: a program that leaves them out, or rounds other values in their place, can miss the bound.
Values may be sent and summed in bfloat16 or wider, within the bound.
A program may use at most 192 MiB of HBM per device.

```python
import math
import jax
import jax.numpy as jnp
from jax import lax

D = 512
HEADS = 16
HD = 32
FF = 2048
SIDE = 14
STEP = 5
IMG_CAP = 8
TOKENS = 25088
LIVE = 12544
N_DP = 16


def draw_image_counts(key, part):
    key = jax.random.fold_in(key, 11)
    count_key, ranking_key = jax.random.split(key)
    lowest = max(1, IMG_CAP // 4)
    counts = jax.random.randint(count_key, (N_DP,), lowest, IMG_CAP * 3 // 4 + 1, dtype=jnp.int32)
    ranking = jax.random.permutation(ranking_key, N_DP)
    counts = counts.at[ranking[0]].set(IMG_CAP)
    counts = counts.at[ranking[1]].set(lowest)
    return counts


def draw_vectors(key, part):
    key = jax.random.fold_in(key, 7)
    centres = jnp.array([1.0, 0.0, 1.0, 0.0, 1.0, 1.0, 0.0], jnp.float32)
    widths = jnp.array([0.15, 0.3, 0.15, 0.3, 0.15, 0.15, 0.3], jnp.float32)
    base = jnp.clip(jax.random.normal(key, (7, D), jnp.float32), -3.0, 3.0)
    return centres[:, None] + widths[:, None] * base


def shard_levels(stream_key, extent, cuts, smallest, largest):
    level, own = 1.0, jax.random.fold_in(stream_key, 6)
    for dim, blocks in cuts:
        steps = jnp.exp(jax.random.uniform(jax.random.fold_in(own, dim), (blocks,), jnp.float32, smallest / len(cuts), largest / len(cuts)))
        level = level * jnp.repeat(steps, extent[dim] // blocks).reshape([-1 if axis == dim else 1 for axis in range(len(extent))])
    return level


def normal_values(stream_key, shape, scale, most, cuts=(), kind=jnp.bfloat16):
    values = scale * jax.random.normal(stream_key, shape, jnp.float32)
    if cuts:
        values = values * shard_levels(stream_key, shape, cuts, -0.22, 0.18)
    return jnp.clip(values, -most, most).astype(kind)


def setup_inputs(seed: int = 0) -> dict:
    key_list = jax.random.split(jax.random.key(seed), 25)
    return {
        "tokens": normal_values(key_list[0], (TOKENS, D), 1.0, 6.0, ((0, 32),)),
        "cotangent": normal_values(key_list[1], (TOKENS, D), 1.0, 6.0, ((0, 32),)),
        "image_counts": draw_image_counts(jax.random.fold_in(key_list[24], 71), 0),
        "w_in": normal_values(key_list[3], (D, 3 * D), D ** -0.5, 0.25, ((1, 2),), jnp.float32),
        "m_in": normal_values(key_list[4], (D, 3 * D), (0.4 * LIVE ** 0.5), 448.0, ((1, 2),), jnp.float32),
        "v_in": jnp.clip(jnp.exp(math.log(8028.16) - 1.3862944 * jax.random.uniform(key_list[5], (D, 3 * D), jnp.float32) ** shard_levels(key_list[5], (D, 3 * D), ((1, 2),), -0.2, 0.2)), 2007.04, 8028.16),
        "w_out": normal_values(key_list[6], (D, D), (D // 32) ** -0.5, 1.5, ((0, 2),), jnp.float32),
        "m_out": normal_values(key_list[7], (D, D), (0.15 * LIVE ** 0.5), 168.0, ((0, 2),), jnp.float32),
        "v_out": jnp.clip(jnp.exp(math.log(1128.96) - 1.3862944 * jax.random.uniform(key_list[8], (D, D), jnp.float32) ** shard_levels(key_list[8], (D, D), ((0, 2),), -0.2, 0.2)), 282.24, 1128.96),
        "w_up": normal_values(key_list[9], (D, FF), D ** -0.5, 0.25, ((1, 2),), jnp.float32),
        "m_up": normal_values(key_list[10], (D, FF), (0.3 * LIVE ** 0.5), 336.0, ((1, 2),), jnp.float32),
        "v_up": jnp.clip(jnp.exp(math.log(4515.84) - 1.3862944 * jax.random.uniform(key_list[11], (D, FF), jnp.float32) ** shard_levels(key_list[11], (D, FF), ((1, 2),), -0.2, 0.2)), 1128.96, 4515.84),
        "w_down": normal_values(key_list[12], (FF, D), FF ** -0.5, 0.125, ((0, 2),), jnp.float32),
        "m_down": normal_values(key_list[13], (FF, D), (0.6 * LIVE ** 0.5), 672.0, ((0, 2),), jnp.float32),
        "v_down": jnp.clip(jnp.exp(math.log(18063.36) - 1.3862944 * jax.random.uniform(key_list[14], (FF, D), jnp.float32) ** shard_levels(key_list[14], (FF, D), ((0, 2),), -0.2, 0.2)), 4515.84, 18063.36),
        "kernel": normal_values(key_list[15], (9, D), 3.0, 12.0, ((1, 2),), jnp.float32),
        "m_kernel": normal_values(key_list[16], (9, D), (0.2 * LIVE ** 0.5), 224.0, ((1, 2),), jnp.float32),
        "v_kernel": jnp.clip(jnp.exp(math.log(2007.04) - 1.3862944 * jax.random.uniform(key_list[17], (9, D), jnp.float32) ** shard_levels(key_list[17], (9, D), ((1, 2),), -0.2, 0.2)), 501.76, 2007.04),
        "up_bias": normal_values(key_list[18], (FF,), 0.3, 1.5, ((0, 2),), jnp.float32),
        "m_bias": normal_values(key_list[19], (FF,), (0.3 * LIVE ** 0.5), 336.0, ((0, 2),), jnp.float32),
        "v_bias": jnp.clip(jnp.exp(math.log(4515.84) - 1.3862944 * jax.random.uniform(key_list[20], (FF,), jnp.float32) ** shard_levels(key_list[20], (FF,), ((0, 2),), -0.2, 0.2)), 1128.96, 4515.84),
        "vectors": draw_vectors(jax.random.fold_in(key_list[24], 71), 0),
        "m_vectors": normal_values(key_list[22], (7, D), (0.7 * LIVE ** 0.5), 784.0, ((1, 2),), jnp.float32),
        "v_vectors": jnp.clip(jnp.exp(math.log(24586.24) - 1.3862944 * jax.random.uniform(key_list[23], (7, D), jnp.float32) ** shard_levels(key_list[23], (7, D), ((1, 2),), -0.2, 0.2)), 6146.56, 24586.24),
    }


highest = lax.Precision.HIGHEST
beta_one = 0.5
beta_two = 0.5
epsilon = 1e-08
decay = 0.05
norm_eps = 1e-05

@jax.custom_vjp
def low(v):
    return lax.optimization_barrier(v.astype(jnp.bfloat16)).astype(jnp.float32)

@jax.custom_vjp
def low_back(v):
    return v

def low_keep(v):
    return (low(v), None)

def low_pass(kept, grad):
    return (grad,)

def back_keep(v):
    return (v, None)

def back_low(kept, grad):
    return (low(grad),)
low.defvjp(low_keep, low_pass)
low_back.defvjp(back_keep, back_low)

def matmul(left_side, right_side):
    return jnp.dot(left_side, right_side, precision=highest, preferred_element_type=jnp.float32)

def layer_norm(values, gain_row, shift_row):
    centred = values - lax.optimization_barrier(jnp.mean(values, axis=-1, keepdims=True))
    variance = lax.optimization_barrier(jnp.mean(centred * centred, axis=-1, keepdims=True))
    return centred * lax.rsqrt(variance + norm_eps) * gain_row + shift_row

def spatial(grid_field, tap_table):
    padded = jnp.pad(grid_field, ((0, 0), (1, 1), (1, 1), (0, 0)))
    summed = jnp.zeros_like(grid_field)
    for row_step in range(3):
        for col_step in range(3):
            summed = summed + tap_table[3 * row_step + col_step] * padded[:, row_step:row_step + SIDE, col_step:col_step + SIDE, :]
    return summed

def generate(gen_pre, kernel):
    image_count, window, channels = gen_pre.shape
    grid_field = jax.nn.gelu(gen_pre).reshape(image_count, SIDE, SIDE, channels)
    convolved = spatial(grid_field, kernel)
    pooled = spatial(convolved, jnp.full((9, channels), 1.0 / 9.0, jnp.float32))
    return pooled.reshape(image_count, window, channels) * HD ** (-0.5)

def layer(inputs, live_block, weights):
    w_in, w_out, w_up, w_down, kernel, up_bias, vectors = weights
    image_count = inputs.shape[0]
    window = SIDE * SIDE
    norm_a = low(layer_norm(inputs, vectors[0], vectors[1]))
    proj = low_back(matmul(norm_a, low(w_in))).reshape(image_count, window, HEADS, 3, HD)
    gen_pre = proj[:, :, :, 0, :].reshape(image_count, window, D)
    keys = low(proj[:, :, :, 1, :])
    values = low(proj[:, :, :, 2, :])
    queries = low(generate(gen_pre, kernel)).reshape(image_count, window, HEADS, HD)
    scores = low_back(jnp.einsum('nqhc,nkhc->nhqk', queries, keys, precision=highest))
    probs = low(jax.nn.softmax(scores, axis=-1))
    mixed = jnp.einsum('nhqk,nkhc->nqhc', probs, values, precision=highest)
    mixed = low_back(low(mixed)).reshape(image_count, window, D)
    attn = low_back(matmul(mixed, low(w_out)))
    after_attn = inputs + vectors[4] * attn
    norm_b = low(layer_norm(after_attn, vectors[2], vectors[3]))
    pre_hidden = low_back(matmul(norm_b, low(w_up)) + up_bias)
    hidden = low(jax.nn.gelu(pre_hidden))
    branch = low_back(matmul(hidden, low(w_down)))
    finished = after_attn + vectors[5] * (branch + vectors[6])
    return finished * live_block[:, None, None]

def rates():
    return ((D ** (-0.5), decay), ((D // 32) ** (-0.5), decay), (D ** (-0.5), decay), (FF ** (-0.5), decay), (2.0, decay), (0.3, 0.0), (0.3, 0.0))

def adam_step(weight, first_moment, second, gradient, setting):
    step_rate, shrink = setting
    first_moment = beta_one * first_moment + (1.0 - beta_one) * gradient
    second = beta_two * second + (1.0 - beta_two) * gradient * gradient
    first_hat = first_moment / (1.0 - beta_one ** STEP)
    second_hat = second / (1.0 - beta_two ** STEP)
    weight = weight - step_rate * (first_hat / (jnp.sqrt(second_hat) + epsilon) + shrink * weight)
    return (weight, first_moment, second)

def reference(tokens, cotangent, image_counts, w_in, m_in, v_in, w_out, m_out, v_out, w_up, m_up, v_up, w_down, m_down, v_down, kernel, m_kernel, v_kernel, up_bias, m_bias, v_bias, vectors, m_vectors, v_vectors):
    window = SIDE * SIDE
    image_total = TOKENS // window
    images = tokens.astype(jnp.float32).reshape(image_total, window, D)
    cotan_images = cotangent.astype(jnp.float32).reshape(image_total, window, D)
    image_index = jnp.arange(image_total, dtype=jnp.int32)
    group_index = (image_index // IMG_CAP).astype(jnp.int32)
    live_images = (image_index % IMG_CAP < image_counts[group_index]).astype(jnp.float32)
    block = 16 if image_total % 16 == 0 else 8
    blocks = image_total // block
    params = (w_in, w_out, w_up, w_down, kernel, up_bias, vectors)

    def visit(totals, pieces):
        image_block, cotan_block, live_block = pieces

        def forward(inputs, weights):
            return layer(inputs, live_block, weights)
        finished, pull = jax.vjp(forward, image_block, params)
        input_grad, weight_grads = pull(cotan_block)
        totals = tuple((summed + piece for summed, piece in zip(totals, weight_grads)))
        return (totals, (finished.astype(jnp.bfloat16), input_grad))
    zeros = tuple((jnp.zeros_like(weight) for weight in params))
    totals, (outputs, input_grads) = lax.scan(visit, zeros, (images.reshape(blocks, block, window, D), cotan_images.reshape(blocks, block, window, D), live_images.reshape(blocks, block)))
    g_in, g_out, g_up, g_down, g_kernel, g_bias, g_vectors = totals
    rate_table = rates()
    new_w_in, new_m_in, new_v_in = adam_step(w_in, m_in, v_in, g_in, rate_table[0])
    new_w_out, new_m_out, new_v_out = adam_step(w_out, m_out, v_out, g_out, rate_table[1])
    new_w_up, new_m_up, new_v_up = adam_step(w_up, m_up, v_up, g_up, rate_table[2])
    new_w_down, new_m_down, new_v_down = adam_step(w_down, m_down, v_down, g_down, rate_table[3])
    new_kernel, new_m_kernel, new_v_kernel = adam_step(kernel, m_kernel, v_kernel, g_kernel, rate_table[4])
    new_up_bias, new_m_bias, new_v_bias = adam_step(up_bias, m_bias, v_bias, g_bias, rate_table[5])
    new_vectors, new_m_vectors, new_v_vectors = adam_step(vectors, m_vectors, v_vectors, g_vectors, rate_table[6])
    return (outputs.reshape(TOKENS, D), input_grads.reshape(TOKENS, D), new_w_in, new_m_in, new_v_in, new_w_in.astype(jnp.bfloat16), new_w_out, new_m_out, new_v_out, new_w_out.astype(jnp.bfloat16), new_w_up, new_m_up, new_v_up, new_w_up.astype(jnp.bfloat16), new_w_down, new_m_down, new_v_down, new_w_down.astype(jnp.bfloat16), new_kernel, new_m_kernel, new_v_kernel, new_up_bias, new_m_bias, new_v_bias, new_vectors, new_m_vectors, new_v_vectors)
```

```python
import functools
import jax
import jax.numpy as jnp
from jax import lax
from jax.experimental import pallas as pl
from jax.experimental.pallas import tpu as pltpu
from jax.sharding import PartitionSpec as P

D = 512
HD = 32
FF = 2048
SIDE = 14
WIDE = 16
WIN = SIDE * SIDE
ROWS = SIDE * WIDE
KEYS = 256
GROUPS = D // 128
STEP = 5
DOWN, UP, OUT, IN, GROWS = 0, 2048, 4096, 4608, 6144
MESH = pl.DeviceIdType.MESH
eps = 1e-05
f32 = jnp.float32
bf16 = jnp.bfloat16
C0 = 0.7978845608028654
C1 = 0.044715


def nn(a, b):
    return lax.dot_general(a, b, (((1,), (0,)), ((), ())), preferred_element_type=f32)


def nt(a, b):
    return lax.dot_general(a, b, (((1,), (1,)), ((), ())), preferred_element_type=f32)


def tn(a, b):
    return lax.dot_general(a, b, (((0,), (0,)), ((), ())), preferred_element_type=f32)


def normed(x):
    c = x - jnp.mean(x, axis=-1, keepdims=True)
    r = lax.rsqrt(jnp.mean(c * c, axis=-1, keepdims=True) + eps)
    return c * r, r


def norm_back(u, xhat, r):
    return r * (
        u
        - jnp.mean(u, axis=-1, keepdims=True)
        - xhat * jnp.mean(u * xhat, axis=-1, keepdims=True)
    )


def gelu_pair(x):
    x2 = x * x
    t = jnp.tanh(x * (C0 + (C0 * C1) * x2))
    h = 0.5 + 0.5 * t
    slope = h + (0.5 * x) * ((1.0 - t * t) * (C0 + (3.0 * C0 * C1) * x2))
    return x * h, slope


def gelu(x):
    return x * (0.5 + 0.5 * jnp.tanh(x * (C0 + (C0 * C1) * (x * x))))


def row_sum(x):
    return jnp.sum(x, axis=0, keepdims=True)


def shift_rows(x, by):
    z = jnp.zeros((abs(by), x.shape[1]), x.dtype)
    if by > 0:
        return jnp.concatenate([z, x[:-by]], axis=0)
    return jnp.concatenate([x[-by:], z], axis=0)


def roll1(x, by):
    return pltpu.roll(x, by % x.shape[0], 0)


def pool(c):
    s = c + roll1(c, 1) + roll1(c, -1)
    return s + shift_rows(s, WIDE) + shift_rows(s, -WIDE)


def block_kernel(images, lim, tok, cot, wi, wo, wu, wd, small, vecs,
           out, gin, grads, gsmall,
           x_s, co_s, gp_s, at_s, af_s, da_s, na_s, q_s, mx_s, nb_s, lb_s, la_s, dm_s,
           k_s, v_s, hd_s, dp_s, pj_s, p_s, mf_s, taps):
    limit = lim[0]
    v0, v1, v2, v3, v4, v5, v6 = (vecs[i : i + 1, :] for i in range(7))
    gsmall[...] = jnp.zeros_like(gsmall)
    for t in range(2):
        taps[:, t * 256 : (t + 1) * 256] = small[t]

    gin[...] = tok[...].astype(f32)
    pad = jnp.zeros((WIDE - SIDE, D), f32)
    for i in range(images * SIDE):
        x_s[i * WIDE : i * WIDE + SIDE, :] = gin[i * SIDE : (i + 1) * SIDE, :]
        x_s[i * WIDE + SIDE : (i + 1) * WIDE, :] = pad
    gin[...] = cot[...].astype(f32)
    for n in range(images):
        live = (n < limit).astype(f32)
        for i in range(n * SIDE, (n + 1) * SIDE):
            co_s[i * WIDE : i * WIDE + SIDE, :] = gin[i * SIDE : (i + 1) * SIDE, :] * live
            co_s[i * WIDE + SIDE : (i + 1) * WIDE, :] = pad

    cell = lax.broadcasted_iota(jnp.int32, (ROWS, 1), 0)
    inside = lax.rem(cell, WIDE) < SIDE
    lane = lax.broadcasted_iota(jnp.int32, (1, 128), 1)
    head_masks = [(lane // HD) == h for h in range(4)]
    key_row = lax.broadcasted_iota(jnp.int32, (KEYS, 128), 0)
    key_lane = lax.broadcasted_iota(jnp.int32, (KEYS, 128), 1)
    key_pad = (lax.rem(key_row, WIDE) >= SIDE) | (key_row >= ROWS)
    key_block = jnp.where(key_pad & (key_lane == 0), -1e30, 0.0).astype(bf16)
    one_block = jnp.where(
        lax.broadcasted_iota(jnp.int32, (ROWS, 128), 1) == 0, 1.0, 0.0
    ).astype(bf16)

    def forward(n, carry):
        rows = pl.ds(pl.multiple_of(n * ROWS, WIDE), ROWS)
        krows = pl.ds(pl.multiple_of(n * KEYS, WIDE), ROWS)
        kall = pl.ds(pl.multiple_of(n * KEYS, WIDE), KEYS)
        kend = pl.ds(pl.multiple_of(n * KEYS + ROWS, WIDE), KEYS - ROWS)
        x = x_s[rows, :]
        xhat, _ = normed(x)
        na = (xhat * v0 + v1).astype(bf16)
        na_s[rows, :] = na
        for t in range(2):
            ts = slice(t * 256, (t + 1) * 256)
            k_s[krows, ts] = nn(na, wi[t, 1]).astype(bf16)
            v_s[krows, ts] = nn(na, wi[t, 2]).astype(bf16)
        k_s[kend, :] = jnp.zeros((KEYS - ROWS, D), bf16)
        v_s[kend, :] = jnp.zeros((KEYS - ROWS, D), bf16)
        for g in range(GROUPS):
            ls = slice(g * 128, (g + 1) * 128)
            gp = nn(na, wi[g // 2, 0, :, (g % 2) * 128 : (g % 2 + 1) * 128])
            gp_s[rows, ls] = gp
            field = jnp.where(inside, gelu(gp), 0.0)
            back, ahead = roll1(field, 1), roll1(field, -1)
            conv = None
            for a in range(3):
                part = (
                    taps[3 * a : 3 * a + 1, ls] * back
                    + taps[3 * a + 1 : 3 * a + 2, ls] * field
                    + taps[3 * a + 2 : 3 * a + 3, ls] * ahead
                )
                if a != 1:
                    part = shift_rows(part, WIDE * (1 - a))
                conv = part if conv is None else conv + part
            pooled = pool(jnp.where(inside, conv, 0.0)) * (HD ** (-0.5) / 9.0)
            qg = pooled.astype(bf16)
            q_s[rows, ls] = qg
            qa = jnp.concatenate([qg, one_block], axis=1)
            kg = k_s[kall, ls]
            vg = v_s[kall, ls]
            acc = None
            for h in range(4):
                kh = jnp.concatenate(
                    [jnp.where(head_masks[h], kg, jnp.zeros_like(kg)), key_block], axis=1
                )
                s = nt(qa, kh)
                e = jnp.exp(s - jnp.max(s, axis=-1, keepdims=True))
                p = (e * (1.0 / jnp.sum(e, axis=-1, keepdims=True))).astype(bf16)
                p_s[n * 16 + (g * 4 + h)] = p
                o = nn(p, jnp.where(head_masks[h], vg, jnp.zeros_like(vg)))
                acc = o if acc is None else acc + o
            mx_s[rows, ls] = acc.astype(bf16)
            mf_s[rows, ls] = acc
        attn = nn(mx_s[rows, :], wo[...])
        at_s[rows, :] = attn
        after = x + v4 * attn
        af_s[rows, :] = after
        xhat_b, _ = normed(after)
        nb_s[rows, :] = (xhat_b * v2 + v3).astype(bf16)
        return carry

    lax.fori_loop(0, images, forward, 0)

    def feed(n, carry):
        rows = pl.ds(pl.multiple_of(n * ROWS, WIDE), ROWS)
        co = co_s[rows, :]
        d_br = v5 * co
        lb = d_br.astype(bf16)
        lb_s[rows, :] = lb
        nb = nb_s[rows, :]
        branch = None
        for c in range(4):
            cs = slice(c * 512, (c + 1) * 512)
            us = slice((c % 2) * 512, (c % 2 + 1) * 512)
            unit_bias = jnp.concatenate(
                [small[c // 2, 9 + (c % 2) * 2 + j : 10 + (c % 2) * 2 + j, :] for j in range(2)],
                axis=1,
            )
            pre = nn(nb, wu[c // 2, :, us]) + unit_bias
            value, slope = gelu_pair(pre)
            hid = value.astype(bf16)
            hd_s[rows, cs] = hid
            br = nn(hid, wd[cs, :])
            d_hid = nt(lb, wd[cs, :])
            dp = (slope * d_hid).astype(bf16)
            dp_s[rows, cs] = dp
            dn = nt(dp, wu[c // 2, :, us])
            gsmall[16 + c : 17 + c, :] += row_sum(dp.astype(f32))
            branch = br if branch is None else branch + br
            d_nb = dn if c == 0 else d_nb + dn
        after = af_s[rows, :]
        xhat, r = normed(after)
        moved = branch + v6
        live = (n < limit).astype(f32)
        af_s[rows, :] = (after + v5 * moved) * live
        gsmall[14:15, :] += row_sum(co * moved)
        gsmall[15:16, :] += row_sum(d_br)
        gsmall[11:12, :] += row_sum(d_nb * xhat)
        gsmall[12:13, :] += row_sum(d_nb)
        d_after = co + norm_back(v2 * d_nb, xhat, r)
        da_s[rows, :] = d_after
        gsmall[13:14, :] += row_sum(d_after * at_s[rows, :])
        la = (v4 * d_after).astype(bf16)
        la_s[rows, :] = la
        dm_s[rows, :] = nt(la, wo[...]).astype(bf16)
        return carry

    lax.fori_loop(0, images, feed, 0)

    for i in range(images * SIDE):
        gin[i * SIDE : (i + 1) * SIDE, :] = af_s[i * WIDE : i * WIDE + SIDE, :]
    out[...] = gin[...].astype(bf16)

    for c in range(FF // 512):
        cs = slice(c * 512, (c + 1) * 512)
        up = tn(nb_s[...], dp_s[:, cs]).astype(bf16)
        down = tn(hd_s[:, cs], lb_s[...]).astype(bf16)
        for j in range(2):
            js = slice(j * 256, (j + 1) * 256)
            first = UP + ((c % 2) * 2 + j) * 512
            grads[c // 2, first : first + 512, :] = up[:, js]
            first = DOWN + j * 1024 + (c % 2) * 512
            grads[c // 2, first : first + 512, :] = down[:, js]
    g_out = tn(mx_s[...], la_s[...]).astype(bf16)
    for t in range(2):
        for j in range(2):
            first = OUT + j * 256
            grads[t, first : first + 256, :] = g_out[t * 256 : (t + 1) * 256, j * 256 : (j + 1) * 256]

    pick_row = lax.broadcasted_iota(jnp.int32, (256, 128), 0)
    pick_lane = lax.broadcasted_iota(jnp.int32, (256, 128), 1)
    pick = jnp.where(
        (lax.rem(pick_row, 128) // HD == lax.rem(pick_lane, 4)) & (pick_lane < 8), 1.0, 0.0
    ).astype(bf16)

    def split(a):
        high = a.astype(bf16)
        return high, (a - high.astype(f32)).astype(bf16)

    def inner_block(a):
        sums = nn(jnp.concatenate(split(a), axis=1), pick)
        high, low = split(sums)
        return jnp.where(lane < 4, high, low)

    def backward(n, carry):
        rows = pl.ds(pl.multiple_of(n * ROWS, WIDE), ROWS)
        kall = pl.ds(pl.multiple_of(n * KEYS, WIDE), KEYS)
        for g in range(GROUPS):
            ls = slice(g * 128, (g + 1) * 128)
            dmg = dm_s[rows, ls]
            qg = q_s[rows, ls]
            kg = k_s[kall, ls]
            vg = v_s[kall, ls]
            dmf = dmg.astype(f32)
            left = jnp.concatenate([dmg, inner_block(dmf * mf_s[rows, ls])], axis=1)
            dmt = jnp.transpose(dmf).astype(bf16)
            qt = jnp.transpose(qg.astype(f32)).astype(bf16)
            dq = None
            dks, dvs = [], []
            for h in range(4):
                minus = jnp.where((lane == h) | (lane == h + 4), -1.0, 0.0).astype(bf16)
                right = jnp.concatenate(
                    [
                        jnp.where(head_masks[h], vg, jnp.zeros_like(vg)),
                        jnp.broadcast_to(minus, (KEYS, 128)),
                    ],
                    axis=1,
                )
                p = p_s[n * 16 + (g * 4 + h)]
                ds = (p.astype(f32) * nt(left, right)).astype(bf16)
                hs = slice(h * HD, (h + 1) * HD)
                part = nn(ds, jnp.where(head_masks[h], kg, jnp.zeros_like(kg)))
                dq = part if dq is None else dq + part
                dvs.append(nn(dmt[hs, :], p))
                dks.append(nn(qt[hs, :], ds))
            dk = jnp.transpose(jnp.concatenate(dks, axis=0))[:ROWS]
            dv = jnp.transpose(jnp.concatenate(dvs, axis=0))[:ROWS]
            pj_s[rows, D + g * 128 : D + (g + 1) * 128] = dk.astype(bf16)
            pj_s[rows, 2 * D + g * 128 : 2 * D + (g + 1) * 128] = dv.astype(bf16)
            value, slope = gelu_pair(gp_s[rows, ls])
            field = jnp.where(inside, value, 0.0)
            d_conv = jnp.where(inside, pool(dq * (HD ** (-0.5) / 9.0)), 0.0)
            shifted = (roll1(field, 1), field, roll1(field, -1))
            d_cols = [None, None, None]
            for a in range(3):
                moved = d_conv if a == 1 else shift_rows(d_conv, WIDE * (a - 1))
                for b in range(3):
                    t = 3 * a + b
                    gsmall[t : t + 1, ls] += row_sum(moved * shifted[b])
                    term = taps[t : t + 1, ls] * moved
                    d_cols[b] = term if d_cols[b] is None else d_cols[b] + term
            d_field = roll1(d_cols[0], -1) + d_cols[1] + roll1(d_cols[2], 1)
            pj_s[rows, ls] = jnp.where(inside, slope * d_field, 0.0).astype(bf16)
        pj = pj_s[rows, :]
        d_na = None
        for part in range(3):
            for t in range(2):
                first = part * D + t * 256
                term = nt(pj[:, first : first + 256], wi[t, part])
                d_na = term if d_na is None else d_na + term
        xhat, r = normed(x_s[rows, :])
        gsmall[9:10, :] += row_sum(d_na * xhat)
        gsmall[10:11, :] += row_sum(d_na)
        co_s[rows, :] = da_s[rows, :] + norm_back(v0 * d_na, xhat, r)
        return carry

    lax.fori_loop(0, images, backward, 0)
    for i in range(images * SIDE):
        gin[i * SIDE : (i + 1) * SIDE, :] = co_s[i * WIDE : i * WIDE + SIDE, :]
    for part in range(3):
        g_in = tn(na_s[...], pj_s[:, part * D : (part + 1) * D]).astype(bf16)
        for t in range(2):
            first = IN + part * 512
            grads[t, first : first + 512, :] = g_in[:, t * 256 : (t + 1) * 256]


def block(lim, tok, cot, wi, wo, wu, wd, small, vecs):
    images = tok.shape[0] // WIN
    R = images * ROWS
    K = images * KEYS
    S = jax.ShapeDtypeStruct
    V = pltpu.VMEM
    return pl.pallas_call(
        functools.partial(block_kernel, images),
        out_shape=(
            S(tok.shape, bf16),
            S(tok.shape, f32),
            S((2, GROWS, 256), bf16),
            S((24, D), f32),
        ),
        in_specs=[pl.BlockSpec(memory_space=pltpu.SMEM)] + [pl.BlockSpec(memory_space=V)] * 8,
        out_specs=[pl.BlockSpec(memory_space=V)] * 4,
        scratch_shapes=[V((R, D), f32)] * 6
        + [V((R, D), bf16)] * 7
        + [V((K, D), bf16)] * 2
        + [V((R, FF), bf16)] * 2
        + [
            V((R, 3 * D), bf16),
            V((images * 16, ROWS, KEYS), bf16),
            V((R, D), f32),
            V((16, D), f32),
        ],
        compiler_params=pltpu.CompilerParams(vmem_limit_bytes=60 * 1024 * 1024),
    )(lim, tok, cot, wi, wo, wu, wd, small, vecs)


def tile_loop(rows, size, body):
    if rows <= size:
        body(0, rows)
        return

    def step(i, carry):
        body(pl.multiple_of(i * size, size), size)
        return carry

    lax.fori_loop(0, rows // size, step, 0)


def aligned(first, size):
    return pl.ds(pl.multiple_of(first, 16), size)


CHUNKS = ((DOWN, 2048), (UP, 2048), (OUT, 512), (IN, 1536))


def reduce_kernel(grads, gsmall, full, small_sum, *scratch):
    count = len(CHUNKS)
    r1s, s1s, rpxs, rqys, p1s, q1s, rpys, rqxs, p2s, q2s, zps, zqs = (
        scratch[i * count : (i + 1) * count] for i in range(12)
    )
    small_in, small_z, send, recv, ssend, srecv = scratch[12 * count :]
    dp, x = lax.axis_index("dp"), lax.axis_index("tensor")
    core = lax.rem(dp, 2)
    y = lax.rem(dp // 2, 2)
    z = dp // 4

    def at(zz, yy, cc, xx):
        return ((zz * 2 + yy) * 2 + cc, xx)

    core_mate = at(z, y, 1 - core, x)
    x_mate = at(z, y, core, 1 - x)
    y_mate = at(z, 1 - y, core, x)
    z_others = [lax.rem(z + k, 4) for k in range(1, 4)]
    z_mates = [at(o, y, core, x) for o in z_others]
    barrier = pltpu.get_barrier_semaphore()
    for mate in (core_mate, x_mate, y_mate, *z_mates):
        pl.semaphore_signal(barrier, inc=1, device_id=mate, device_id_type=MESH)
    pl.semaphore_wait(barrier, 6)

    def copy(src, dst, chunk, slot, mate):
        return pltpu.make_async_remote_copy(
            src_ref=src,
            dst_ref=dst,
            send_sem=send.at[chunk, slot],
            recv_sem=recv.at[chunk, slot],
            device_id=mate,
            device_id_type=MESH,
        )

    def small_copy(src, dst, slot, mate):
        return pltpu.make_async_remote_copy(
            src_ref=src,
            dst_ref=dst,
            send_sem=ssend.at[slot],
            recv_sem=srecv.at[slot],
            device_id=mate,
            device_id_type=MESH,
        )

    def add(target, one, two):
        target[...] = (one.astype(f32) + two.astype(f32)).astype(bf16)

    flights = {}

    def stage(c, s):
        base, R = CHUNKS[c]
        half, quarter, eighth, piece = R // 2, R // 4, R // 8, R // 32
        r1, s1, rpx, rqy, p1, q1, rpy, rqx, p2, q2, zp, zq = (
            group[c]
            for group in (r1s, s1s, rpxs, rqys, p1s, q1s, rpys, rqxs, p2s, q2s, zps, zqs)
        )
        for flight in flights.pop((c, s - 1), ()):
            flight.wait()
        go = []
        mine = base + core * half
        if s == 0:
            go = [copy(grads.at[:, aligned(base + (1 - core) * half, half), :], r1, c, 0, core_mate)]
        elif s == 1:

            def body(i, size):
                rows = pl.ds(i, size)
                own = aligned(mine + i, size)
                for t in range(2):
                    s1[t, rows, :] = (
                        grads[t, own, :].astype(f32) + r1[t, rows, :].astype(f32)
                    ).astype(bf16)

            tile_loop(half, 128, body)
            go = [
                copy(s1.at[1 - x, pl.ds(0, quarter), :], rpx, c, 1, x_mate),
                copy(s1.at[:, aligned(quarter + (1 - y) * eighth, eighth), :], rqy, c, 2, y_mate),
            ]
        elif s == 2:

            def body_p(i, size):
                rows = pl.ds(i, size)
                p1[rows, :] = (s1[x, rows, :].astype(f32) + rpx[rows, :].astype(f32)).astype(bf16)

            def body_q(i, size):
                rows = pl.ds(i, size)
                own = aligned(quarter + y * eighth + i, size)
                for t in range(2):
                    q1[t, rows, :] = (
                        s1[t, own, :].astype(f32) + rqy[t, rows, :].astype(f32)
                    ).astype(bf16)

            tile_loop(quarter, 128, body_p)
            tile_loop(eighth, 64, body_q)
            go = [
                copy(p1.at[aligned((1 - y) * eighth, eighth), :], rpy, c, 3, y_mate),
                copy(q1.at[1 - x], rqx, c, 4, x_mate),
            ]
        elif s == 3:

            def body(i, size):
                rows = pl.ds(i, size)
                own = aligned(y * eighth + i, size)
                p2[rows, :] = (p1[own, :].astype(f32) + rpy[rows, :].astype(f32)).astype(bf16)
                q2[rows, :] = (q1[x, rows, :].astype(f32) + rqx[rows, :].astype(f32)).astype(bf16)

            tile_loop(eighth, 64, body)
            for k in range(3):
                theirs = aligned(z_others[k] * piece, piece)
                go.append(copy(p2.at[theirs, :], zp.at[k], c, 5 + k, z_mates[k]))
                go.append(copy(q2.at[theirs, :], zq.at[k], c, 8 + k, z_mates[k]))
        elif s == 4:
            own = aligned(z * piece, piece)
            for j, (part, got) in enumerate(((p2, zp), (q2, zq))):
                total = part[own, :].astype(f32)
                for k in range(3):
                    total = total + got[k].astype(f32)
                place = aligned(mine + j * quarter + y * eighth + z * piece, piece)
                full[place, :] = total.astype(bf16)
                for k in range(3):
                    go.append(
                        copy(full.at[place, :], full.at[place, :], c, 11 + 3 * j + k, z_mates[k])
                    )
        elif s == 5:
            for j in range(2):
                place = aligned(mine + j * quarter + y * eighth, eighth)
                go.append(copy(full.at[place, :], full.at[place, :], c, 17 + j, y_mate))
        elif s == 6:
            place = aligned(mine, half)
            go = [copy(full.at[place, :], full.at[place, :], c, 19, core_mate)]
        for flight in go:
            flight.start()
        if go:
            flights[(c, s)] = go

    def small_stage(s):
        if s == 0:
            small_z[0] = gsmall[...]
        elif s <= 3:
            flights.pop(("s", s - 1))[0].wait()
            small_z[s] = small_z[s - 1] + small_in[s - 1]
        else:
            for flight in flights.pop(("s", 3)):
                flight.wait()
            total = None
            for k in range(4):
                part = small_z[4 + k]
                total = part if total is None else total + part
            small_sum[...] = total
            return
        if s < 3:
            mate = (core_mate, x_mate, y_mate)[s]
            go = [small_copy(small_z.at[s], small_in.at[s], s, mate)]
        else:
            small_z[4 + z] = small_z[3]
            go = [
                small_copy(small_z.at[3], small_z.at[4 + z], 3 + k, z_mates[k]) for k in range(3)
            ]
        for flight in go:
            flight.start()
        flights[("s", s)] = go

    for step in range(8 + count - 1):
        for c in range(count):
            if 0 <= step - c <= 7:
                stage(c, step - c)
        if 0 <= step <= 4:
            small_stage(step)


def reduce_gradients(grads, gsmall):
    S = jax.ShapeDtypeStruct
    V = pltpu.VMEM
    shapes = [
        lambda R: (2, R // 2, 256),
        lambda R: (2, R // 2, 256),
        lambda R: (R // 4, 256),
        lambda R: (2, R // 8, 256),
        lambda R: (R // 4, 256),
        lambda R: (2, R // 8, 256),
        lambda R: (R // 8, 256),
        lambda R: (R // 8, 256),
        lambda R: (R // 8, 256),
        lambda R: (R // 8, 256),
        lambda R: (3, R // 32, 256),
        lambda R: (3, R // 32, 256),
    ]
    count = len(CHUNKS)
    return pl.pallas_call(
        reduce_kernel,
        out_shape=(S((GROWS, 256), bf16), S((24, D), f32)),
        in_specs=[pl.BlockSpec(memory_space=V)] * 2,
        out_specs=[pl.BlockSpec(memory_space=V)] * 2,
        scratch_shapes=[V(shape(R), bf16) for shape in shapes for _, R in CHUNKS]
        + [
            V((3, 24, D), f32),
            V((8, 24, D), f32),
            pltpu.SemaphoreType.DMA((count, 20)),
            pltpu.SemaphoreType.DMA((count, 20)),
            pltpu.SemaphoreType.DMA((6,)),
            pltpu.SemaphoreType.DMA((6,)),
        ],
        compiler_params=pltpu.CompilerParams(
            collective_id=1, has_side_effects=True, vmem_limit_bytes=48 * 1024 * 1024
        ),
    )(grads, gsmall)


def spread(part, transposed):
    shape = (768, 256) if transposed else (256, 768)
    narrow_side, wide_side = (1, 0) if transposed else (0, 1)
    a = lax.broadcasted_iota(jnp.int32, shape, narrow_side)
    b = lax.broadcasted_iota(jnp.int32, shape, wide_side)
    return jnp.where(b == (a // HD) * (3 * HD) + part * HD + lax.rem(a, HD), 1.0, 0.0).astype(bf16)


def adam(w, m, v, g, rate, decay):
    m = 0.5 * m + 0.5 * g
    v = 0.5 * v + 0.5 * g * g
    scale = 1.0 / (1.0 - 0.5**STEP)
    w = w - rate * ((m * scale) / (jnp.sqrt(v * scale) + 1e-08) + decay * w)
    return w, m, v


MATRICES = (
    (1024, 512, FF**-0.5, 4),
    (512, 1024, D**-0.5, 4),
    (256, 512, (D // HD) ** -0.5, 1),
    (512, 768, D**-0.5, 2),
)


def adam_kernel(*refs):
    full, small_sum = refs[:2]
    mats = refs[2:14]
    smalls = refs[14:23]
    outs = refs[23:39]
    small_outs = refs[39:48]
    bufs = refs[48:60]
    lows = refs[60:64]
    in_sem, out_sem = refs[64:]
    loads = {}
    for i, (rows, cols, rate, pieces) in enumerate(MATRICES):
        size = rows // pieces
        for p in range(pieces):
            rs = pl.ds(p * size, size)
            for j in range(3):
                go = pltpu.make_async_copy(
                    mats[3 * i + j].at[rs, :], bufs[3 * i + j].at[rs, :], in_sem.at[i, p, j]
                )
                go.start()
                loads[i, p, j] = go
    stores = []
    for i, (rows, cols, rate, pieces) in enumerate(MATRICES):
        size = rows // pieces
        bw, bm, bv = bufs[3 * i : 3 * i + 3]
        low = lows[i]
        for p in range(pieces):
            for j in range(3):
                loads[i, p, j].wait()

            def body(first, tile, i=i, p=p, bw=bw, bm=bm, bv=bv, low=low, rate=rate, size=size):
                rs = pl.ds(p * size + first, tile)
                if i == 0:
                    g = [full[pl.ds(DOWN + j * 1024 + p * size + first, tile), :] for j in range(2)]
                elif i == 1:
                    g = [full[pl.ds(UP + j * 512 + p * size + first, tile), :] for j in range(4)]
                elif i == 2:
                    g = [full[pl.ds(OUT + j * 256 + p * size + first, tile), :] for j in range(2)]
                else:
                    g = None
                    for part in range(3):
                        own = full[pl.ds(IN + part * 512 + p * size + first, tile), :]
                        term = nn(own, spread(part, False))
                        g = term if g is None else g + term
                if i < 3:
                    g = jnp.concatenate(g, axis=1).astype(f32)
                w, m, v = adam(bw[rs, :], bm[rs, :], bv[rs, :], g, rate, 0.05)
                bw[rs, :] = w
                bm[rs, :] = m
                bv[rs, :] = v
                low[rs, :] = w.astype(bf16)

            tile_loop(size, 32, body)
            rs = pl.ds(p * size, size)
            for j, src in enumerate((bw, bm, bv, low)):
                go = pltpu.make_async_copy(
                    src.at[rs, :], outs[4 * i + j].at[rs, :], out_sem.at[i, p, j]
                )
                go.start()
                stores.append(go)
    x = lax.axis_index("tensor")
    mine = pl.ds(pl.multiple_of(x * 256, 256), 256)
    g_small = small_sum[:, mine]
    both = small_sum[16:20, :]
    first = jnp.where(x == 0, 1.0, 0.0)
    g_bias = jnp.concatenate(
        [
            (both[j : j + 1, :] * first + both[2 + j : 3 + j, :] * (1.0 - first))
            for j in range(2)
        ],
        axis=1,
    )
    for i, (g, rate, decay) in enumerate(
        ((g_small[0:9], 2.0, 0.05), (g_bias, 0.3, 0.0), (g_small[9:16], 0.3, 0.0))
    ):
        w = smalls[3 * i][...] if i < 2 else smalls[6][:, mine]
        new = adam(w, smalls[3 * i + 1][...], smalls[3 * i + 2][...], g, rate, decay)
        for j in range(3):
            small_outs[3 * i + j][...] = new[j]
    for go in stores:
        go.wait()


def adam_step(full, small_sum, mats, smalls):
    S = jax.ShapeDtypeStruct
    V = pltpu.VMEM
    mat_shapes = [(rows, cols) for rows, cols, _, _ in MATRICES]
    any_spec = pl.BlockSpec(memory_space=pl.ANY)
    vmem_spec = pl.BlockSpec(memory_space=V)
    small_shapes = [(9, 256)] * 3 + [(1, 1024)] * 3 + [(7, 256)] * 3
    return pl.pallas_call(
        adam_kernel,
        out_shape=tuple(
            S(shape, kind) for shape in mat_shapes for kind in (f32, f32, f32, bf16)
        )
        + tuple(S(shape, f32) for shape in small_shapes),
        in_specs=[vmem_spec] * 2 + [any_spec] * 12 + [vmem_spec] * 9,
        out_specs=[any_spec] * 16 + [vmem_spec] * 9,
        scratch_shapes=[V(shape, f32) for shape in mat_shapes for _ in range(3)]
        + [V(shape, bf16) for shape in mat_shapes]
        + [pltpu.SemaphoreType.DMA((4, 4, 3)), pltpu.SemaphoreType.DMA((4, 4, 4))],
        compiler_params=pltpu.CompilerParams(vmem_limit_bytes=48 * 1024 * 1024),
    )(full, small_sum, *mats, *smalls)


def gather_kernel(w_in, w_out, w_up, w_down, own_small, wi, wo, wu, wd, small, send, recv):
    dp, x = lax.axis_index("dp"), lax.axis_index("tensor")
    core = lax.rem(dp, 2)
    y = lax.rem(dp // 2, 2)
    z = dp // 4

    def at(yy, cc, xx):
        return ((z * 2 + yy) * 2 + cc, xx)

    core_mate, x_mate, y_mate = at(y, 1 - core, x), at(y, core, 1 - x), at(1 - y, core, x)
    barrier = pltpu.get_barrier_semaphore()
    for mate in (core_mate, x_mate, y_mate):
        pl.semaphore_signal(barrier, inc=1, device_id=mate, device_id_type=MESH)
    pl.semaphore_wait(barrier, 3)

    def copy(src, dst, item, slot, mate):
        go = pltpu.make_async_remote_copy(
            src_ref=src,
            dst_ref=dst,
            send_sem=send.at[item, slot],
            recv_sem=recv.at[item, slot],
            device_id=mate,
            device_id_type=MESH,
        )
        go.start()
        return go

    small[x] = own_small[...]
    extra = copy(small.at[x], small.at[x], 4, 0, x_mate)

    def view(item, half, yy, cc):
        quarter = yy * 2 + cc
        if item == 0:
            return wi.at[half, :, aligned(quarter * 128, 128), :]
        ref, size = ((wo, 64), (wu, 128), (wd, 256))[item - 1]
        return ref.at[half, aligned(quarter * size, size), :]

    crossing = []
    for item in range(4):
        if item == 0:
            spreads = [spread(part, True) for part in range(3)]

            def body(first, tile):
                rows = pl.ds(first, tile)
                low = w_in[rows, :].astype(bf16)
                for part in range(3):
                    wi[x, part, rows, :] = nn(low, spreads[part]).astype(bf16)

            tile_loop(512, 128, body)
        else:
            src, dst = ((w_out, wo), (w_up, wu), (w_down, wd))[item - 1]

            def body(first, tile, src=src, dst=dst):
                rows = pl.ds(first, tile)
                dst[x, rows, :] = src[rows, :].astype(bf16)

            tile_loop(src.shape[0], 64, body)
        mine = view(item, x, y, core)
        crossing.append(copy(mine, mine, item, 0, x_mate))

    flying = [extra]
    aside = {}
    for item in range(5):
        if item < 4:
            crossing[item].wait()
            got = view(item, 1 - x, y, core)
            flying.append(copy(got, got, item, 1, core_mate))
            aside[item] = copy(got, got, item, 2, y_mate)
        if item > 0:
            aside[item - 1].wait()
            got = view(item - 1, 1 - x, 1 - y, core)
            flying.append(copy(got, got, item - 1, 3, core_mate))
    for go in flying:
        go.wait()


def gather_weights(w_in, w_out, w_up, w_down, own_small):
    S = jax.ShapeDtypeStruct
    spec = pl.BlockSpec(memory_space=pltpu.VMEM)
    return pl.pallas_call(
        gather_kernel,
        out_shape=(
            S((2, 3, D, 256), bf16),
            S((2, 256, D), bf16),
            S((2, D, 1024), bf16),
            S((2, 1024, D), bf16),
            S((2, 16, 256), f32),
        ),
        in_specs=[spec] * 5,
        out_specs=[spec] * 5,
        scratch_shapes=[pltpu.SemaphoreType.DMA((5, 4)), pltpu.SemaphoreType.DMA((5, 4))],
        compiler_params=pltpu.CompilerParams(
            collective_id=2, has_side_effects=True, vmem_limit_bytes=40 * 1024 * 1024
        ),
    )(w_in, w_out, w_up, w_down, own_small)


def local(
    tokens, cotangent, image_counts,
    w_in, m_in, v_in, w_out, m_out, v_out, w_up, m_up, v_up, w_down, m_down, v_down,
    kernel, m_kernel, v_kernel, up_bias, m_bias, v_bias, vectors, m_vectors, v_vectors,
):
    images = tokens.shape[0] // WIN
    live = image_counts[lax.axis_index("dp")] - lax.axis_index("tensor") * images
    own_small = jnp.concatenate(
        [kernel, up_bias.reshape(4, 256), jnp.zeros((3, 256), f32)], axis=0
    )
    wi, wo, wu, wd, small = gather_weights(w_in, w_out, w_up, w_down, own_small)
    out, grad_in, grads, g_small = block(
        live.reshape(1), tokens, cotangent, wi, wo.reshape(D, D), wu, wd.reshape(FF, D), small, vectors
    )
    full, small_sum = reduce_gradients(grads, g_small)
    new = adam_step(
        full,
        small_sum,
        (w_down, m_down, v_down, w_up, m_up, v_up, w_out, m_out, v_out, w_in, m_in, v_in),
        (kernel, m_kernel, v_kernel)
        + tuple(a.reshape(1, -1) for a in (up_bias, m_bias, v_bias))
        + (vectors, m_vectors, v_vectors),
    )
    down, up, mid, first = new[:4], new[4:8], new[8:12], new[12:16]
    bias = tuple(a.reshape(-1) for a in new[19:22])
    return (out, grad_in, *first, *mid, *up, *down, *new[16:19], *bias, *new[22:25])


def general(
    tokens, cotangent, image_counts,
    w_in, m_in, v_in, w_out, m_out, v_out, w_up, m_up, v_up, w_down, m_down, v_down,
    kernel, m_kernel, v_kernel, up_bias, m_bias, v_bias, vectors, m_vectors, v_vectors,
):
    images = tokens.shape[0] // WIN
    place = lax.axis_index("tensor")
    live = image_counts[lax.axis_index("dp")] - place * images

    def whole(a, axis):
        return lax.all_gather(a, "tensor", axis=axis, tiled=True)

    wi = whole(w_in.astype(bf16), 1).reshape(D, 2, 8, 3, HD).transpose(1, 3, 0, 2, 4)
    wi = wi.reshape(2, 3, D, 256)
    wo, wd = whole(w_out.astype(bf16), 0), whole(w_down.astype(bf16), 0)
    wu = whole(w_up.astype(bf16), 1).reshape(D, 2, 1024).transpose(1, 0, 2)
    small = jnp.concatenate(
        [
            whole(kernel, 1).reshape(9, 2, 256).transpose(1, 0, 2),
            whole(up_bias, 0).reshape(2, 4, 256),
            jnp.zeros((2, 3, 256), f32),
        ],
        axis=1,
    )
    out, grad_in, grads, gs = block(
        live.reshape(1), tokens, cotangent, wi, wo, wu, wd, small, vectors
    )
    grads = grads.astype(f32)

    def columns(first, rows, count):
        part = grads[:, first : first + rows * count].reshape(2, count, rows, 256)
        return part

    g_down = columns(DOWN, 1024, 2).transpose(0, 2, 1, 3).reshape(FF, D)
    g_up = columns(UP, 512, 4).transpose(2, 0, 1, 3).reshape(D, FF)
    g_out = columns(OUT, 256, 2).transpose(0, 2, 1, 3).reshape(D, D)
    g_in = columns(IN, 512, 3).reshape(2, 3, D, 8, HD).transpose(2, 0, 3, 1, 4).reshape(D, 3 * D)

    def owned(a, axis):
        return lax.psum(lax.psum_scatter(a, "tensor", scatter_dimension=axis, tiled=True), "dp")

    g_in, g_out, g_up, g_down = owned(g_in, 1), owned(g_out, 0), owned(g_up, 1), owned(g_down, 0)
    g_kernel, g_bias, g_vectors = owned(gs[0:9], 1), owned(gs[16:20].reshape(-1), 0), owned(gs[9:16], 1)
    vector_width = m_vectors.shape[1]
    own_vectors = lax.dynamic_slice_in_dim(vectors, place * vector_width, vector_width, 1)
    results = [out, grad_in]
    for w, m, v, g, rate in (
        (w_in, m_in, v_in, g_in, D**-0.5),
        (w_out, m_out, v_out, g_out, (D // HD) ** -0.5),
        (w_up, m_up, v_up, g_up, D**-0.5),
        (w_down, m_down, v_down, g_down, FF**-0.5),
    ):
        new = adam(w, m, v, g, rate, 0.05)
        results += [*new, new[0].astype(bf16)]
    results += adam(kernel, m_kernel, v_kernel, g_kernel, 2.0, 0.05)
    results += adam(up_bias, m_bias, v_bias, g_bias, 0.3, 0.0)
    results += adam(own_vectors, m_vectors, v_vectors, g_vectors, 0.3, 0.0)
    return tuple(results)


def solution(mesh):
    rows, columns = P("tensor", None), P(None, "tensor")
    tokens = P(("dp", "tensor"), None)
    mats = (columns,) * 3 + (rows,) * 3 + (columns,) * 3 + (rows,) * 3
    news = (columns,) * 4 + (rows,) * 4 + (columns,) * 4 + (rows,) * 4
    pairs = mesh.shape["dp"] == 16 and mesh.shape["tensor"] == 2
    return jax.shard_map(
        local if pairs else general,
        mesh=mesh,
        in_specs=(tokens, tokens, P(), *mats)
        + (columns,) * 3
        + (P("tensor"),) * 3
        + (P(), columns, columns),
        out_specs=(tokens, tokens, *news) + (columns,) * 3 + (P("tensor"),) * 3 + (columns,) * 3,
        check_vma=False,
    )
```

```python
import functools
import jax
import jax.numpy as jnp
from jax import lax
from jax.experimental import pallas as pl
from jax.experimental.pallas import tpu as pltpu
from jax.sharding import PartitionSpec as P

D = 512
HD = 32
FF = 2048
SIDE = 14
WIDE = 16
WIN = SIDE * SIDE
ROWS = SIDE * WIDE
KEYS = 256
GROUPS = D // 128
STEP = 5
DOWN, UP, OUT, IN, GROWS = 0, 2048, 4096, 4608, 6144
MESH = pl.DeviceIdType.MESH
eps = 1e-05
f32 = jnp.float32
bf16 = jnp.bfloat16
C0 = 0.7978845608028654
C1 = 0.044715


def nn(a, b):
    return lax.dot_general(a, b, (((1,), (0,)), ((), ())), preferred_element_type=f32)


def nt(a, b):
    return lax.dot_general(a, b, (((1,), (1,)), ((), ())), preferred_element_type=f32)


def tn(a, b):
    return lax.dot_general(a, b, (((0,), (0,)), ((), ())), preferred_element_type=f32)


def normed(x):
    c = x - jnp.mean(x, axis=-1, keepdims=True)
    r = lax.rsqrt(jnp.mean(c * c, axis=-1, keepdims=True) + eps)
    return c * r, r


def norm_back(u, xhat, r):
    return r * (
        u
        - jnp.mean(u, axis=-1, keepdims=True)
        - xhat * jnp.mean(u * xhat, axis=-1, keepdims=True)
    )


def gelu_pair(x):
    x2 = x * x
    t = 0.5 * jnp.tanh(x * (C0 + (C0 * C1) * x2))
    h = 0.5 + t
    value = x * h
    return value, h + value * ((0.5 - t) * (2.0 * C0 + (6.0 * C0 * C1) * x2))


def gelu(x):
    return x * (0.5 + 0.5 * jnp.tanh(x * (C0 + (C0 * C1) * (x * x))))


def row_sum(x):
    return jnp.sum(x, axis=0, keepdims=True)


def shift_rows(x, by):
    z = jnp.zeros((abs(by), x.shape[1]), x.dtype)
    if by > 0:
        return jnp.concatenate([z, x[:-by]], axis=0)
    return jnp.concatenate([x[-by:], z], axis=0)


def roll1(x, by):
    return pltpu.roll(x, by % x.shape[0], 0)


def pool(c):
    s = c + roll1(c, 1) + roll1(c, -1)
    return s + shift_rows(s, WIDE) + shift_rows(s, -WIDE)


def block_body(images, limit, first_half, hooks, wi, wo, wu, wd, small, vecs,
               gin, grads, gsmall,
               x_s, co_s, at_s, af_s, da_s, gp_s, mf_s, na_s, nb_s, lb_s, la_s, mx_s,
               q_s, k_s, v_s, dm_s, hd_s, dp_s, pj_s, p_s, taps_s, ds_s):
    gain_a, shift_a, gain_b, shift_b, scale_a, scale_f, bias_f = (
        vecs[i : i + 1, :] for i in range(7)
    )
    gsmall[...] = jnp.zeros_like(gsmall)
    dn_s = at_s
    gtaps = taps_s
    gtaps[...] = jnp.zeros_like(gtaps)
    blank = jnp.zeros((KEYS - ROWS, 256), bf16)
    for ref in (q_s, k_s, v_s, dm_s):
        for t in range(2):
            for n in range(images):
                ref[t, n * KEYS + ROWS : (n + 1) * KEYS, :] = blank

    cell = lax.broadcasted_iota(jnp.int32, (ROWS, 1), 0)
    inside = lax.rem(cell, WIDE) < SIDE
    lane = lax.broadcasted_iota(jnp.int32, (1, 128), 1)
    head_masks = [(lane // HD) == h for h in range(4)]
    key_row = lax.broadcasted_iota(jnp.int32, (KEYS, 128), 0)
    key_lane = lax.broadcasted_iota(jnp.int32, (KEYS, 128), 1)
    key_pad = (lax.rem(key_row, WIDE) >= SIDE) | (key_row >= ROWS)
    key_block = jnp.where(key_pad & (key_lane == 0), -1e30, 0.0).astype(bf16)
    one_block = jnp.where(key_lane == 0, 1.0, 0.0).astype(bf16)

    def padded(n):
        return pl.ds(pl.multiple_of(n * ROWS, WIDE), ROWS)

    def held(n):
        return pl.ds(pl.multiple_of(n * KEYS, WIDE), ROWS)

    def whole(n):
        return pl.ds(pl.multiple_of(n * KEYS, WIDE), KEYS)

    def masked(h, a):
        return jnp.where(head_masks[h], a, jnp.zeros_like(a))

    def prepare(n, carry):
        rows = padded(n)
        xhat, _ = normed(x_s[rows, :].astype(f32))
        na_s[rows, :] = (xhat * gain_a + shift_a).astype(bf16)
        return carry

    def tap(t, i, ls):
        return small[t, pl.ds(i, 1), ls]

    def attend(t, n):
        rows = padded(n)
        na = na_s[rows, :]
        k_s[t, held(n), :] = nn(na, wi[t, 1]).astype(bf16)
        v_s[t, held(n), :] = nn(na, wi[t, 2]).astype(bf16)
        for g in range(2):
            ls = slice(g * 128, (g + 1) * 128)
            gp = nn(na, wi[t, 0, :, ls])
            gp_s[t, rows, ls] = gp
            field = jnp.where(inside, gelu(gp), 0.0)
            back, ahead = roll1(field, 1), roll1(field, -1)
            conv = None
            for a in range(3):
                part = (
                    tap(t, 3 * a, ls) * back
                    + tap(t, 3 * a + 1, ls) * field
                    + tap(t, 3 * a + 2, ls) * ahead
                )
                if a != 1:
                    part = shift_rows(part, WIDE * (1 - a))
                conv = part if conv is None else conv + part
            pooled = pool(jnp.where(inside, conv, 0.0)) * (HD ** (-0.5) / 9.0)
            q_s[t, held(n), ls] = pooled.astype(bf16)
        for g in range(2):
            ls = slice(g * 128, (g + 1) * 128)
            qa = jnp.concatenate([q_s[t, whole(n), ls], one_block], axis=1)
            kg = k_s[t, whole(n), ls]
            vt = jnp.transpose(v_s[t, whole(n), ls])
            mixed = []
            keys = jnp.concatenate(
                [jnp.concatenate([masked(h, kg), key_block], axis=1) for h in range(4)], axis=0
            )
            scores = nt(keys, qa)
            for h in range(4):
                hs = slice(h * KEYS, (h + 1) * KEYS)
                s = scores[hs]
                e = jnp.exp(s - jnp.max(s, axis=0, keepdims=True))
                p_s[t, n * 2 + g, :, hs] = (e * (1.0 / jnp.sum(e, axis=0, keepdims=True))).astype(bf16)
            for h in range(4):
                p = p_s[t, n * 2 + g, :, h * KEYS : (h + 1) * KEYS]
                mixed.append(nn(vt[h * HD : (h + 1) * HD], p))
            mix = jnp.transpose(jnp.concatenate(mixed, axis=0))[:ROWS]
            mf_s[t, rows, ls] = mix
            mx_s[t, rows, ls] = mix.astype(bf16)

    def finish(n, carry):
        rows = padded(n)
        attn = nn(mx_s[0, rows, :], wo[0]) + nn(mx_s[1, rows, :], wo[1])
        at_s[rows, :] = attn
        after = x_s[rows, :].astype(f32) + scale_a * attn
        af_s[rows, :] = after
        xhat, _ = normed(after)
        nb_s[rows, :] = (xhat * gain_b + shift_b).astype(bf16)
        return carry

    def feed(n, carry):
        rows = padded(n)
        co = co_s[rows, :].astype(f32)
        d_branch = scale_f * co
        lb = d_branch.astype(bf16)
        lb_s[rows, :] = lb
        nb = nb_s[rows, :]
        branch = None
        for c in range(4):
            cs = slice(c * 512, (c + 1) * 512)
            us = slice((c % 2) * 512, (c % 2 + 1) * 512)
            unit_bias = jnp.concatenate(
                [small[c // 2, 9 + (c % 2) * 2 + j : 10 + (c % 2) * 2 + j, :] for j in range(2)],
                axis=1,
            )
            pre = nn(nb, wu[c // 2, :, us]) + unit_bias
            value, slope = gelu_pair(pre)
            hid = value.astype(bf16)
            hd_s[rows, cs] = hid
            br = nn(hid, wd[c // 2, us, :])
            d_pre = slope * nt(lb, wd[c // 2, us, :])
            gsmall[16 + c : 17 + c, :] += row_sum(d_pre)
            dp = d_pre.astype(bf16)
            dp_s[rows, cs] = dp
            dn = nt(dp, wu[c // 2, :, us])
            branch = br if branch is None else branch + br
            d_nb = dn if c == 0 else d_nb + dn
        after = af_s[rows, :]
        xhat, r = normed(after)
        moved = branch + bias_f
        live = (n < limit).astype(f32)
        af_s[rows, :] = (after + scale_f * moved) * live
        gsmall[14:15, :] += row_sum(co * moved)
        gsmall[15:16, :] += row_sum(d_branch)
        gsmall[11:12, :] += row_sum(d_nb * xhat)
        gsmall[12:13, :] += row_sum(d_nb)
        d_after = co + norm_back(gain_b * d_nb, xhat, r)
        da_s[rows, :] = d_after
        gsmall[13:14, :] += row_sum(d_after * at_s[rows, :])
        la = (scale_a * d_after).astype(bf16)
        la_s[rows, :] = la
        for t in range(2):
            dm_s[t, held(n), :] = nt(la, wo[t]).astype(bf16)
        return carry

    pick_row = lax.broadcasted_iota(jnp.int32, (256, 128), 0)
    pick_lane = lax.broadcasted_iota(jnp.int32, (256, 128), 1)
    pick = jnp.where(
        (lax.rem(pick_row, 128) // HD == lax.rem(pick_lane, 4)) & (pick_lane < 8), 1.0, 0.0
    ).astype(bf16)

    def split(a):
        high = a.astype(bf16)
        return high, (a - high.astype(f32)).astype(bf16)

    def inner_block(a):
        sums = nn(jnp.concatenate(split(a), axis=1), pick)
        high, low = split(sums)
        return jnp.where(lane < 4, high, low)

    blank_rows = jnp.zeros((KEYS - ROWS, 128), bf16)

    minus = [
        jnp.where((lane == h) | (lane == h + 4), -1.0, 0.0).astype(bf16) for h in range(4)
    ]

    def recede(t, n):
        rows = padded(n)
        for g in range(2):
            ls = slice(g * 128, (g + 1) * 128)
            inner = inner_block(dm_s[t, held(n), ls].astype(f32) * mf_s[t, rows, ls])
            dmg = dm_s[t, whole(n), ls]
            left = jnp.concatenate(
                [dmg, jnp.concatenate([inner, blank_rows], axis=0)], axis=1
            )
            qg = q_s[t, whole(n), ls]
            kg = k_s[t, whole(n), ls]
            vg = v_s[t, whole(n), ls]
            kt = jnp.transpose(kg)
            dqs = []
            right = jnp.concatenate(
                [
                    jnp.concatenate([masked(h, vg), jnp.broadcast_to(minus[h], (KEYS, 128))], axis=1)
                    for h in range(4)
                ],
                axis=0,
            )
            d_probs = nt(right, left)
            for h in range(4):
                hs = slice(h * KEYS, (h + 1) * KEYS)
                e = p_s[t, n * 2 + g, :, hs]
                ds_s[:, hs] = (e.astype(f32) * d_probs[hs]).astype(bf16)
            dv = nn(
                p_s[t, n * 2 + g], jnp.concatenate([masked(h, dmg) for h in range(4)], axis=0)
            )
            dk = nn(ds_s[...], jnp.concatenate([masked(h, qg) for h in range(4)], axis=0))
            for h in range(4):
                dqs.append(nn(kt[h * HD : (h + 1) * HD], ds_s[:, h * KEYS : (h + 1) * KEYS]))
            dq = jnp.transpose(jnp.concatenate(dqs, axis=0))[:ROWS]
            pj_s[t, 1, rows, ls] = dk[:ROWS].astype(bf16)
            pj_s[t, 2, rows, ls] = dv[:ROWS].astype(bf16)
            value, slope = gelu_pair(gp_s[t, rows, ls])
            field = jnp.where(inside, value, 0.0)
            d_conv = jnp.where(inside, pool(dq * (HD ** (-0.5) / 9.0)), 0.0)
            shifted = (roll1(field, 1), field, roll1(field, -1))
            d_cols = [None, None, None]
            for a in range(3):
                moved = d_conv if a == 1 else shift_rows(d_conv, WIDE * (a - 1))
                for b in range(3):
                    i = 3 * a + b
                    gtaps[t, i : i + 1, ls] += row_sum(moved * shifted[b])
                    term = tap(t, i, ls) * moved
                    d_cols[b] = term if d_cols[b] is None else d_cols[b] + term
            d_field = roll1(d_cols[0], -1) + d_cols[1] + roll1(d_cols[2], 1)
            pj_s[t, 0, rows, ls] = jnp.where(inside, slope * d_field, 0.0).astype(bf16)
        d_na = None
        for part in range(3):
            term = nt(pj_s[t, part, rows, :], wi[t, part])
            d_na = term if d_na is None else d_na + term
        return d_na

    def rise(n, carry):
        rows = padded(n)
        d_na = dn_s[rows, :]
        xhat, r = normed(x_s[rows, :].astype(f32))
        gsmall[9:10, :] += row_sum(d_na * xhat)
        gsmall[10:11, :] += row_sum(d_na)
        da_s[rows, :] += norm_back(gain_a * d_na, xhat, r)
        return carry

    def narrow_rows(target, source):
        for i in range(images * SIDE):
            target[i * SIDE : (i + 1) * SIDE, :] = source[i * WIDE : i * WIDE + SIDE, :]

    def store_down(u):
        for t in range(2):
            cs = slice((2 * t + u) * 512, (2 * t + u + 1) * 512)
            down = tn(hd_s[:, cs], lb_s[...]).astype(bf16)
            for j in range(2):
                first = DOWN + (2 * u + j) * 512
                grads[t, first : first + 512, :] = down[:, j * 256 : (j + 1) * 256]

    def store_up(u):
        for t in range(2):
            cs = slice((2 * t + u) * 512, (2 * t + u + 1) * 512)
            up = tn(nb_s[...], dp_s[:, cs]).astype(bf16)
            for j in range(2):
                first = UP + (2 * u + j) * 512
                grads[t, first : first + 512, :] = up[:, j * 256 : (j + 1) * 256]

    def store_out():
        for t in range(2):
            g_out = tn(mx_s[t], la_s[...]).astype(bf16)
            for j in range(2):
                first = OUT + j * 256
                grads[t, first : first + 256, :] = g_out[:, j * 256 : (j + 1) * 256]

    def store_in(t, part):
        first = IN + part * 512
        grads[t, first : first + 512, :] = tn(na_s[...], pj_s[t, part]).astype(bf16)

    def widen(source, temp, spare, target, scaled):
        temp[0 : images * WIN, :] = source[0 : images * WIN, :].astype(f32)
        pad = jnp.zeros((WIDE - SIDE, D), f32)
        for n in range(images):
            for i in range(n * SIDE, (n + 1) * SIDE):
                cells = temp[i * SIDE : (i + 1) * SIDE, :]
                if scaled:
                    cells = cells * (n < limit).astype(f32)
                spare[i * WIDE : i * WIDE + SIDE, :] = cells
                spare[i * WIDE + SIDE : (i + 1) * WIDE, :] = pad
        target[...] = spare[...].astype(bf16)

    loop = lax.fori_loop
    hooks.tokens()
    widen(nb_s, at_s, af_s, x_s, False)
    loop(0, images, prepare, 0)
    hooks.weights()
    other_half = 1 - first_half

    def fore(i, carry):
        later = i // images
        attend(first_half + (other_half - first_half) * later, lax.rem(i, images))
        hooks.fore(i)
        return carry

    loop(0, 2 * images, fore, 0)
    hooks.cotangent()
    widen(lb_s, at_s, da_s, co_s, True)
    loop(0, images, finish, 0)
    hooks.arrived()
    loop(0, images, feed, 0)
    narrow_rows(gin, af_s)
    hooks.output()
    for u in range(2):
        store_down(u)
        hooks.point("D%d" % u)
    for u in range(2):
        store_up(u)
        hooks.point("U%d" % u)
    store_out()
    hooks.point("O")

    def aft(n, carry):
        dn_s[padded(n), :] = recede(other_half, n)
        hooks.back(n)
        return carry

    loop(0, images, aft, 0)
    for part in (2, 1, 0):
        store_in(other_half, part)
        hooks.point("A%d" % part)

    def aft2(n, carry):
        dn_s[padded(n), :] += recede(first_half, n)
        hooks.back(images + n)
        return carry

    loop(0, images, aft2, 0)
    for part in (2, 1, 0):
        store_in(first_half, part)
        hooks.point("B%d" % part)
    loop(0, images, rise, 0)
    narrow_rows(gin, da_s)
    for t in range(2):
        gsmall[0:9, t * 256 : (t + 1) * 256] = gtaps[t, 0:9, :]
    hooks.finished()


class Quiet:
    def __init__(self, tok, cot, nb_s, lb_s, out, gin):
        self.refs = tok, cot, nb_s, lb_s, out, gin

    def tokens(self):
        tok, cot, nb_s, lb_s, _, _ = self.refs
        rows = tok.shape[0]
        nb_s[0:rows, :] = tok[...]
        lb_s[0:rows, :] = cot[...]

    def output(self):
        _, _, _, _, out, gin = self.refs
        out[...] = gin[...].astype(bf16)

    def point(self, name):
        pass

    back = fore = point

    def weights(self):
        pass

    cotangent = arrived = finished = weights


def block_kernel(images, lim, tok, cot, wi, wo, wu, wd, small, vecs, out, gin, grads, gsmall, *scratch):
    quiet = Quiet(tok, cot, scratch[8], scratch[9], out, gin)
    block_body(images, lim[0], 0, quiet, wi, wo, wu, wd, small, vecs, gin, grads, gsmall, *scratch)


def block_scratch(images):
    R = images * ROWS
    K = images * KEYS
    V = pltpu.VMEM
    return (
        [V((R, D), bf16)] * 2
        + [V((R, D), f32)] * 3
        + [V((2, R, 256), f32)] * 2
        + [V((R, D), bf16)] * 4
        + [V((2, R, 256), bf16)]
        + [V((2, K, 256), bf16)] * 4
        + [V((R, FF), bf16)] * 2
        + [
            V((2, 3, R, 256), bf16),
            V((2, images * 2, KEYS, 4 * KEYS), bf16),
            V((2, 16, 256), f32),
            V((KEYS, 4 * KEYS), bf16),
        ]
    )


def block(lim, tok, cot, wi, wo, wu, wd, small, vecs):
    images = tok.shape[0] // WIN
    S = jax.ShapeDtypeStruct
    V = pltpu.VMEM
    return pl.pallas_call(
        functools.partial(block_kernel, images),
        out_shape=(
            S(tok.shape, bf16),
            S(tok.shape, f32),
            S((2, GROWS, 256), bf16),
            S((24, D), f32),
        ),
        in_specs=[pl.BlockSpec(memory_space=pltpu.SMEM)] + [pl.BlockSpec(memory_space=V)] * 8,
        out_specs=[pl.BlockSpec(memory_space=V)] * 4,
        scratch_shapes=block_scratch(images),
        compiler_params=pltpu.CompilerParams(vmem_limit_bytes=62 * 1024 * 1024),
    )(lim, tok, cot, wi, wo, wu, wd, small, vecs)


def tile_loop(rows, size, body):
    if rows <= size:
        body(0, rows)
        return

    def step(i, carry):
        body(pl.multiple_of(i * size, size), size)
        return carry

    lax.fori_loop(0, rows // size, step, 0)


def aligned(first, size):
    return pl.ds(pl.multiple_of(first, 16), size)


def spread(part, transposed):
    shape = (768, 256) if transposed else (256, 768)
    narrow_side, wide_side = (1, 0) if transposed else (0, 1)
    a = lax.broadcasted_iota(jnp.int32, shape, narrow_side)
    b = lax.broadcasted_iota(jnp.int32, shape, wide_side)
    return jnp.where(b == (a // HD) * (3 * HD) + part * HD + lax.rem(a, HD), 1.0, 0.0).astype(bf16)


def adam(w, m, v, g, rate, decay):
    m = 0.5 * m + 0.5 * g
    v = 0.5 * v + 0.5 * g * g
    scale = 1.0 / (1.0 - 0.5**STEP)
    w = w - rate * ((m * scale) / (jnp.sqrt(v * scale) + 1e-08) + decay * w)
    return w, m, v


MATRICES = (
    (1024, 512, FF**-0.5, 4),
    (512, 1024, D**-0.5, 4),
    (256, 512, (D // HD) ** -0.5, 1),
    (512, 768, D**-0.5, 2),
)


def adam_kernel(*refs):
    full, small_sum = refs[:2]
    mats = refs[2:14]
    smalls = refs[14:23]
    outs = refs[23:39]
    small_outs = refs[39:48]
    bufs = refs[48:60]
    lows = refs[60:64]
    in_sem, out_sem = refs[64:]
    loads = {}
    for i, (rows, cols, rate, pieces) in enumerate(MATRICES):
        size = rows // pieces
        for p in range(pieces):
            rs = pl.ds(p * size, size)
            for j in range(3):
                go = pltpu.make_async_copy(
                    mats[3 * i + j].at[rs, :], bufs[3 * i + j].at[rs, :], in_sem.at[i, p, j]
                )
                go.start()
                loads[i, p, j] = go
    stores = []
    for i, (rows, cols, rate, pieces) in enumerate(MATRICES):
        size = rows // pieces
        bw, bm, bv = bufs[3 * i : 3 * i + 3]
        low = lows[i]
        for p in range(pieces):
            for j in range(3):
                loads[i, p, j].wait()

            def body(first, tile, i=i, p=p, bw=bw, bm=bm, bv=bv, low=low, rate=rate, size=size):
                rs = pl.ds(p * size + first, tile)
                if i == 0:
                    g = [
                        full[pl.ds(DOWN + (p // 2 * 2 + j) * 512 + p % 2 * size + first, tile), :]
                        for j in range(2)
                    ]
                elif i == 1:
                    g = [full[pl.ds(UP + j * 512 + p * size + first, tile), :] for j in range(4)]
                elif i == 2:
                    g = [full[pl.ds(OUT + j * 256 + p * size + first, tile), :] for j in range(2)]
                else:
                    g = None
                    for part in range(3):
                        own = full[pl.ds(IN + part * 512 + p * size + first, tile), :]
                        term = nn(own, spread(part, False))
                        g = term if g is None else g + term
                if i < 3:
                    g = jnp.concatenate(g, axis=1).astype(f32)
                w, m, v = adam(bw[rs, :], bm[rs, :], bv[rs, :], g, rate, 0.05)
                bw[rs, :] = w
                bm[rs, :] = m
                bv[rs, :] = v
                low[rs, :] = w.astype(bf16)

            tile_loop(size, 32, body)
            rs = pl.ds(p * size, size)
            for j, src in enumerate((bw, bm, bv, low)):
                go = pltpu.make_async_copy(
                    src.at[rs, :], outs[4 * i + j].at[rs, :], out_sem.at[i, p, j]
                )
                go.start()
                stores.append(go)
    x = lax.axis_index("tensor")
    mine = pl.ds(pl.multiple_of(x * 256, 256), 256)
    g_small = small_sum[:, mine]
    both = small_sum[16:20, :]
    first = jnp.where(x == 0, 1.0, 0.0)
    g_bias = jnp.concatenate(
        [
            (both[j : j + 1, :] * first + both[2 + j : 3 + j, :] * (1.0 - first))
            for j in range(2)
        ],
        axis=1,
    )
    for i, (g, rate, decay) in enumerate(
        ((g_small[0:9], 2.0, 0.05), (g_bias, 0.3, 0.0), (g_small[9:16], 0.3, 0.0))
    ):
        w = smalls[3 * i][...] if i < 2 else smalls[6][:, mine]
        new = adam(w, smalls[3 * i + 1][...], smalls[3 * i + 2][...], g, rate, decay)
        for j in range(3):
            small_outs[3 * i + j][...] = new[j]
    for go in stores:
        go.wait()


def adam_step(full, small_sum, mats, smalls):
    S = jax.ShapeDtypeStruct
    V = pltpu.VMEM
    mat_shapes = [(rows, cols) for rows, cols, _, _ in MATRICES]
    any_spec = pl.BlockSpec(memory_space=pl.ANY)
    vmem_spec = pl.BlockSpec(memory_space=V)
    small_shapes = [(9, 256)] * 3 + [(1, 1024)] * 3 + [(7, 256)] * 3
    return pl.pallas_call(
        adam_kernel,
        out_shape=tuple(
            S(shape, kind) for shape in mat_shapes for kind in (f32, f32, f32, bf16)
        )
        + tuple(S(shape, f32) for shape in small_shapes),
        in_specs=[vmem_spec] * 2 + [any_spec] * 12 + [vmem_spec] * 9,
        out_specs=[any_spec] * 16 + [vmem_spec] * 9,
        scratch_shapes=[V(shape, f32) for shape in mat_shapes for _ in range(3)]
        + [V(shape, bf16) for shape in mat_shapes]
        + [pltpu.SemaphoreType.DMA((4, 4, 3)), pltpu.SemaphoreType.DMA((4, 4, 4))],
        compiler_params=pltpu.CompilerParams(vmem_limit_bytes=48 * 1024 * 1024),
    )(full, small_sum, *mats, *smalls)


CHUNKS = (
    (DOWN, 1024), (DOWN + 1024, 1024), (UP, 1024), (UP + 1024, 1024), (OUT, 512),
    (IN + 1024, 512), (IN + 512, 512), (IN, 512),
)
D0, D1, U0, U1, O0, V0, K0, G0 = range(8)
SLOTS = 12
PLAN = {
    "D0": ((D0, 0),),
    "D1": ((D1, 0), (D0, 1)),
    "U0": ((U0, 0), (D1, 1)),
    "U1": ((U1, 0), (U0, 1)),
    "O": ((O0, 0), (U1, 1)),
    0: ((O0, 1),),
    1: ((D0, 2),),
    2: (),
    3: ((D0, 3),),
    "A2": ((V0, 0),),
    "A1": ((K0, 0), (V0, 1)),
    "A0": ((G0, 0), (K0, 1)),
    4: ((G0, 1), (D1, 2), (D0, 4)),
    5: (),
    6: ((D0, 5), (D1, 3)),
    7: ((U0, 2), (D0, 6), (D1, 4)),
    "B2": ((V0, 2),),
    "B1": ((K0, 2),),
    "B0": ((G0, 2),),
}
TAIL = (
    ((D0, 7), (D1, 5), (U0, 3), (U1, 2)),
    ((D1, 6), (U0, 4), (U1, 3), (O0, 2)),
    ((D1, 7), (U0, 5), (U1, 4), (O0, 3), (V0, 3)),
    ((U0, 6), (U1, 5), (O0, 4), (V0, 4), (K0, 3)),
    ((U0, 7), (U1, 6), (O0, 5), (V0, 5), (K0, 4), (G0, 3)),
    ((U1, 7), (O0, 6), (V0, 6), (K0, 5), (G0, 4)),
    ((O0, 7), (V0, 7), (K0, 6), (G0, 5)),
    ((V0, 8), (K0, 7), (G0, 6)),
    ((K0, 8), (G0, 7)),
    ((G0, 8),),
)


class Traffic:
    def __init__(self, images, refs):
        (self.tok, self.cot, self.w_in, self.w_out, self.w_up, self.w_down, self.own_small,
         self.out, self.gin, self.full, self.small_sum,
         self.gin_v, self.grads, self.gsmall, self.wi, self.wo, self.wu, self.wd, self.small,
         self.at_s, self.af_s, self.da_s, self.gp_s, self.mf_s, self.nb_s, self.lb_s, self.out_v,
         self.cores, self.xs, self.ys, self.zs, self.firsts,
         self.small_in, self.small_z, self.send, self.recv, self.ssend, self.srecv,
         self.wsend, self.wrecv, self.load, self.save) = refs
        self.images = images
        dp, x = lax.axis_index("dp"), lax.axis_index("tensor")
        core, y, z = lax.rem(dp, 2), lax.rem(dp // 2, 2), dp // 4

        def at(zz, yy, cc, xx):
            return ((zz * 2 + yy) * 2 + cc, xx)

        self.x, self.core, self.y, self.z = x, core, y, z
        self.core_mate = at(z, y, 1 - core, x)
        self.x_mate = at(z, y, core, 1 - x)
        self.y_mate = at(z, 1 - y, core, x)
        self.z_others = [lax.rem(z + k, 4) for k in range(1, 4)]
        self.z_mates = [at(o, y, core, x) for o in self.z_others]
        self.loads = [
            pltpu.make_async_copy(src, dst, self.load.at[i])
            for i, (src, dst) in enumerate(
                (
                    (self.w_in.at[:, 0:256], self.mf_s.at[0, 0:512, :]),
                    (self.w_in.at[:, 256:512], self.mf_s.at[1, 0:512, :]),
                    (self.w_in.at[:, 512:768], self.gp_s.at[0, 0:512, :]),
                    (self.w_out, self.da_s.at[512:768, :]),
                    (self.w_up.at[:, 0:512], self.da_s.at[0:512, :]),
                    (self.w_up.at[:, 512:1024], self.af_s.at[0:512, :]),
                    (self.w_down.at[0:512, :], self.gin_v.at[0:512, :]),
                    (self.w_down.at[512:896, :], self.af_s.at[512:896, :]),
                    (self.w_down.at[896:1024, :], self.da_s.at[768:896, :]),
                    (self.tok, self.nb_s.at[0 : images * WIN, :]),
                    (self.cot, self.lb_s.at[0 : images * WIN, :]),
                )
            )
        ]


    def weight_copy(self, src, dst, item, slot, mate):
        return pltpu.make_async_remote_copy(
            src_ref=src,
            dst_ref=dst,
            send_sem=self.wsend.at[item, slot],
            recv_sem=self.wrecv.at[item, slot],
            device_id=mate,
            device_id_type=MESH,
        )

    def view(self, item, half, yy, cc):
        quarter = yy * 2 + cc
        if item == 0:
            return self.wi.at[half, :, aligned(quarter * 128, 128), :]
        ref, size = ((self.wo, 64), (self.wu, 128), (self.wd, 256))[item - 1]
        return ref.at[half, aligned(quarter * size, size), :]

    def crossing(self, item):
        if item == 4:
            own = self.small.at[self.x]
        else:
            own = self.view(item, self.x, self.y, self.core)
        return self.weight_copy(own, own, item, 0, self.x_mate)

    def inward(self, item):
        got = self.view(item, 1 - self.x, self.y, self.core)
        return self.weight_copy(got, got, item, 1, self.core_mate)

    def aside(self, item):
        got = self.view(item, 1 - self.x, self.y, self.core)
        return self.weight_copy(got, got, item, 2, self.y_mate)

    def onward(self, item):
        got = self.view(item, 1 - self.x, 1 - self.y, self.core)
        return self.weight_copy(got, got, item, 3, self.core_mate)

    def cast(self, rows, size, source, target):
        def body(first, tile):
            here = pl.ds(first, tile)
            target[here, :] = source[here, :].astype(bf16)

        tile_loop(rows, size, body)

    def begin(self):
        for go in self.loads:
            go.start()
        barrier = pltpu.get_barrier_semaphore()
        for mate in (self.core_mate, self.x_mate, self.y_mate, *self.z_mates):
            pl.semaphore_signal(barrier, inc=1, device_id=mate, device_id_type=MESH)
        x = self.x
        self.small[x] = self.own_small[...]
        for go in self.loads[0:3]:
            go.wait()
        spreads = [spread(part, True) for part in range(3)]

        def body(first, tile):
            rows = pl.ds(first, tile)
            low = jnp.concatenate(
                [self.mf_s[0, rows, :], self.mf_s[1, rows, :], self.gp_s[0, rows, :]], axis=1
            ).astype(bf16)
            for part in range(3):
                self.wi[x, part, rows, :] = nn(low, spreads[part]).astype(bf16)

        tile_loop(512, 128, body)
        pl.semaphore_wait(barrier, 6)
        self.crossing(0).start()
        self.crossing(4).start()
        for go in self.loads[3:9]:
            go.wait()
        self.cast(256, 64, self.da_s.at[512:768, :], self.wo.at[x])
        self.crossing(1).start()
        self.cast(512, 64, self.da_s.at[0:512, :], self.wu.at[x, :, 0:512])
        self.cast(512, 64, self.af_s.at[0:512, :], self.wu.at[x, :, 512:1024])
        self.crossing(2).start()
        self.cast(512, 64, self.gin_v.at[0:512, :], self.wd.at[x, 0:512, :])
        self.cast(384, 64, self.af_s.at[512:896, :], self.wd.at[x, 512:896, :])
        self.cast(128, 64, self.da_s.at[768:896, :], self.wd.at[x, 896:1024, :])
        self.crossing(3).start()

    def tokens(self):
        self.loads[9].wait()

    def weights(self):
        pass

    def fore(self, i):
        def passed(item):
            self.crossing(item).wait()
            self.inward(item).start()
            self.aside(item).start()

        def turned(item):
            self.aside(item).wait()
            self.onward(item).start()

        def done(item):
            self.inward(item).wait()
            self.onward(item).wait()

        last = self.images - 1

        @pl.when(i == 1)
        def _():
            passed(0)

        @pl.when(i == 2)
        def _():
            passed(1)

        @pl.when(i == last)
        def _():
            turned(0)
            self.crossing(4).wait()
            done(0)

        @pl.when(i == last + 1)
        def _():
            passed(2)
            turned(1)

        @pl.when(i == last + 3)
        def _():
            passed(3)
            turned(2)

        @pl.when(i == last + 4)
        def _():
            turned(3)
            done(1)

    def cotangent(self):
        self.loads[10].wait()

    def arrived(self):
        for item in (2, 3):
            self.inward(item).wait()
            self.onward(item).wait()


    def output(self):
        self.out_v[...] = self.gin_v[...].astype(bf16)
        self.saving(0).start()

    def saving(self, i):
        src, dst = (
            (self.out_v, self.out),
            (self.gin_v, self.gin),
            (self.grads.at[0], self.full),
        )[i]
        return pltpu.make_async_copy(src, dst, self.save.at[i])

    def finished(self):
        self.saving(1).start()


    def copy(self, src, dst, chunk, slot, mate):
        return pltpu.make_async_remote_copy(
            src_ref=src,
            dst_ref=dst,
            send_sem=self.send.at[chunk, slot],
            recv_sem=self.recv.at[chunk, slot],
            device_id=mate,
            device_id_type=MESH,
        )

    def flights(self, c, s):
        base, R = CHUNKS[c]
        half, quarter, piece = R // 2, R // 4, R // 16
        x, y, z, core, grads = self.x, self.y, self.z, self.core, self.grads
        mine = base + core * half
        theirs = aligned(base + (1 - core) * half, half)
        if c >= V0:
            if s == 0:
                src = grads.at[1 - x, theirs, :]
                return [self.copy(src, self.firsts[c - V0], c, 11, self.core_mate)]
            if s == 1:
                return [self.copy(self.firsts[c - V0], self.xs[c], c, 1, self.x_mate)]
            if s == 2:
                return [self.copy(grads.at[x, theirs, :], self.cores[c], c, 0, self.core_mate)]
            s -= 1
        else:
            if s == 0:
                return [self.copy(grads.at[:, theirs, :], self.cores[c], c, 0, self.core_mate)]
            if s == 1:
                return [self.copy(self.cores[c].at[1 - x], self.xs[c], c, 1, self.x_mate)]
        if s == 2:
            src = self.xs[c].at[aligned((1 - y) * quarter, quarter), :]
            return [self.copy(src, self.ys[c], c, 2, self.y_mate)]
        if s == 3:
            return [
                self.copy(
                    self.ys[c].at[aligned(self.z_others[k] * piece, piece), :],
                    self.zs[c].at[k],
                    c,
                    3 + k,
                    self.z_mates[k],
                )
                for k in range(3)
            ]
        if s == 4:
            own = grads.at[0, aligned(mine + y * quarter + z * piece, piece), :]
            return [self.copy(own, own, c, 6 + k, self.z_mates[k]) for k in range(3)]
        if s == 5:
            own = grads.at[0, aligned(mine + y * quarter, quarter), :]
            return [self.copy(own, own, c, 9, self.y_mate)]
        if s == 6:
            own = grads.at[0, aligned(mine, half), :]
            return [self.copy(own, own, c, 10, self.core_mate)]
        return []

    def stage(self, c, s):
        base, R = CHUNKS[c]
        half, quarter, piece = R // 2, R // 4, R // 16
        x, y, z, core, grads = self.x, self.y, self.z, self.core, self.grads
        mine = base + core * half
        late = c >= V0
        if s > 0 and not (late and s == 2):
            for flight in self.flights(c, s - 1):
                flight.wait()
        if late and s == 3:
            self.flights(c, 1)[0].wait()

        def total(target, *parts):
            out = None
            for part in parts:
                part = part.astype(f32)
                out = part if out is None else out + part
            return out.astype(bf16)

        cores, xs, ys, zs = self.cores[c], self.xs[c], self.ys[c], self.zs[c]
        step = s - 1 if late else s
        if late and s == 1:
            first = self.firsts[c - V0]

            def body(i, size):
                rows, own = pl.ds(i, size), aligned(mine + i, size)
                first[rows, :] = total(None, grads[1 - x, own, :], first[rows, :])

            tile_loop(half, 128, body)
        elif late and s == 3:

            def body(i, size):
                rows, own = pl.ds(i, size), aligned(mine + i, size)
                xs[rows, :] = total(None, grads[x, own, :], cores[rows, :], xs[rows, :])

            tile_loop(half, 128, body)
        elif not late and s == 1:

            def body(i, size):
                rows, own = pl.ds(i, size), aligned(mine + i, size)
                for t in range(2):
                    cores[t, rows, :] = total(None, grads[t, own, :], cores[t, rows, :])

            tile_loop(half, 128, body)
        elif not late and s == 2:

            def body(i, size):
                rows = pl.ds(i, size)
                xs[rows, :] = total(None, cores[x, rows, :], xs[rows, :])

            tile_loop(half, 128, body)
        elif step == 3:

            def body(i, size):
                rows, own = pl.ds(i, size), aligned(y * quarter + i, size)
                ys[rows, :] = total(None, xs[own, :], ys[rows, :])

            tile_loop(quarter, 128, body)
        elif step == 4:
            own = aligned(z * piece, piece)
            grads[0, aligned(mine + y * quarter + z * piece, piece), :] = total(
                None, ys[own, :], zs[0], zs[1], zs[2]
            )
        for flight in self.flights(c, s):
            flight.start()

    def small_flights(self, s):
        def small_copy(src, dst, slot, mate):
            return pltpu.make_async_remote_copy(
                src_ref=src,
                dst_ref=dst,
                send_sem=self.ssend.at[slot],
                recv_sem=self.srecv.at[slot],
                device_id=mate,
                device_id_type=MESH,
            )

        if s < 3:
            mate = (self.core_mate, self.x_mate, self.y_mate)[s]
            return [small_copy(self.small_z.at[s], self.small_in.at[s], s, mate)]
        return [
            small_copy(self.small_z.at[3], self.small_z.at[4 + self.z], 3 + k, self.z_mates[k])
            for k in range(3)
        ]

    def small_stage(self, s):
        small_z = self.small_z
        if s > 0:
            for flight in self.small_flights(s - 1):
                flight.wait()
        if s == 0:
            small_z[0] = self.gsmall[...]
        elif s <= 3:
            small_z[s] = small_z[s - 1] + self.small_in[s - 1]
        else:
            self.small_sum[...] = (small_z[4] + small_z[5]) + (small_z[6] + small_z[7])
            return
        if s == 3:
            small_z[4 + self.z] = small_z[3]
        for flight in self.small_flights(s):
            flight.start()

    def point(self, name):
        for c, s in PLAN[name]:
            self.stage(c, s)

    def back(self, i):
        for k in range(2 * self.images):
            if PLAN[k]:

                @pl.when(i == k)
                def _(k=k):
                    self.point(k)

    def end(self):
        self.small_stage(0)
        for k, wave in enumerate(TAIL):
            for c, s in wave:
                self.stage(c, s)
            if k < 4:
                self.small_stage(k + 1)
        self.saving(2).start()
        for i in range(3):
            self.saving(i).wait()


def main_kernel(images, counts, tok, cot, w_in, w_out, w_up, w_down, own_small, vecs,
                out, gin, full, small_sum, *scratch):
    n = len(block_scratch(images))
    inner, rest = scratch[:n], scratch[n:]
    gin_v, grads, gsmall, wi, wo, wu, wd, small = rest[:8]
    rest = rest[8:]
    cores, xs, ys, zs = (rest[8 * i : 8 * i + 8] for i in range(4))
    firsts = rest[32:35]
    x_s, co_s, at_s, af_s, da_s, gp_s, mf_s, na_s, nb_s, lb_s = inner[:10]
    traffic = Traffic(
        images,
        (tok, cot, w_in, w_out, w_up, w_down, own_small, out, gin, full, small_sum,
         gin_v, grads, gsmall, wi, wo, wu, wd, small,
         at_s, af_s, da_s, gp_s, mf_s, nb_s, lb_s, co_s.at[0 : images * WIN, :],
         cores, xs, ys, zs, firsts, *rest[35:]),
    )
    x = lax.axis_index("tensor")
    limit = counts[lax.axis_index("dp")] - x * images
    traffic.begin()
    block_body(
        images, limit, x, traffic, wi, wo, wu, wd, small, vecs, gin_v, grads, gsmall, *inner
    )
    traffic.end()


def main_call(counts, tok, cot, w_in, w_out, w_up, w_down, own_small, vecs):
    images = tok.shape[0] // WIN
    S = jax.ShapeDtypeStruct
    V = pltpu.VMEM
    away = pl.BlockSpec(memory_space=pl.ANY)
    here = pl.BlockSpec(memory_space=V)
    sizes = [R for _, R in CHUNKS]
    dma = pltpu.SemaphoreType.DMA
    return pl.pallas_call(
        functools.partial(main_kernel, images),
        out_shape=(
            S(tok.shape, bf16),
            S(tok.shape, f32),
            S((GROWS, 256), bf16),
            S((24, D), f32),
        ),
        in_specs=[pl.BlockSpec(memory_space=pltpu.SMEM)] + [away] * 6 + [here] * 2,
        out_specs=[away] * 3 + [here],
        scratch_shapes=block_scratch(images)
        + [
            V(tok.shape, f32),
            V((2, GROWS, 256), bf16),
            V((24, D), f32),
            V((2, 3, D, 256), bf16),
            V((2, 256, D), bf16),
            V((2, D, 1024), bf16),
            V((2, 1024, D), bf16),
            V((2, 16, 256), f32),
        ]
        + [V((2, R // 2, 256), bf16) for R in sizes[:5]]
        + [V((R // 2, 256), bf16) for R in sizes[5:]]
        + [V((R // 2, 256), bf16) for R in sizes]
        + [V((R // 4, 256), bf16) for R in sizes]
        + [V((3, R // 16, 256), bf16) for R in sizes]
        + [V((R // 2, 256), bf16) for R in sizes[5:]]
        + [
            V((3, 24, D), f32),
            V((8, 24, D), f32),
            dma((8, SLOTS)),
            dma((8, SLOTS)),
            dma((6,)),
            dma((6,)),
            dma((5, 4)),
            dma((5, 4)),
            dma((11,)),
            dma((3,)),
        ],
        compiler_params=pltpu.CompilerParams(
            collective_id=1, has_side_effects=True, vmem_limit_bytes=63 * 1024 * 1024
        ),
    )(counts, tok, cot, w_in, w_out, w_up, w_down, own_small, vecs)


def local(
    tokens, cotangent, image_counts,
    w_in, m_in, v_in, w_out, m_out, v_out, w_up, m_up, v_up, w_down, m_down, v_down,
    kernel, m_kernel, v_kernel, up_bias, m_bias, v_bias, vectors, m_vectors, v_vectors,
):
    own_small = jnp.concatenate(
        [kernel, up_bias.reshape(4, 256), jnp.zeros((3, 256), f32)], axis=0
    )
    out, grad_in, full, small_sum = main_call(
        image_counts, tokens, cotangent, w_in, w_out, w_up, w_down, own_small, vectors
    )
    new = adam_step(
        full,
        small_sum,
        (w_down, m_down, v_down, w_up, m_up, v_up, w_out, m_out, v_out, w_in, m_in, v_in),
        (kernel, m_kernel, v_kernel)
        + tuple(a.reshape(1, -1) for a in (up_bias, m_bias, v_bias))
        + (vectors, m_vectors, v_vectors),
    )
    down, up, mid, first = new[:4], new[4:8], new[8:12], new[12:16]
    bias = tuple(a.reshape(-1) for a in new[19:22])
    return (out, grad_in, *first, *mid, *up, *down, *new[16:19], *bias, *new[22:25])


def general(
    tokens, cotangent, image_counts,
    w_in, m_in, v_in, w_out, m_out, v_out, w_up, m_up, v_up, w_down, m_down, v_down,
    kernel, m_kernel, v_kernel, up_bias, m_bias, v_bias, vectors, m_vectors, v_vectors,
):
    images = tokens.shape[0] // WIN
    place = lax.axis_index("tensor")
    live = image_counts[lax.axis_index("dp")] - place * images

    def whole(a, axis):
        return lax.all_gather(a, "tensor", axis=axis, tiled=True)

    wi = whole(w_in.astype(bf16), 1).reshape(D, 2, 8, 3, HD).transpose(1, 3, 0, 2, 4)
    wi = wi.reshape(2, 3, D, 256)
    wo = whole(w_out.astype(bf16), 0).reshape(2, 256, D)
    wd = whole(w_down.astype(bf16), 0).reshape(2, 1024, D)
    wu = whole(w_up.astype(bf16), 1).reshape(D, 2, 1024).transpose(1, 0, 2)
    small = jnp.concatenate(
        [
            whole(kernel, 1).reshape(9, 2, 256).transpose(1, 0, 2),
            whole(up_bias, 0).reshape(2, 4, 256),
            jnp.zeros((2, 3, 256), f32),
        ],
        axis=1,
    )
    out, grad_in, grads, gs = block(
        live.reshape(1), tokens, cotangent, wi, wo, wu, wd, small, vectors
    )
    grads = grads.astype(f32)

    def columns(first, rows, count):
        part = grads[:, first : first + rows * count].reshape(2, count, rows, 256)
        return part

    g_down = grads[:, DOWN:UP].reshape(2, 2, 2, 512, 256).transpose(0, 1, 3, 2, 4).reshape(FF, D)
    g_up = columns(UP, 512, 4).transpose(2, 0, 1, 3).reshape(D, FF)
    g_out = columns(OUT, 256, 2).transpose(0, 2, 1, 3).reshape(D, D)
    g_in = columns(IN, 512, 3).reshape(2, 3, D, 8, HD).transpose(2, 0, 3, 1, 4).reshape(D, 3 * D)

    def owned(a, axis):
        return lax.psum(lax.psum_scatter(a, "tensor", scatter_dimension=axis, tiled=True), "dp")

    g_in, g_out, g_up, g_down = owned(g_in, 1), owned(g_out, 0), owned(g_up, 1), owned(g_down, 0)
    g_kernel, g_bias, g_vectors = owned(gs[0:9], 1), owned(gs[16:20].reshape(-1), 0), owned(gs[9:16], 1)
    vector_width = m_vectors.shape[1]
    own_vectors = lax.dynamic_slice_in_dim(vectors, place * vector_width, vector_width, 1)
    results = [out, grad_in]
    for w, m, v, g, rate in (
        (w_in, m_in, v_in, g_in, D**-0.5),
        (w_out, m_out, v_out, g_out, (D // HD) ** -0.5),
        (w_up, m_up, v_up, g_up, D**-0.5),
        (w_down, m_down, v_down, g_down, FF**-0.5),
    ):
        new = adam(w, m, v, g, rate, 0.05)
        results += [*new, new[0].astype(bf16)]
    results += adam(kernel, m_kernel, v_kernel, g_kernel, 2.0, 0.05)
    results += adam(up_bias, m_bias, v_bias, g_bias, 0.3, 0.0)
    results += adam(own_vectors, m_vectors, v_vectors, g_vectors, 0.3, 0.0)
    return tuple(results)


def solution(mesh):
    rows, columns = P("tensor", None), P(None, "tensor")
    tokens = P(("dp", "tensor"), None)
    mats = (columns,) * 3 + (rows,) * 3 + (columns,) * 3 + (rows,) * 3
    news = (columns,) * 4 + (rows,) * 4 + (columns,) * 4 + (rows,) * 4
    pairs = mesh.shape["dp"] == 16 and mesh.shape["tensor"] == 2
    return jax.shard_map(
        local if pairs else general,
        mesh=mesh,
        in_specs=(tokens, tokens, P(), *mats)
        + (columns,) * 3
        + (P("tensor"),) * 3
        + (P(), columns, columns),
        out_specs=(tokens, tokens, *news) + (columns,) * 3 + (P("tensor"),) * 3 + (columns,) * 3,
        check_vma=False,
    )
```

```python
import functools
import jax
import jax.numpy as jnp
from jax import lax
from jax.experimental import pallas as pl
from jax.experimental.pallas import tpu as pltpu
from jax.sharding import PartitionSpec as P

D = 512
HD = 32
FF = 2048
SIDE = 14
WIDE = 16
WIN = SIDE * SIDE
ROWS = SIDE * WIDE
KEYS = 256
GROUPS = D // 128
STEP = 5
DOWN, UP, OUT, IN, GROWS = 0, 2048, 4096, 4608, 6144
MESH = pl.DeviceIdType.MESH
eps = 1e-05
f32 = jnp.float32
bf16 = jnp.bfloat16
C0 = 0.7978845608028654
C1 = 0.044715


def nn(a, b):
    return lax.dot_general(a, b, (((1,), (0,)), ((), ())), preferred_element_type=f32)


def nt(a, b):
    return lax.dot_general(a, b, (((1,), (1,)), ((), ())), preferred_element_type=f32)


def tn(a, b):
    return lax.dot_general(a, b, (((0,), (0,)), ((), ())), preferred_element_type=f32)


def normed(x):
    c = x - jnp.mean(x, axis=-1, keepdims=True)
    r = lax.rsqrt(jnp.mean(c * c, axis=-1, keepdims=True) + eps)
    return c * r, r


def norm_back(u, xhat, r):
    return r * (
        u
        - jnp.mean(u, axis=-1, keepdims=True)
        - xhat * jnp.mean(u * xhat, axis=-1, keepdims=True)
    )


def gelu_pair(x):
    x2 = x * x
    t = 0.5 * jnp.tanh(x * (C0 + (C0 * C1) * x2))
    h = 0.5 + t
    value = x * h
    return value, h + value * ((0.5 - t) * (2.0 * C0 + (6.0 * C0 * C1) * x2))


def gelu(x):
    return x * (0.5 + 0.5 * jnp.tanh(x * (C0 + (C0 * C1) * (x * x))))


def row_sum(x):
    return jnp.sum(x, axis=0, keepdims=True)


def shift_rows(x, by):
    z = jnp.zeros((abs(by), x.shape[1]), x.dtype)
    if by > 0:
        return jnp.concatenate([z, x[:-by]], axis=0)
    return jnp.concatenate([x[-by:], z], axis=0)


def roll1(x, by):
    return pltpu.roll(x, by % x.shape[0], 0)


def pool(c):
    s = c + roll1(c, 1) + roll1(c, -1)
    return s + shift_rows(s, WIDE) + shift_rows(s, -WIDE)


def block_body(images, limit, first_half, hooks, wi, wo, wu, wd, small, vecs,
               gin, grads, gsmall,
               x_s, co_s, at_s, af_s, da_s, gp_s, mf_s, na_s, nb_s, lb_s, la_s, mx_s,
               q_s, k_s, v_s, dm_s, hd_s, dp_s, pj_s, p_s, taps_s, ds_s):
    gain_a, shift_a, gain_b, shift_b, scale_a, scale_f, bias_f = (
        vecs[i : i + 1, :] for i in range(7)
    )
    gsmall[...] = jnp.zeros_like(gsmall)
    dn_s = at_s
    gtaps = taps_s
    gtaps[...] = jnp.zeros_like(gtaps)
    blank = jnp.zeros((KEYS - ROWS, 256), bf16)
    for ref in (q_s, k_s, v_s, dm_s):
        for t in range(2):
            for n in range(images):
                ref[t, n * KEYS + ROWS : (n + 1) * KEYS, :] = blank

    cell = lax.broadcasted_iota(jnp.int32, (ROWS, 1), 0)
    inside = lax.rem(cell, WIDE) < SIDE
    lane = lax.broadcasted_iota(jnp.int32, (1, 128), 1)
    head_masks = [(lane // HD) == h for h in range(4)]
    key_row = lax.broadcasted_iota(jnp.int32, (KEYS, 128), 0)
    key_lane = lax.broadcasted_iota(jnp.int32, (KEYS, 128), 1)
    key_pad = (lax.rem(key_row, WIDE) >= SIDE) | (key_row >= ROWS)
    key_block = jnp.where(key_pad & (key_lane == 0), -1e30, 0.0).astype(bf16)
    one_block = jnp.where(key_lane == 0, 1.0, 0.0).astype(bf16)

    def padded(n):
        return pl.ds(pl.multiple_of(n * ROWS, WIDE), ROWS)

    def held(n):
        return pl.ds(pl.multiple_of(n * KEYS, WIDE), ROWS)

    def whole(n):
        return pl.ds(pl.multiple_of(n * KEYS, WIDE), KEYS)

    def masked(h, a):
        return jnp.where(head_masks[h], a, jnp.zeros_like(a))

    def prepare(n, carry):
        rows = padded(n)
        xhat, _ = normed(x_s[rows, :].astype(f32))
        na_s[rows, :] = (xhat * gain_a + shift_a).astype(bf16)
        return carry

    def tap(t, i, ls):
        return small[t, pl.ds(i, 1), ls]

    def attend(t, n):
        rows = padded(n)
        na = na_s[rows, :]
        k_s[t, held(n), :] = nn(na, wi[t, 1]).astype(bf16)
        v_s[t, held(n), :] = nn(na, wi[t, 2]).astype(bf16)
        for g in range(2):
            ls = slice(g * 128, (g + 1) * 128)
            gp = nn(na, wi[t, 0, :, ls])
            gp_s[t, rows, ls] = gp
            field = jnp.where(inside, gelu(gp), 0.0)
            back, ahead = roll1(field, 1), roll1(field, -1)
            conv = None
            for a in range(3):
                part = (
                    tap(t, 3 * a, ls) * back
                    + tap(t, 3 * a + 1, ls) * field
                    + tap(t, 3 * a + 2, ls) * ahead
                )
                if a != 1:
                    part = shift_rows(part, WIDE * (1 - a))
                conv = part if conv is None else conv + part
            pooled = pool(jnp.where(inside, conv, 0.0)) * (HD ** (-0.5) / 9.0)
            q_s[t, held(n), ls] = pooled.astype(bf16)
        for g in range(2):
            ls = slice(g * 128, (g + 1) * 128)
            qa = jnp.concatenate([q_s[t, whole(n), ls], one_block], axis=1)
            kg = k_s[t, whole(n), ls]
            vt = jnp.transpose(v_s[t, whole(n), ls])
            mixed = []
            keys = jnp.concatenate(
                [jnp.concatenate([masked(h, kg), key_block], axis=1) for h in range(4)], axis=0
            )
            scores = nt(keys, qa)
            for h in range(4):
                hs = slice(h * KEYS, (h + 1) * KEYS)
                s = scores[hs]
                e = jnp.exp(s - jnp.max(s, axis=0, keepdims=True))
                p_s[t, n * 2 + g, :, hs] = (e * (1.0 / jnp.sum(e, axis=0, keepdims=True))).astype(bf16)
            for h in range(4):
                p = p_s[t, n * 2 + g, :, h * KEYS : (h + 1) * KEYS]
                mixed.append(nn(vt[h * HD : (h + 1) * HD], p))
            mix = jnp.transpose(jnp.concatenate(mixed, axis=0))[:ROWS]
            mf_s[t, rows, ls] = mix
            mx_s[t, rows, ls] = mix.astype(bf16)

    def finish(n, carry):
        rows = padded(n)
        attn = nn(mx_s[0, rows, :], wo[0]) + nn(mx_s[1, rows, :], wo[1])
        at_s[rows, :] = attn
        after = x_s[rows, :].astype(f32) + scale_a * attn
        af_s[rows, :] = after
        xhat, _ = normed(after)
        nb_s[rows, :] = (xhat * gain_b + shift_b).astype(bf16)
        lb_s[rows, :] = (scale_f * co_s[rows, :].astype(f32)).astype(bf16)
        return carry

    def feed(u, n):
        rows = padded(n)
        lb = lb_s[rows, :]
        nb = nb_s[rows, :]
        us = slice(u * 512, (u + 1) * 512)
        for t in range(2):
            c = 2 * t + u
            cs = slice(c * 512, (c + 1) * 512)
            unit_bias = jnp.concatenate(
                [small[t, 9 + 2 * u + j : 10 + 2 * u + j, :] for j in range(2)], axis=1
            )
            value, slope = gelu_pair(nn(nb, wu[t, :, us]) + unit_bias)
            hd_s[rows, cs] = value.astype(bf16)
            d_pre = slope * nt(lb, wd[t, us, :])
            gsmall[16 + c : 17 + c, :] += row_sum(d_pre)
            dp_s[rows, cs] = d_pre.astype(bf16)

    def digest(n, carry):
        rows = padded(n)
        branch = nn(hd_s[rows, 0:1024], wd[0]) + nn(hd_s[rows, 1024:2048], wd[1])
        d_nb = nt(dp_s[rows, 0:1024], wu[0]) + nt(dp_s[rows, 1024:2048], wu[1])
        co = co_s[rows, :].astype(f32)
        after = af_s[rows, :]
        xhat, r = normed(after)
        moved = branch + bias_f
        live = (n < limit).astype(f32)
        af_s[rows, :] = (after + scale_f * moved) * live
        gsmall[14:15, :] += row_sum(co * moved)
        gsmall[15:16, :] += scale_f * row_sum(co)
        gsmall[11:12, :] += row_sum(d_nb * xhat)
        gsmall[12:13, :] += row_sum(d_nb)
        d_after = co + norm_back(gain_b * d_nb, xhat, r)
        da_s[rows, :] = d_after
        gsmall[13:14, :] += row_sum(d_after * at_s[rows, :])
        la = (scale_a * d_after).astype(bf16)
        la_s[rows, :] = la
        for t in range(2):
            dm_s[t, held(n), :] = nt(la, wo[t]).astype(bf16)
        hooks.turn("d", n, images)
        return carry

    pick_row = lax.broadcasted_iota(jnp.int32, (256, 128), 0)
    pick_lane = lax.broadcasted_iota(jnp.int32, (256, 128), 1)
    pick = jnp.where(
        (lax.rem(pick_row, 128) // HD == lax.rem(pick_lane, 4)) & (pick_lane < 8), 1.0, 0.0
    ).astype(bf16)

    def split(a):
        high = a.astype(bf16)
        return high, (a - high.astype(f32)).astype(bf16)

    def inner_block(a):
        sums = nn(jnp.concatenate(split(a), axis=1), pick)
        high, low = split(sums)
        return jnp.where(lane < 4, high, low)

    blank_rows = jnp.zeros((KEYS - ROWS, 128), bf16)

    minus = [
        jnp.where((lane == h) | (lane == h + 4), -1.0, 0.0).astype(bf16) for h in range(4)
    ]

    def recede(t, n, turn):
        rows = padded(n)
        for g in range(2):
            ls = slice(g * 128, (g + 1) * 128)
            inner = inner_block(dm_s[t, held(n), ls].astype(f32) * mf_s[t, rows, ls])
            dmg = dm_s[t, whole(n), ls]
            left = jnp.concatenate(
                [dmg, jnp.concatenate([inner, blank_rows], axis=0)], axis=1
            )
            qg = q_s[t, whole(n), ls]
            kg = k_s[t, whole(n), ls]
            vg = v_s[t, whole(n), ls]
            kt = jnp.transpose(kg)
            dqs = []
            right = jnp.concatenate(
                [
                    jnp.concatenate([masked(h, vg), jnp.broadcast_to(minus[h], (KEYS, 128))], axis=1)
                    for h in range(4)
                ],
                axis=0,
            )
            d_probs = nt(right, left)
            for h in range(4):
                hs = slice(h * KEYS, (h + 1) * KEYS)
                e = p_s[t, n * 2 + g, :, hs]
                ds_s[:, hs] = (e.astype(f32) * d_probs[hs]).astype(bf16)
            dv = nn(
                p_s[t, n * 2 + g], jnp.concatenate([masked(h, dmg) for h in range(4)], axis=0)
            )
            dk = nn(ds_s[...], jnp.concatenate([masked(h, qg) for h in range(4)], axis=0))
            for h in range(4):
                dqs.append(nn(kt[h * HD : (h + 1) * HD], ds_s[:, h * KEYS : (h + 1) * KEYS]))
            dq = jnp.transpose(jnp.concatenate(dqs, axis=0))[:ROWS]
            pj_s[t, 1, rows, ls] = dk[:ROWS].astype(bf16)
            pj_s[t, 2, rows, ls] = dv[:ROWS].astype(bf16)
            value, slope = gelu_pair(gp_s[t, rows, ls])
            field = jnp.where(inside, value, 0.0)
            d_conv = jnp.where(inside, pool(dq * (HD ** (-0.5) / 9.0)), 0.0)
            shifted = (roll1(field, 1), field, roll1(field, -1))
            d_cols = [None, None, None]
            for a in range(3):
                moved = d_conv if a == 1 else shift_rows(d_conv, WIDE * (a - 1))
                for b in range(3):
                    i = 3 * a + b
                    gtaps[t, i : i + 1, ls] += row_sum(moved * shifted[b])
                    term = tap(t, i, ls) * moved
                    d_cols[b] = term if d_cols[b] is None else d_cols[b] + term
            d_field = roll1(d_cols[0], -1) + d_cols[1] + roll1(d_cols[2], 1)
            pj_s[t, 0, rows, ls] = jnp.where(inside, slope * d_field, 0.0).astype(bf16)
            hooks.turn("r", turn + g, 4 * images)
        d_na = None
        for part in range(3):
            term = nt(pj_s[t, part, rows, :], wi[t, part])
            d_na = term if d_na is None else d_na + term
        return d_na

    def rise(n, carry):
        rows = padded(n)
        d_na = dn_s[rows, :]
        xhat, r = normed(x_s[rows, :].astype(f32))
        gsmall[9:10, :] += row_sum(d_na * xhat)
        gsmall[10:11, :] += row_sum(d_na)
        da_s[rows, :] += norm_back(gain_a * d_na, xhat, r)
        return carry

    def narrow_rows(target, source):
        for i in range(images * SIDE):
            target[i * SIDE : (i + 1) * SIDE, :] = source[i * WIDE : i * WIDE + SIDE, :]

    def store_down(u):
        for t in range(2):
            cs = slice((2 * t + u) * 512, (2 * t + u + 1) * 512)
            down = tn(hd_s[:, cs], lb_s[...]).astype(bf16)
            for j in range(2):
                first = DOWN + (2 * u + j) * 512
                grads[t, first : first + 512, :] = down[:, j * 256 : (j + 1) * 256]

    def store_up(u):
        for t in range(2):
            cs = slice((2 * t + u) * 512, (2 * t + u + 1) * 512)
            up = tn(nb_s[...], dp_s[:, cs]).astype(bf16)
            for j in range(2):
                first = UP + (2 * u + j) * 512
                grads[t, first : first + 512, :] = up[:, j * 256 : (j + 1) * 256]

    def store_out():
        for t in range(2):
            g_out = tn(mx_s[t], la_s[...]).astype(bf16)
            for j in range(2):
                first = OUT + j * 256
                grads[t, first : first + 256, :] = g_out[:, j * 256 : (j + 1) * 256]

    def store_in(t, part):
        first = IN + part * 512
        grads[t, first : first + 512, :] = tn(na_s[...], pj_s[t, part]).astype(bf16)

    def widen(source, spares, target, scaled):
        temp = at_s
        temp[0 : images * WIN, :] = source[0 : images * WIN, :].astype(f32)
        for first, width, spare in spares:
            cs = slice(first, first + width)
            pad = jnp.zeros((WIDE - SIDE, width), f32)
            for n in range(images):
                for i in range(n * SIDE, (n + 1) * SIDE):
                    cells = temp[i * SIDE : (i + 1) * SIDE, cs]
                    if scaled:
                        cells = cells * (n < limit).astype(f32)
                    spare[i * WIDE : i * WIDE + SIDE, :] = cells
                    spare[i * WIDE + SIDE : (i + 1) * WIDE, :] = pad
            target[:, cs] = spare[...].astype(bf16)

    loop = lax.fori_loop
    hooks.tokens()
    widen(nb_s, [(t * 256, 256, gp_s.at[t]) for t in range(2)], x_s, False)
    loop(0, images, prepare, 0)
    hooks.weights()
    other_half = 1 - first_half

    def fore(i, carry):
        later = i // images
        attend(first_half + (other_half - first_half) * later, lax.rem(i, images))
        hooks.fore(i)
        return carry

    loop(0, 2 * images, fore, 0)
    hooks.cotangent()
    widen(lb_s, [(0, D, da_s)], co_s, True)
    loop(0, images, finish, 0)
    hooks.arrived()

    def feed_first(n, carry):
        feed(0, n)
        return carry

    def feed_second(n, carry):
        feed(1, n)
        hooks.turn("f", n, images)
        return carry

    loop(0, images, feed_first, 0)
    store_down(0)
    hooks.point("D0")
    store_up(0)
    hooks.point("U0")
    loop(0, images, feed_second, 0)
    store_down(1)
    hooks.point("D1")
    store_up(1)
    hooks.point("U1")
    loop(0, images, digest, 0)
    store_out()
    hooks.point("O")
    narrow_rows(gin, af_s)
    hooks.output()
    hooks.point("N")

    def aft(n, carry):
        dn_s[padded(n), :] = recede(other_half, n, 2 * n)
        return carry

    loop(0, images, aft, 0)
    for part in (2, 1, 0):
        store_in(other_half, part)
        hooks.point("A%d" % part)

    def aft2(n, carry):
        dn_s[padded(n), :] += recede(first_half, n, 2 * (images + n))
        return carry

    loop(0, images, aft2, 0)
    for part in (2, 1, 0):
        store_in(first_half, part)
        hooks.point("B%d" % part)
    loop(0, images, rise, 0)
    narrow_rows(gin, da_s)
    for t in range(2):
        gsmall[0:9, t * 256 : (t + 1) * 256] = gtaps[t, 0:9, :]
    hooks.finished()
    hooks.point("R")


class Quiet:
    def __init__(self, tok, cot, nb_s, lb_s, out, gin):
        self.refs = tok, cot, nb_s, lb_s, out, gin

    def tokens(self):
        tok, cot, nb_s, lb_s, _, _ = self.refs
        rows = tok.shape[0]
        nb_s[0:rows, :] = tok[...]
        lb_s[0:rows, :] = cot[...]

    def output(self):
        _, _, _, _, out, gin = self.refs
        out[...] = gin[...].astype(bf16)

    def point(self, name):
        pass

    def turn(self, name, i, count):
        pass

    fore = point

    def weights(self):
        pass

    cotangent = arrived = finished = weights


def block_kernel(images, lim, tok, cot, wi, wo, wu, wd, small, vecs, out, gin, grads, gsmall, *scratch):
    quiet = Quiet(tok, cot, scratch[8], scratch[9], out, gin)
    block_body(images, lim[0], 0, quiet, wi, wo, wu, wd, small, vecs, gin, grads, gsmall, *scratch)


def block_scratch(images):
    R = images * ROWS
    K = images * KEYS
    V = pltpu.VMEM
    return (
        [V((R, D), bf16)] * 2
        + [V((R, D), f32)] * 3
        + [V((2, R, 256), f32)] * 2
        + [V((R, D), bf16)] * 4
        + [V((2, R, 256), bf16)]
        + [V((2, K, 256), bf16)] * 4
        + [V((R, FF), bf16)] * 2
        + [
            V((2, 3, R, 256), bf16),
            V((2, images * 2, KEYS, 4 * KEYS), bf16),
            V((2, 16, 256), f32),
            V((KEYS, 4 * KEYS), bf16),
        ]
    )


def block(lim, tok, cot, wi, wo, wu, wd, small, vecs):
    images = tok.shape[0] // WIN
    S = jax.ShapeDtypeStruct
    V = pltpu.VMEM
    return pl.pallas_call(
        functools.partial(block_kernel, images),
        out_shape=(
            S(tok.shape, bf16),
            S(tok.shape, f32),
            S((2, GROWS, 256), bf16),
            S((24, D), f32),
        ),
        in_specs=[pl.BlockSpec(memory_space=pltpu.SMEM)] + [pl.BlockSpec(memory_space=V)] * 8,
        out_specs=[pl.BlockSpec(memory_space=V)] * 4,
        scratch_shapes=block_scratch(images),
        compiler_params=pltpu.CompilerParams(vmem_limit_bytes=62 * 1024 * 1024),
    )(lim, tok, cot, wi, wo, wu, wd, small, vecs)


def tile_loop(rows, size, body):
    if rows <= size:
        body(0, rows)
        return

    def step(i, carry):
        body(pl.multiple_of(i * size, size), size)
        return carry

    lax.fori_loop(0, rows // size, step, 0)


def aligned(first, size):
    return pl.ds(pl.multiple_of(first, 16), size)


def spread_four(part):
    a = lax.broadcasted_iota(jnp.int32, (384, 128), 1)
    b = lax.broadcasted_iota(jnp.int32, (384, 128), 0)
    return jnp.where(b == (a // HD) * (3 * HD) + part * HD + lax.rem(a, HD), 1.0, 0.0).astype(bf16)


def spread(part):
    a = lax.broadcasted_iota(jnp.int32, (256, 768), 0)
    b = lax.broadcasted_iota(jnp.int32, (256, 768), 1)
    return jnp.where(b == (a // HD) * (3 * HD) + part * HD + lax.rem(a, HD), 1.0, 0.0).astype(bf16)


def adam(w, m, v, g, rate, decay):
    half = 0.5 * g
    m = 0.5 * m + half
    v = 0.5 * v + half * g
    scale = 1.0 / (1.0 - 0.5**STEP)
    w = w - ((rate * scale) * m / (jnp.sqrt(v * scale) + 1e-08) + (rate * decay) * w)
    return w, m, v


def adam_tile(w, m, v, g, rate, decay):
    half = 0.5 * g
    m = 0.5 * m + half
    v = 0.5 * v + half * g
    scale = 1.0 / (1.0 - 0.5**STEP)
    seen = v * scale
    below = seen * lax.rsqrt(seen) + 1e-08
    inverse = pl.reciprocal(below, approx=True)
    inverse = inverse * (2.0 - below * inverse)
    w = w - ((rate * scale) * m * inverse + (rate * decay) * w)
    return w, m, v


MATRICES = (
    (1024, 512, FF**-0.5, 4, 64),
    (512, 1024, D**-0.5, 4, 32),
    (256, 512, (D // HD) ** -0.5, 1, 64),
    (512, 768, D**-0.5, 4, 64),
)


def adam_kernel(*refs):
    full, small_sum, raw_out, raw_gin = refs[:4]
    mats = refs[4:16]
    smalls = refs[16:25]
    outs = refs[25:41]
    small_outs = refs[41:50]
    out, gin = refs[50:52]
    bufs = refs[52:64]
    lows = refs[64:68]
    g_vm, out_vm, gin_vm, in_sem, out_sem, more_sem = refs[68:]
    g_load = pltpu.make_async_copy(full, g_vm, more_sem.at[2])
    g_load.start()
    loads = {}
    for i, (rows, cols, rate, pieces, tile) in enumerate(MATRICES):
        size = rows // pieces
        for p in range(pieces):
            rs = pl.ds(p * size, size)
            for j in range(3):
                go = pltpu.make_async_copy(
                    mats[3 * i + j].at[rs, :], bufs[3 * i + j].at[rs, :], in_sem.at[i, p, j]
                )
                go.start()
                loads[i, p, j] = go
    passing = [
        pltpu.make_async_copy(raw_out, out_vm, more_sem.at[0]),
        pltpu.make_async_copy(raw_gin, gin_vm, more_sem.at[1]),
    ]
    moves = [
        pltpu.make_async_copy(out_vm, out, more_sem.at[3]),
        pltpu.make_async_copy(gin_vm, gin, more_sem.at[4]),
    ]
    for go in passing:
        go.start()
    stores = []
    g_load.wait()
    for i, (rows, cols, rate, pieces, tile) in enumerate(MATRICES):
        size = rows // pieces
        bw, bm, bv = bufs[3 * i : 3 * i + 3]
        low = lows[i]
        spreads = [spread(part) for part in range(3)] if i == 3 else None
        for p in range(pieces):
            for j in range(3):
                loads[i, p, j].wait()

            def body(first, tile, i=i, p=p, bw=bw, bm=bm, bv=bv, low=low, rate=rate, size=size, spreads=spreads):
                rs = pl.ds(p * size + first, tile)
                if i == 0:
                    g = [
                        g_vm[pl.ds(DOWN + (p // 2 * 2 + j) * 512 + p % 2 * size + first, tile), :]
                        for j in range(2)
                    ]
                elif i == 1:
                    g = [g_vm[pl.ds(UP + j * 512 + p * size + first, tile), :] for j in range(4)]
                elif i == 2:
                    g = [g_vm[pl.ds(OUT + j * 256 + p * size + first, tile), :] for j in range(2)]
                else:
                    g = None
                    for part in range(3):
                        own = g_vm[pl.ds(IN + part * 512 + p * size + first, tile), :]
                        term = nn(own, spreads[part])
                        g = term if g is None else g + term
                if i < 3:
                    g = jnp.concatenate(g, axis=1).astype(f32)
                w, m, v = adam_tile(bw[rs, :], bm[rs, :], bv[rs, :], g, rate, 0.05)
                bw[rs, :] = w
                bm[rs, :] = m
                bv[rs, :] = v
                low[rs, :] = w.astype(bf16)

            tile_loop(size, tile, body)
            rs = pl.ds(p * size, size)
            for j, src in enumerate((bw, bm, bv, low)):
                go = pltpu.make_async_copy(
                    src.at[rs, :], outs[4 * i + j].at[rs, :], out_sem.at[i, p, j]
                )
                go.start()
                stores.append(go)
        if i == 0:
            for come, go in zip(passing, moves):
                come.wait()
                go.start()
    x = lax.axis_index("tensor")
    mine = pl.ds(pl.multiple_of(x * 256, 256), 256)
    g_small = small_sum[:, mine]
    both = small_sum[16:20, :]
    first = jnp.where(x == 0, 1.0, 0.0)
    g_bias = jnp.concatenate(
        [
            (both[j : j + 1, :] * first + both[2 + j : 3 + j, :] * (1.0 - first))
            for j in range(2)
        ],
        axis=1,
    )
    for i, (g, rate, decay) in enumerate(
        ((g_small[0:9], 2.0, 0.05), (g_bias, 0.3, 0.0), (g_small[9:16], 0.3, 0.0))
    ):
        w = smalls[3 * i][...] if i < 2 else smalls[6][:, mine]
        new = adam(w, smalls[3 * i + 1][...], smalls[3 * i + 2][...], g, rate, decay)
        for j in range(3):
            small_outs[3 * i + j][...] = new[j]
    for go in stores + moves:
        go.wait()


def adam_step(full, small_sum, raw_out, raw_gin, mats, smalls):
    S = jax.ShapeDtypeStruct
    V = pltpu.VMEM
    mat_shapes = [shape[:2] for shape in MATRICES]
    any_spec = pl.BlockSpec(memory_space=pl.ANY)
    vmem_spec = pl.BlockSpec(memory_space=V)
    small_shapes = [(9, 256)] * 3 + [(1, 1024)] * 3 + [(7, 256)] * 3
    return pl.pallas_call(
        adam_kernel,
        out_shape=tuple(
            S(shape, kind) for shape in mat_shapes for kind in (f32, f32, f32, bf16)
        )
        + tuple(S(shape, f32) for shape in small_shapes)
        + (S(raw_out.shape, bf16), S(raw_gin.shape, f32)),
        in_specs=[any_spec, vmem_spec, any_spec, any_spec] + [any_spec] * 12 + [vmem_spec] * 9,
        out_specs=[any_spec] * 16 + [vmem_spec] * 9 + [any_spec] * 2,
        scratch_shapes=[V(shape, f32) for shape in mat_shapes for _ in range(3)]
        + [V(shape, bf16) for shape in mat_shapes]
        + [
            V((GROWS, 256), bf16),
            V(raw_out.shape, bf16),
            V(raw_gin.shape, f32),
            pltpu.SemaphoreType.DMA((4, 4, 3)),
            pltpu.SemaphoreType.DMA((4, 4, 4)),
            pltpu.SemaphoreType.DMA((5,)),
        ],
        compiler_params=pltpu.CompilerParams(vmem_limit_bytes=62 * 1024 * 1024),
    )(full, small_sum, raw_out, raw_gin, *mats, *smalls)


CHUNKS = (
    (0, 1024),
    (2048, 1024),
    (1024, 1024),
    (3072, 1024),
    (4096, 512),
    (5632, 512),
    (5120, 512),
    (4608, 512),
)
LATE = 5
SLOTS = 12
PLAN = {
    'D0': ((0, 0),),
    'U0': ((1, 0),),
    'f0': ((0, 1),),
    'f1': ((1, 1),),
    'D1': ((2, 0),),
    'U1': ((3, 0),),
    'd0': ((2, 1), (3, 1), (0, 2),),
    'd3': ((1, 2), (0, 3),),
    'O': ((4, 0),),
    'r0': ((4, 1),),
    'r1': ((1, 3), (2, 2),),
    'r2': ((0, 4),),
    'r5': ((2, 3), (1, 4), (3, 2),),
    'r7': ((0, 5), (4, 2),),
    'A2': ((5, 0),),
    'A1': ((6, 0), (3, 3), (5, 1), (2, 4), (6, 1),),
    'A0': ((7, 0),),
    'r8': ((7, 1), (0, 6),),
    'r9': ((4, 3), (1, 5), (0, 7),),
    'r10': ((3, 4),),
    'r13': ((2, 5), (1, 6), (4, 4),),
    'r14': ((1, 7),),
    'B2': ((5, 2), (3, 5),),
    'B1': ((6, 2), (5, 3), (4, 5), (2, 6),),
    'B0': ((7, 2), (6, 3),),
    'R': ((7, 3), (3, 6), (2, 7),),
}
TAIL = (
    (3, 7), (5, 4), (4, 6), (4, 7), (6, 4), (5, 5),
    (7, 4), (6, 5), (5, 6), (7, 5), (6, 6), (5, 7),
    (5, 8), (7, 6), (6, 7), (6, 8), (7, 7), (7, 8),
)


ITEMS = ((0, 0, 64), (0, 64, 64), (1, 0, 64), (2, 0, 64), (2, 64, 64), (3, 0, 128), (3, 128, 128))


class Traffic:
    def __init__(self, images, refs):
        (self.tok, self.cot, self.w_in, self.w_out, self.w_up, self.w_down, self.taps, self.bias,
         self.out, self.gin, self.full, self.small_sum,
         self.gin_v, self.grads, self.gsmall, self.wi, self.wo, self.wu, self.wd, self.small,
         self.at_s, self.af_s, self.da_s, self.gp_s, self.mf_s, self.nb_s, self.lb_s, self.out_v,
         self.cores, self.xs, self.ys, self.zs, self.firsts,
         self.small_in, self.small_z, self.send, self.recv, self.ssend, self.srecv,
         self.wsend, self.wrecv, self.load, self.save) = refs
        self.images = images
        dp, x = lax.axis_index("dp"), lax.axis_index("tensor")
        core, y, z = lax.rem(dp, 2), lax.rem(dp // 2, 2), dp // 4

        def at(zz, yy, cc, xx):
            return ((zz * 2 + yy) * 2 + cc, xx)

        self.x, self.core, self.y, self.z = x, core, y, z
        self.core_mate = at(z, y, 1 - core, x)
        self.x_mate = at(z, y, core, 1 - x)
        self.y_mate = at(z, 1 - y, core, x)
        self.z_others = [lax.rem(z + k, 4) for k in range(1, 4)]
        self.z_mates = [at(o, y, core, x) for o in self.z_others]
        quarter = y * 2 + core
        self.quarter = quarter

        def load(i, src, dst):
            return pltpu.make_async_copy(src, dst, self.load.at[i])

        w_in, w_out, w_up, w_down = self.w_in, self.w_out, self.w_up, self.w_down
        at_s, af_s, da_s, mf_s, gin = self.at_s, self.af_s, self.da_s, self.mf_s, self.gin_v
        q_in, q_out = aligned(quarter * 128, 128), aligned(quarter * 64, 64)
        q_down = aligned(quarter * 256, 256)
        self.early = [
            load(0, w_in.at[q_in, 0:256], at_s.at[0:128, 0:256]),
            load(1, w_in.at[q_in, 256:512], at_s.at[0:128, 256:512]),
            load(2, w_in.at[q_in, 512:768], at_s.at[128:256, 0:256]),
            load(3, w_out.at[q_out, :], at_s.at[256:320, :]),
            load(4, w_up.at[q_in, 0:512], at_s.at[320:448, :]),
            load(5, w_up.at[q_in, 512:1024], at_s.at[448:576, :]),
            load(6, w_down.at[q_down, :], at_s.at[576:832, :]),
        ]
        self.own_in = [
            load(7, w_in.at[:, 0:256], mf_s.at[0, 0:512, :]),
            load(8, w_in.at[:, 256:512], mf_s.at[1, 0:512, :]),
            load(9, w_in.at[:, 512:768], gin.at[0:512, 0:256]),
        ]
        self.tok_load = load(10, self.tok, self.nb_s.at[0 : images * WIN, :])
        self.cot_load = load(11, self.cot, self.lb_s.at[0 : images * WIN, :])
        self.own_rest = [
            load(12, w_out.at[:, 0:256], gin.at[0:256, 256:512]),
            load(13, w_out.at[:, 256:512], gin.at[256:512, 256:512]),
            load(14, w_up.at[:, 0:512], da_s.at[0:512, :]),
            load(15, w_up.at[:, 512:1024], af_s.at[0:512, :]),
            load(16, w_down.at[0:256, :], da_s.at[512:768, :]),
            load(17, w_down.at[256:512, :], af_s.at[512:768, :]),
            load(18, w_down.at[512:768, :], gin.at[512:768, :]),
            load(19, w_down.at[768:896, :], da_s.at[768:896, :]),
            load(20, w_down.at[896:1024, :], af_s.at[768:896, :]),
        ]


    def weight_copy(self, src, dst, item, slot, mate):
        return pltpu.make_async_remote_copy(
            src_ref=src,
            dst_ref=dst,
            send_sem=self.wsend.at[item, slot],
            recv_sem=self.wrecv.at[item, slot],
            device_id=mate,
            device_id_type=MESH,
        )

    def view(self, item, half, yy, cc):
        kind, first, size = ITEMS[item]
        quarter = yy * 2 + cc
        if kind == 0:
            return self.wi.at[half, :, aligned(quarter * 128 + first, size), :]
        ref, rows = ((self.wo, 64), (self.wu, 128), (self.wd, 256))[kind - 1]
        return ref.at[half, aligned(quarter * rows + first, size), :]

    def crossing(self, item):
        if item == len(ITEMS):
            own = self.small.at[self.x]
        else:
            own = self.view(item, self.x, self.y, self.core)
        return self.weight_copy(own, own, item, 0, self.x_mate)

    def inward(self, item):
        got = self.view(item, 1 - self.x, self.y, self.core)
        return self.weight_copy(got, got, item, 1, self.core_mate)

    def aside(self, item):
        got = self.view(item, 1 - self.x, self.y, self.core)
        return self.weight_copy(got, got, item, 2, self.y_mate)

    def onward(self, item):
        got = self.view(item, 1 - self.x, 1 - self.y, self.core)
        return self.weight_copy(got, got, item, 3, self.core_mate)

    def permuted(self, pieces, rows):
        low = jnp.concatenate(pieces, axis=1).astype(bf16)
        for part in range(3):
            for j in range(2):
                four = nn(low[:, j * 384 : (j + 1) * 384], spread_four(part))
                self.wi[self.x, part, rows, j * 128 : (j + 1) * 128] = four.astype(bf16)

    def begin(self):
        for go in self.early:
            go.start()
        barrier = pltpu.get_barrier_semaphore()
        for mate in (self.core_mate, self.x_mate, self.y_mate, *self.z_mates):
            pl.semaphore_signal(barrier, inc=1, device_id=mate, device_id_type=MESH)
        for go in self.own_in:
            go.start()
        self.tok_load.start()
        x, quarter, at_s = self.x, self.quarter, self.at_s
        self.small[x, 0:9, :] = self.taps[...]
        for j in range(4):
            self.small[x, 9 + j : 10 + j, :] = self.bias[:, j * 256 : (j + 1) * 256]
        for go in self.early[0:3]:
            go.wait()
        self.permuted(
            [at_s[0:128, 0:256], at_s[0:128, 256:512], at_s[128:256, 0:256]],
            aligned(quarter * 128, 128),
        )
        pl.semaphore_wait(barrier, 6)
        self.crossing(0).start()
        self.crossing(1).start()
        self.crossing(len(ITEMS)).start()
        self.early[3].wait()
        self.wo[x, aligned(quarter * 64, 64), :] = at_s[256:320, :].astype(bf16)
        self.crossing(2).start()
        for go in self.early[4:6]:
            go.wait()
        rows = aligned(quarter * 128, 128)
        self.wu[x, rows, 0:512] = at_s[320:448, :].astype(bf16)
        self.wu[x, rows, 512:1024] = at_s[448:576, :].astype(bf16)
        self.crossing(3).start()
        self.crossing(4).start()
        self.early[6].wait()
        self.wd[x, aligned(quarter * 256, 256), :] = at_s[576:832, :].astype(bf16)
        self.crossing(5).start()
        self.crossing(6).start()
        self.cot_load.start()
        for go in self.own_rest:
            go.start()

    def tokens(self):
        self.tok_load.wait()

    def others(self, body):
        for j in range(4):

            @pl.when(self.quarter != j)
            def _(j=j):
                body(j)

    def weights(self):
        for go in self.own_in:
            go.wait()
        mf_s, gin = self.mf_s, self.gin_v

        def body(j):
            rows = slice(j * 128, (j + 1) * 128)
            self.permuted([mf_s[0, rows, :], mf_s[1, rows, :], gin[rows, 0:256]], rows)

        self.others(body)

    def passed(self, *items):
        for item in items:
            self.crossing(item).wait()
            self.inward(item).start()
            self.aside(item).start()

    def turned(self, *items):
        for item in items:
            self.aside(item).wait()
            self.onward(item).start()

    def done(self, *items):
        for item in items:
            self.inward(item).wait()
            self.onward(item).wait()

    def fore(self, i):
        last = self.images - 1
        for k, steps in {
            0: (("passed", 0), ("passed", 1)),
            1: (("turned", 0), ("passed", 2)),
            2: (("turned", 1),),
            last: (("done", 0), ("done", 1), ("passed", 3)),
            last + 1: (("turned", 2), ("passed", 4)),
            last + 2: (("turned", 3),),
            last + 3: (("passed", 5),),
            last + 4: (("turned", 4), ("passed", 6)),
        }.items():

            @pl.when(i == k)
            def _(k=k, steps=steps):
                for name, item in steps:
                    {"passed": self.passed, "turned": self.turned, "done": self.done}[name](item)
                if k == last:
                    self.crossing(len(ITEMS)).wait()

    def cotangent(self):
        self.done(2)
        for go in self.own_rest:
            go.wait()
        x, gin, da_s, af_s = self.x, self.gin_v, self.da_s, self.af_s

        def body(j):
            rows = slice(j * 64, (j + 1) * 64)
            self.wo[x, rows, 0:256] = gin[rows, 256:512].astype(bf16)
            self.wo[x, rows, 256:512] = gin[j * 64 + 256 : (j + 1) * 64 + 256, 256:512].astype(bf16)
            rows = slice(j * 128, (j + 1) * 128)
            self.wu[x, rows, 0:512] = da_s[rows, :].astype(bf16)
            self.wu[x, rows, 512:1024] = af_s[rows, :].astype(bf16)
            rows = slice(j * 256, (j + 1) * 256)
            if j < 3:
                self.wd[x, rows, :] = (da_s, af_s, gin)[j][512:768, :].astype(bf16)
            else:
                self.wd[x, 768:896, :] = da_s[768:896, :].astype(bf16)
                self.wd[x, 896:1024, :] = af_s[768:896, :].astype(bf16)

        self.others(body)
        self.cot_load.wait()

    def arrived(self):
        self.turned(5, 6)
        self.done(3, 4, 5, 6)


    def output(self):
        self.out_v[...] = self.gin_v[...].astype(bf16)
        self.saving(0).start()

    def saving(self, i):
        src, dst = (
            (self.out_v, self.out),
            (self.gin_v, self.gin),
            (self.grads.at[0], self.full),
        )[i]
        return pltpu.make_async_copy(src, dst, self.save.at[i])

    def finished(self):
        self.saving(1).start()


    def copy(self, src, dst, chunk, slot, mate):
        return pltpu.make_async_remote_copy(
            src_ref=src,
            dst_ref=dst,
            send_sem=self.send.at[chunk, slot],
            recv_sem=self.recv.at[chunk, slot],
            device_id=mate,
            device_id_type=MESH,
        )

    def flights(self, c, s):
        base, R = CHUNKS[c]
        half, quarter, piece = R // 2, R // 4, R // 16
        x, y, z, core, grads = self.x, self.y, self.z, self.core, self.grads
        mine = base + core * half
        theirs = aligned(base + (1 - core) * half, half)
        if c >= LATE:
            if s == 0:
                src = grads.at[1 - x, theirs, :]
                return [self.copy(src, self.firsts[c - LATE], c, 11, self.core_mate)]
            if s == 1:
                return [self.copy(self.firsts[c - LATE], self.xs[c], c, 1, self.x_mate)]
            if s == 2:
                return [self.copy(grads.at[x, theirs, :], self.cores[c], c, 0, self.core_mate)]
            s -= 1
        else:
            if s == 0:
                return [self.copy(grads.at[:, theirs, :], self.cores[c], c, 0, self.core_mate)]
            if s == 1:
                return [self.copy(self.cores[c].at[1 - x], self.xs[c], c, 1, self.x_mate)]
        if s == 2:
            src = self.xs[c].at[aligned((1 - y) * quarter, quarter), :]
            return [self.copy(src, self.ys[c], c, 2, self.y_mate)]
        if s == 3:
            return [
                self.copy(
                    self.ys[c].at[aligned(self.z_others[k] * piece, piece), :],
                    self.zs[c].at[k],
                    c,
                    3 + k,
                    self.z_mates[k],
                )
                for k in range(3)
            ]
        if s == 4:
            own = grads.at[0, aligned(mine + y * quarter + z * piece, piece), :]
            return [self.copy(own, own, c, 6 + k, self.z_mates[k]) for k in range(3)]
        if s == 5:
            own = grads.at[0, aligned(mine + y * quarter, quarter), :]
            return [self.copy(own, own, c, 9, self.y_mate)]
        if s == 6:
            own = grads.at[0, aligned(mine, half), :]
            return [self.copy(own, own, c, 10, self.core_mate)]
        return []

    def stage(self, c, s):
        base, R = CHUNKS[c]
        half, quarter, piece = R // 2, R // 4, R // 16
        x, y, z, core, grads = self.x, self.y, self.z, self.core, self.grads
        mine = base + core * half
        late = c >= LATE
        if s > 0 and not (late and s == 2):
            for flight in self.flights(c, s - 1):
                flight.wait()
        if late and s == 3:
            self.flights(c, 1)[0].wait()

        def total(*parts):
            out = None
            for part in parts:
                part = part.astype(f32)
                out = part if out is None else out + part
            return out.astype(bf16)

        cores, xs, ys, zs = self.cores[c], self.xs[c], self.ys[c], self.zs[c]
        step = s - 1 if late else s
        if late and s == 1:
            first = self.firsts[c - LATE]

            def body(i, size):
                rows, own = pl.ds(i, size), aligned(mine + i, size)
                first[rows, :] = total(grads[1 - x, own, :], first[rows, :])

            tile_loop(half, 128, body)
        elif late and s == 3:

            def body(i, size):
                rows, own = pl.ds(i, size), aligned(mine + i, size)
                xs[rows, :] = total(grads[x, own, :], cores[rows, :], xs[rows, :])

            tile_loop(half, 128, body)
        elif not late and s == 1:

            def body(i, size):
                rows, own = pl.ds(i, size), aligned(mine + i, size)
                for t in range(2):
                    cores[t, rows, :] = total(grads[t, own, :], cores[t, rows, :])

            tile_loop(half, 128, body)
        elif not late and s == 2:

            def body(i, size):
                rows = pl.ds(i, size)
                xs[rows, :] = total(cores[x, rows, :], xs[rows, :])

            tile_loop(half, 128, body)
        elif step == 3:

            def body(i, size):
                rows, own = pl.ds(i, size), aligned(y * quarter + i, size)
                ys[rows, :] = total(xs[own, :], ys[rows, :])

            tile_loop(quarter, 128, body)
        elif step == 4:
            own = aligned(z * piece, piece)
            grads[0, aligned(mine + y * quarter + z * piece, piece), :] = total(
                ys[own, :], zs[0], zs[1], zs[2]
            )
        for flight in self.flights(c, s):
            flight.start()

    def small_flights(self, s):
        def small_copy(src, dst, slot, mate):
            return pltpu.make_async_remote_copy(
                src_ref=src,
                dst_ref=dst,
                send_sem=self.ssend.at[slot],
                recv_sem=self.srecv.at[slot],
                device_id=mate,
                device_id_type=MESH,
            )

        if s < 3:
            mate = (self.core_mate, self.x_mate, self.y_mate)[s]
            return [small_copy(self.small_z.at[s], self.small_in.at[s], s, mate)]
        return [
            small_copy(self.small_z.at[3], self.small_z.at[4 + self.z], 3 + k, self.z_mates[k])
            for k in range(3)
        ]

    def small_stage(self, s):
        small_z = self.small_z
        if s > 0:
            for flight in self.small_flights(s - 1):
                flight.wait()
        if s == 0:
            small_z[0] = self.gsmall[...]
        elif s <= 3:
            small_z[s] = small_z[s - 1] + self.small_in[s - 1]
        else:
            self.small_sum[...] = (small_z[4] + small_z[5]) + (small_z[6] + small_z[7])
            return
        if s == 3:
            small_z[4 + self.z] = small_z[3]
        for flight in self.small_flights(s):
            flight.start()

    def point(self, name):
        for c, s in PLAN.get(name, ()):
            self.stage(c, s)

    def turn(self, name, i, count):
        for k in range(count):
            if name + str(k) in PLAN:

                @pl.when(i == k)
                def _(k=k):
                    self.point(name + str(k))

    def end(self):
        self.small_stage(0)
        gap = len(TAIL) // 6
        for k, (c, s) in enumerate(TAIL):
            self.stage(c, s)
            if k % gap == gap - 1 and k // gap < 4:
                self.small_stage(k // gap + 1)
        self.saving(2).start()
        for i in range(3):
            self.saving(i).wait()


def main_kernel(images, counts, tok, cot, w_in, w_out, w_up, w_down, taps, bias, vecs,
                out, gin, full, small_sum, *scratch):
    n = len(block_scratch(images))
    inner, rest = scratch[:n], scratch[n:]
    gin_v, grads, gsmall, wi, wo, wu, wd, small = rest[:8]
    rest = rest[8:]
    count = len(CHUNKS)
    cores, xs, ys, zs = (rest[count * i : count * (i + 1)] for i in range(4))
    rest = rest[4 * count :]
    firsts, rest = rest[: count - LATE], rest[count - LATE :]
    x_s, co_s, at_s, af_s, da_s, gp_s, mf_s, na_s, nb_s, lb_s = inner[:10]
    traffic = Traffic(
        images,
        (tok, cot, w_in, w_out, w_up, w_down, taps, bias, out, gin, full, small_sum,
         gin_v, grads, gsmall, wi, wo, wu, wd, small,
         at_s, af_s, da_s, gp_s, mf_s, nb_s, lb_s, co_s.at[0 : images * WIN, :],
         cores, xs, ys, zs, firsts, *rest),
    )
    x = lax.axis_index("tensor")
    limit = counts[lax.axis_index("dp")] - x * images
    traffic.begin()
    block_body(
        images, limit, x, traffic, wi, wo, wu, wd, small, vecs, gin_v, grads, gsmall, *inner
    )
    traffic.end()


def main_call(counts, tok, cot, w_in, w_out, w_up, w_down, taps, bias, vecs):
    images = tok.shape[0] // WIN
    S = jax.ShapeDtypeStruct
    V = pltpu.VMEM
    away = pl.BlockSpec(memory_space=pl.ANY)
    here = pl.BlockSpec(memory_space=V)
    sizes = [R for _, R in CHUNKS]
    dma = pltpu.SemaphoreType.DMA
    return pl.pallas_call(
        functools.partial(main_kernel, images),
        out_shape=(
            S(tok.shape, bf16),
            S(tok.shape, f32),
            S((GROWS, 256), bf16),
            S((24, D), f32),
        ),
        in_specs=[pl.BlockSpec(memory_space=pltpu.SMEM)] + [away] * 6 + [here] * 3,
        out_specs=[away] * 3 + [here],
        scratch_shapes=block_scratch(images)
        + [
            V(tok.shape, f32),
            V((2, GROWS, 256), bf16),
            V((24, D), f32),
            V((2, 3, D, 256), bf16),
            V((2, 256, D), bf16),
            V((2, D, 1024), bf16),
            V((2, 1024, D), bf16),
            V((2, 16, 256), f32),
        ]
        + [V((2, R // 2, 256), bf16) for R in sizes[:LATE]]
        + [V((R // 2, 256), bf16) for R in sizes[LATE:]]
        + [V((R // 2, 256), bf16) for R in sizes]
        + [V((R // 4, 256), bf16) for R in sizes]
        + [V((3, R // 16, 256), bf16) for R in sizes]
        + [V((R // 2, 256), bf16) for R in sizes[LATE:]]
        + [
            V((3, 24, D), f32),
            V((8, 24, D), f32),
            dma((len(sizes), SLOTS)),
            dma((len(sizes), SLOTS)),
            dma((6,)),
            dma((6,)),
            dma((8, 4)),
            dma((8, 4)),
            dma((21,)),
            dma((3,)),
        ],
        compiler_params=pltpu.CompilerParams(
            collective_id=1, has_side_effects=True, vmem_limit_bytes=63 * 1024 * 1024
        ),
    )(counts, tok, cot, w_in, w_out, w_up, w_down, taps, bias, vecs)


def local(
    tokens, cotangent, image_counts,
    w_in, m_in, v_in, w_out, m_out, v_out, w_up, m_up, v_up, w_down, m_down, v_down,
    kernel, m_kernel, v_kernel, up_bias, m_bias, v_bias, vectors, m_vectors, v_vectors,
):
    biases = tuple(a.reshape(1, -1) for a in (up_bias, m_bias, v_bias))
    raw_out, raw_gin, full, small_sum = main_call(
        image_counts, tokens, cotangent, w_in, w_out, w_up, w_down, kernel, biases[0], vectors
    )
    new = adam_step(
        full,
        small_sum,
        raw_out,
        raw_gin,
        (w_down, m_down, v_down, w_up, m_up, v_up, w_out, m_out, v_out, w_in, m_in, v_in),
        (kernel, m_kernel, v_kernel)
        + biases
        + (vectors, m_vectors, v_vectors),
    )
    down, up, mid, first = new[:4], new[4:8], new[8:12], new[12:16]
    bias = tuple(a.reshape(-1) for a in new[19:22])
    return (*new[25:27], *first, *mid, *up, *down, *new[16:19], *bias, *new[22:25])


def general(
    tokens, cotangent, image_counts,
    w_in, m_in, v_in, w_out, m_out, v_out, w_up, m_up, v_up, w_down, m_down, v_down,
    kernel, m_kernel, v_kernel, up_bias, m_bias, v_bias, vectors, m_vectors, v_vectors,
):
    images = tokens.shape[0] // WIN
    place = lax.axis_index("tensor")
    live = image_counts[lax.axis_index("dp")] - place * images

    def whole(a, axis):
        return lax.all_gather(a, "tensor", axis=axis, tiled=True)

    wi = whole(w_in.astype(bf16), 1).reshape(D, 2, 8, 3, HD).transpose(1, 3, 0, 2, 4)
    wi = wi.reshape(2, 3, D, 256)
    wo = whole(w_out.astype(bf16), 0).reshape(2, 256, D)
    wd = whole(w_down.astype(bf16), 0).reshape(2, 1024, D)
    wu = whole(w_up.astype(bf16), 1).reshape(D, 2, 1024).transpose(1, 0, 2)
    small = jnp.concatenate(
        [
            whole(kernel, 1).reshape(9, 2, 256).transpose(1, 0, 2),
            whole(up_bias, 0).reshape(2, 4, 256),
            jnp.zeros((2, 3, 256), f32),
        ],
        axis=1,
    )
    out, grad_in, grads, gs = block(
        live.reshape(1), tokens, cotangent, wi, wo, wu, wd, small, vectors
    )
    grads = grads.astype(f32)

    def columns(first, rows, count):
        part = grads[:, first : first + rows * count].reshape(2, count, rows, 256)
        return part

    g_down = grads[:, DOWN:UP].reshape(2, 2, 2, 512, 256).transpose(0, 1, 3, 2, 4).reshape(FF, D)
    g_up = columns(UP, 512, 4).transpose(2, 0, 1, 3).reshape(D, FF)
    g_out = columns(OUT, 256, 2).transpose(0, 2, 1, 3).reshape(D, D)
    g_in = columns(IN, 512, 3).reshape(2, 3, D, 8, HD).transpose(2, 0, 3, 1, 4).reshape(D, 3 * D)

    def owned(a, axis):
        return lax.psum(lax.psum_scatter(a, "tensor", scatter_dimension=axis, tiled=True), "dp")

    g_in, g_out, g_up, g_down = owned(g_in, 1), owned(g_out, 0), owned(g_up, 1), owned(g_down, 0)
    g_kernel, g_bias, g_vectors = owned(gs[0:9], 1), owned(gs[16:20].reshape(-1), 0), owned(gs[9:16], 1)
    vector_width = m_vectors.shape[1]
    own_vectors = lax.dynamic_slice_in_dim(vectors, place * vector_width, vector_width, 1)
    results = [out, grad_in]
    for w, m, v, g, rate in (
        (w_in, m_in, v_in, g_in, D**-0.5),
        (w_out, m_out, v_out, g_out, (D // HD) ** -0.5),
        (w_up, m_up, v_up, g_up, D**-0.5),
        (w_down, m_down, v_down, g_down, FF**-0.5),
    ):
        new = adam(w, m, v, g, rate, 0.05)
        results += [*new, new[0].astype(bf16)]
    results += adam(kernel, m_kernel, v_kernel, g_kernel, 2.0, 0.05)
    results += adam(up_bias, m_bias, v_bias, g_bias, 0.3, 0.0)
    results += adam(own_vectors, m_vectors, v_vectors, g_vectors, 0.3, 0.0)
    return tuple(results)


def solution(mesh):
    rows, columns = P("tensor", None), P(None, "tensor")
    tokens = P(("dp", "tensor"), None)
    mats = (columns,) * 3 + (rows,) * 3 + (columns,) * 3 + (rows,) * 3
    news = (columns,) * 4 + (rows,) * 4 + (columns,) * 4 + (rows,) * 4
    pairs = mesh.shape["dp"] == 16 and mesh.shape["tensor"] == 2
    return jax.shard_map(
        local if pairs else general,
        mesh=mesh,
        in_specs=(tokens, tokens, P(), *mats)
        + (columns,) * 3
        + (P("tensor"),) * 3
        + (P(), columns, columns),
        out_specs=(tokens, tokens, *news) + (columns,) * 3 + (P("tensor"),) * 3 + (columns,) * 3,
        check_vma=False,
    )
```

```python
import functools
import jax
import jax.numpy as jnp
from jax import lax
from jax.experimental import pallas as pl
from jax.experimental.pallas import tpu as pltpu
from jax.sharding import PartitionSpec as P

D = 512
HD = 32
FF = 2048
SIDE = 14
WIDE = 16
WIN = SIDE * SIDE
ROWS = SIDE * WIDE
KEYS = 256
GROUPS = D // 128
STEP = 5
DOWN, UP, OUT, IN, GROWS = 0, 2048, 4096, 4608, 6144
MESH = pl.DeviceIdType.MESH
eps = 1e-05
f32 = jnp.float32
bf16 = jnp.bfloat16
C0 = 0.7978845608028654
C1 = 0.044715


def nn(a, b):
    return lax.dot_general(a, b, (((1,), (0,)), ((), ())), preferred_element_type=f32)


def nt(a, b):
    return lax.dot_general(a, b, (((1,), (1,)), ((), ())), preferred_element_type=f32)


def tn(a, b):
    return lax.dot_general(a, b, (((0,), (0,)), ((), ())), preferred_element_type=f32)


def normed(x):
    c = x - jnp.mean(x, axis=-1, keepdims=True)
    r = lax.rsqrt(jnp.mean(c * c, axis=-1, keepdims=True) + eps)
    return c * r, r


def norm_back(u, xhat, r):
    return r * (
        u
        - jnp.mean(u, axis=-1, keepdims=True)
        - xhat * jnp.mean(u * xhat, axis=-1, keepdims=True)
    )


def gelu_pair(x):
    x2 = x * x
    t = 0.5 * jnp.tanh(x * (C0 + (C0 * C1) * x2))
    h = 0.5 + t
    value = x * h
    return value, h + value * ((0.5 - t) * (2.0 * C0 + (6.0 * C0 * C1) * x2))


def gelu(x):
    return x * (0.5 + 0.5 * jnp.tanh(x * (C0 + (C0 * C1) * (x * x))))


def row_sum(x):
    return jnp.sum(x, axis=0, keepdims=True)


def shift_rows(x, by):
    z = jnp.zeros((abs(by), x.shape[1]), x.dtype)
    if by > 0:
        return jnp.concatenate([z, x[:-by]], axis=0)
    return jnp.concatenate([x[-by:], z], axis=0)


def roll1(x, by):
    return pltpu.roll(x, by % x.shape[0], 0)


def pool(c):
    s = c + roll1(c, 1) + roll1(c, -1)
    return s + shift_rows(s, WIDE) + shift_rows(s, -WIDE)


def block_body(images, limit, first_half, hooks, wi, wo, wu, wd, small, vecs,
               gin, grads, gsmall,
               x_s, co_s, at_s, af_s, da_s, gp_s, mf_s, na_s, nb_s, lb_s, la_s, mx_s,
               q_s, k_s, v_s, dm_s, hd_s, dp_s, pj_s, p_s, taps_s, ds_s):
    gain_a, shift_a, gain_b, shift_b, scale_a, scale_f, bias_f = (
        vecs[i : i + 1, :] for i in range(7)
    )
    gsmall[...] = jnp.zeros_like(gsmall)
    gtaps = taps_s
    gtaps[...] = jnp.zeros_like(gtaps)
    blank = jnp.zeros((KEYS - ROWS, 256), bf16)
    for ref in (q_s, k_s, v_s, dm_s):
        for t in range(2):
            for n in range(images):
                ref[t, n * KEYS + ROWS : (n + 1) * KEYS, :] = blank

    cell = lax.broadcasted_iota(jnp.int32, (ROWS, 1), 0)
    inside = lax.rem(cell, WIDE) < SIDE
    lane = lax.broadcasted_iota(jnp.int32, (1, 128), 1)
    head_masks = [(lane // HD) == h for h in range(4)]
    key_row = lax.broadcasted_iota(jnp.int32, (KEYS, 128), 0)
    key_lane = lax.broadcasted_iota(jnp.int32, (KEYS, 128), 1)
    key_pad = (lax.rem(key_row, WIDE) >= SIDE) | (key_row >= ROWS)
    key_block = jnp.where(key_pad & (key_lane == 0), -1e30, 0.0).astype(bf16)
    one_block = jnp.where(key_lane == 0, 1.0, 0.0).astype(bf16)

    def padded(n):
        return pl.ds(pl.multiple_of(n * ROWS, WIDE), ROWS)

    def held(n):
        return pl.ds(pl.multiple_of(n * KEYS, WIDE), ROWS)

    def whole(n):
        return pl.ds(pl.multiple_of(n * KEYS, WIDE), KEYS)

    def masked(h, a):
        return jnp.where(head_masks[h], a, jnp.zeros_like(a))

    def prepare(n, carry):
        rows = padded(n)
        xhat, _ = normed(x_s[rows, :].astype(f32))
        na_s[rows, :] = (xhat * gain_a + shift_a).astype(bf16)
        return carry

    def tap(t, i, ls):
        return small[t, pl.ds(i, 1), ls]

    def attend(t, n):
        rows = padded(n)
        na = na_s[rows, :]
        k_s[t, held(n), :] = nn(na, wi[t, 1]).astype(bf16)
        v_s[t, held(n), :] = nn(na, wi[t, 2]).astype(bf16)
        for g in range(2):
            ls = slice(g * 128, (g + 1) * 128)
            gp = nn(na, wi[t, 0, :, ls])
            gp_s[t, rows, ls] = gp
            field = jnp.where(inside, gelu(gp), 0.0)
            back, ahead = roll1(field, 1), roll1(field, -1)
            conv = None
            for a in range(3):
                part = (
                    tap(t, 3 * a, ls) * back
                    + tap(t, 3 * a + 1, ls) * field
                    + tap(t, 3 * a + 2, ls) * ahead
                )
                if a != 1:
                    part = shift_rows(part, WIDE * (1 - a))
                conv = part if conv is None else conv + part
            pooled = pool(jnp.where(inside, conv, 0.0)) * (HD ** (-0.5) / 9.0)
            q_s[t, held(n), ls] = pooled.astype(bf16)
        for g in range(2):
            ls = slice(g * 128, (g + 1) * 128)
            qa = jnp.concatenate([q_s[t, whole(n), ls], one_block], axis=1)
            kg = k_s[t, whole(n), ls]
            vt = jnp.transpose(v_s[t, whole(n), ls])
            mixed = []
            keys = jnp.concatenate(
                [jnp.concatenate([masked(h, kg), key_block], axis=1) for h in range(4)], axis=0
            )
            scores = nt(keys, qa)
            for h in range(4):
                hs = slice(h * KEYS, (h + 1) * KEYS)
                s = scores[hs]
                e = jnp.exp(s - jnp.max(s, axis=0, keepdims=True))
                p_s[t, n * 2 + g, :, hs] = (e * (1.0 / jnp.sum(e, axis=0, keepdims=True))).astype(bf16)
            for h in range(4):
                p = p_s[t, n * 2 + g, :, h * KEYS : (h + 1) * KEYS]
                mixed.append(nn(vt[h * HD : (h + 1) * HD], p))
            mix = jnp.transpose(jnp.concatenate(mixed, axis=0))[:ROWS]
            mf_s[t, rows, ls] = mix
            mx_s[t, rows, ls] = mix.astype(bf16)

    def finish(n, carry):
        rows = padded(n)
        attn = nn(mx_s[0, rows, :], wo[0]) + nn(mx_s[1, rows, :], wo[1])
        at_s[rows, :] = attn
        after = x_s[rows, :].astype(f32) + scale_a * attn
        af_s[rows, :] = after
        xhat, _ = normed(after)
        nb_s[rows, :] = (xhat * gain_b + shift_b).astype(bf16)
        lb_s[rows, :] = (scale_f * co_s[rows, :].astype(f32)).astype(bf16)
        return carry

    def feed(t, u, n):
        rows = padded(n)
        us = slice(u * 512, (u + 1) * 512)
        cs = pl.ds(pl.multiple_of(t * 1024 + u * 512, 512), 512)
        unit_bias = jnp.concatenate(
            [small[t, 9 + 2 * u + j : 10 + 2 * u + j, :] for j in range(2)], axis=1
        )
        value, slope = gelu_pair(nn(nb_s[rows, :], wu[t, :, us]) + unit_bias)
        hd_s[rows, cs] = value.astype(bf16)
        d_pre = slope * nt(lb_s[rows, :], wd[t, us, :])
        gsmall[pl.ds(16 + 2 * t + u, 1), :] += row_sum(d_pre)
        dp_s[rows, cs] = d_pre.astype(bf16)

    def digest(n, carry):
        rows = padded(n)
        branch = nn(hd_s[rows, 0:1024], wd[0]) + nn(hd_s[rows, 1024:2048], wd[1])
        d_nb = nt(dp_s[rows, 0:1024], wu[0]) + nt(dp_s[rows, 1024:2048], wu[1])
        co = co_s[rows, :].astype(f32)
        after = af_s[rows, :]
        xhat, r = normed(after)
        moved = branch + bias_f
        live = (n < limit).astype(f32)
        af_s[rows, :] = (after + scale_f * moved) * live
        gsmall[14:15, :] += row_sum(co * moved)
        gsmall[15:16, :] += scale_f * row_sum(co)
        gsmall[11:12, :] += row_sum(d_nb * xhat)
        gsmall[12:13, :] += row_sum(d_nb)
        d_after = co + norm_back(gain_b * d_nb, xhat, r)
        da_s[rows, :] = d_after
        gsmall[13:14, :] += row_sum(d_after * at_s[rows, :])
        la = (scale_a * d_after).astype(bf16)
        la_s[rows, :] = la
        for t in range(2):
            dm_s[t, held(n), :] = nt(la, wo[t]).astype(bf16)
        hooks.turn("d", n, images)
        return carry

    pick_row = lax.broadcasted_iota(jnp.int32, (256, 128), 0)
    pick_lane = lax.broadcasted_iota(jnp.int32, (256, 128), 1)
    pick = jnp.where(
        (lax.rem(pick_row, 128) // HD == lax.rem(pick_lane, 4)) & (pick_lane < 8), 1.0, 0.0
    ).astype(bf16)

    def split(a):
        high = a.astype(bf16)
        return high, (a - high.astype(f32)).astype(bf16)

    def inner_block(a):
        sums = nn(jnp.concatenate(split(a), axis=1), pick)
        high, low = split(sums)
        return jnp.where(lane < 4, high, low)

    blank_rows = jnp.zeros((KEYS - ROWS, 128), bf16)

    minus = [
        jnp.where((lane == h) | (lane == h + 4), -1.0, 0.0).astype(bf16) for h in range(4)
    ]

    def recede(t, n, turn):
        rows = padded(n)
        for g in range(2):
            ls = slice(g * 128, (g + 1) * 128)
            inner = inner_block(dm_s[t, held(n), ls].astype(f32) * mf_s[t, rows, ls])
            dmg = dm_s[t, whole(n), ls]
            left = jnp.concatenate(
                [dmg, jnp.concatenate([inner, blank_rows], axis=0)], axis=1
            )
            qg = q_s[t, whole(n), ls]
            kg = k_s[t, whole(n), ls]
            vg = v_s[t, whole(n), ls]
            kt = jnp.transpose(kg)
            dqs = []
            right = jnp.concatenate(
                [
                    jnp.concatenate([masked(h, vg), jnp.broadcast_to(minus[h], (KEYS, 128))], axis=1)
                    for h in range(4)
                ],
                axis=0,
            )
            d_probs = nt(right, left)
            for h in range(4):
                hs = slice(h * KEYS, (h + 1) * KEYS)
                e = p_s[t, n * 2 + g, :, hs]
                ds_s[:, hs] = (e.astype(f32) * d_probs[hs]).astype(bf16)
            dv = nn(
                p_s[t, n * 2 + g], jnp.concatenate([masked(h, dmg) for h in range(4)], axis=0)
            )
            dk = nn(ds_s[...], jnp.concatenate([masked(h, qg) for h in range(4)], axis=0))
            for h in range(4):
                dqs.append(nn(kt[h * HD : (h + 1) * HD], ds_s[:, h * KEYS : (h + 1) * KEYS]))
            dq = jnp.transpose(jnp.concatenate(dqs, axis=0))[:ROWS]
            pj_s[t, 1, rows, ls] = dk[:ROWS].astype(bf16)
            pj_s[t, 2, rows, ls] = dv[:ROWS].astype(bf16)
            value, slope = gelu_pair(gp_s[t, rows, ls])
            field = jnp.where(inside, value, 0.0)
            d_conv = jnp.where(inside, pool(dq * (HD ** (-0.5) / 9.0)), 0.0)
            shifted = (roll1(field, 1), field, roll1(field, -1))
            d_cols = [None, None, None]
            for a in range(3):
                moved = d_conv if a == 1 else shift_rows(d_conv, WIDE * (a - 1))
                for b in range(3):
                    i = 3 * a + b
                    gtaps[t, i : i + 1, ls] += row_sum(moved * shifted[b])
                    term = tap(t, i, ls) * moved
                    d_cols[b] = term if d_cols[b] is None else d_cols[b] + term
            d_field = roll1(d_cols[0], -1) + d_cols[1] + roll1(d_cols[2], 1)
            pj_s[t, 0, rows, ls] = jnp.where(inside, slope * d_field, 0.0).astype(bf16)
            hooks.turn("r", turn + g, 4 * images)

    def rise(n, carry):
        rows = padded(n)
        d_na = None
        for t in range(2):
            for part in range(3):
                term = nt(pj_s[t, part, rows, :], wi[t, part])
                d_na = term if d_na is None else d_na + term
        xhat, r = normed(x_s[rows, :].astype(f32))
        gsmall[9:10, :] += row_sum(d_na * xhat)
        gsmall[10:11, :] += row_sum(d_na)
        da_s[rows, :] += norm_back(gain_a * d_na, xhat, r)
        hooks.turn("s", n, images)
        return carry

    def narrow_rows(target, source):
        for i in range(images * SIDE):
            target[i * SIDE : (i + 1) * SIDE, :] = source[i * WIDE : i * WIDE + SIDE, :]

    def store_down(u):
        for t in range(2):
            cs = slice((2 * t + u) * 512, (2 * t + u + 1) * 512)
            down = tn(hd_s[:, cs], lb_s[...]).astype(bf16)
            for j in range(2):
                first = DOWN + (2 * u + j) * 512
                grads[t, first : first + 512, :] = down[:, j * 256 : (j + 1) * 256]

    def store_up(u):
        for t in range(2):
            cs = slice((2 * t + u) * 512, (2 * t + u + 1) * 512)
            up = tn(nb_s[...], dp_s[:, cs]).astype(bf16)
            for j in range(2):
                first = UP + (2 * u + j) * 512
                grads[t, first : first + 512, :] = up[:, j * 256 : (j + 1) * 256]

    def store_out():
        for t in range(2):
            g_out = tn(mx_s[t], la_s[...]).astype(bf16)
            for j in range(2):
                first = OUT + j * 256
                grads[t, first : first + 256, :] = g_out[:, j * 256 : (j + 1) * 256]

    def store_in(t, part):
        first = IN + part * 512
        grads[t, first : first + 512, :] = tn(na_s[...], pj_s[t, part]).astype(bf16)

    def widen(source, spares, target, scaled):
        temp = at_s
        temp[0 : images * WIN, :] = source[0 : images * WIN, :].astype(f32)
        for first, width, spare in spares:
            cs = slice(first, first + width)
            pad = jnp.zeros((WIDE - SIDE, width), f32)
            for n in range(images):
                for i in range(n * SIDE, (n + 1) * SIDE):
                    cells = temp[i * SIDE : (i + 1) * SIDE, cs]
                    if scaled:
                        cells = cells * (n < limit).astype(f32)
                    spare[i * WIDE : i * WIDE + SIDE, :] = cells
                    spare[i * WIDE + SIDE : (i + 1) * WIDE, :] = pad
            target[:, cs] = spare[...].astype(bf16)

    loop = lax.fori_loop
    hooks.tokens()
    widen(nb_s, [(t * 256, 256, gp_s.at[t]) for t in range(2)], x_s, False)
    loop(0, images, prepare, 0)
    hooks.weights()
    other_half = 1 - first_half

    def fore(i, carry):
        later = i // images
        attend(first_half + (other_half - first_half) * later, lax.rem(i, images))
        hooks.fore(i)
        return carry

    loop(0, 2 * images, fore, 0)
    hooks.cotangent()
    widen(lb_s, [(0, D, da_s)], co_s, True)
    loop(0, images, finish, 0)
    hooks.near()

    def feed_own(n, carry):
        for u in range(2):
            feed(first_half, u, n)
        return carry

    def feed_first(n, carry):
        feed(other_half, 0, n)
        return carry

    def feed_second(n, carry):
        feed(other_half, 1, n)
        hooks.turn("f", n, images)
        return carry

    loop(0, images, feed_own, 0)
    hooks.arrived()
    loop(0, images, feed_first, 0)
    store_down(0)
    hooks.point("D0")
    store_up(0)
    hooks.point("U0")
    loop(0, images, feed_second, 0)
    store_down(1)
    hooks.point("D1")
    store_up(1)
    hooks.point("U1")
    loop(0, images, digest, 0)
    store_out()
    hooks.point("O")

    def aft(n, carry):
        recede(other_half, n, 2 * n)
        return carry

    loop(0, images, aft, 0)
    for part in (2, 1, 0):
        store_in(other_half, part)
        hooks.point("A%d" % part)

    def aft2(n, carry):
        recede(first_half, n, 2 * (images + n))
        return carry

    loop(0, images, aft2, 0)
    for part in (2, 1, 0):
        store_in(first_half, part)
        hooks.point("B%d" % part)
    loop(0, images, rise, 0)
    for t in range(2):
        gsmall[0:9, t * 256 : (t + 1) * 256] = gtaps[t, 0:9, :]
    hooks.sums(0)
    narrow_rows(gin, af_s)
    hooks.output()
    hooks.sums(1)
    hooks.point("N")
    narrow_rows(gin, da_s)
    hooks.finished()
    hooks.point("R")


class Quiet:
    def __init__(self, tok, cot, nb_s, lb_s, out, gin):
        self.refs = tok, cot, nb_s, lb_s, out, gin

    def tokens(self):
        tok, cot, nb_s, lb_s, _, _ = self.refs
        rows = tok.shape[0]
        nb_s[0:rows, :] = tok[...]
        lb_s[0:rows, :] = cot[...]

    def output(self):
        _, _, _, _, out, gin = self.refs
        out[...] = gin[...].astype(bf16)

    def point(self, name):
        pass

    def turn(self, name, i, count):
        pass

    sums = fore = point

    def weights(self):
        pass

    cotangent = near = arrived = finished = weights


def block_kernel(images, lim, tok, cot, wi, wo, wu, wd, small, vecs, out, gin, grads, gsmall, *scratch):
    quiet = Quiet(tok, cot, scratch[8], scratch[9], out, gin)
    block_body(images, lim[0], 0, quiet, wi, wo, wu, wd, small, vecs, gin, grads, gsmall, *scratch)


def block_scratch(images):
    R = images * ROWS
    K = images * KEYS
    V = pltpu.VMEM
    return (
        [V((R, D), bf16)] * 2
        + [V((R, D), f32)] * 3
        + [V((2, R, 256), f32)] * 2
        + [V((R, D), bf16)] * 4
        + [V((2, R, 256), bf16)]
        + [V((2, K, 256), bf16)] * 4
        + [V((R, FF), bf16)] * 2
        + [
            V((2, 3, R, 256), bf16),
            V((2, images * 2, KEYS, 4 * KEYS), bf16),
            V((2, 16, 256), f32),
            V((KEYS, 4 * KEYS), bf16),
        ]
    )


def block(lim, tok, cot, wi, wo, wu, wd, small, vecs):
    images = tok.shape[0] // WIN
    S = jax.ShapeDtypeStruct
    V = pltpu.VMEM
    return pl.pallas_call(
        functools.partial(block_kernel, images),
        out_shape=(
            S(tok.shape, bf16),
            S(tok.shape, f32),
            S((2, GROWS, 256), bf16),
            S((24, D), f32),
        ),
        in_specs=[pl.BlockSpec(memory_space=pltpu.SMEM)] + [pl.BlockSpec(memory_space=V)] * 8,
        out_specs=[pl.BlockSpec(memory_space=V)] * 4,
        scratch_shapes=block_scratch(images),
        compiler_params=pltpu.CompilerParams(vmem_limit_bytes=62 * 1024 * 1024),
    )(lim, tok, cot, wi, wo, wu, wd, small, vecs)


def tile_loop(rows, size, body):
    if rows <= size:
        body(0, rows)
        return

    def step(i, carry):
        body(pl.multiple_of(i * size, size), size)
        return carry

    lax.fori_loop(0, rows // size, step, 0)


def aligned(first, size):
    return pl.ds(pl.multiple_of(first, 16), size)


def spread_four(part):
    a = lax.broadcasted_iota(jnp.int32, (384, 128), 1)
    b = lax.broadcasted_iota(jnp.int32, (384, 128), 0)
    return jnp.where(b == (a // HD) * (3 * HD) + part * HD + lax.rem(a, HD), 1.0, 0.0).astype(bf16)


def spread(part):
    a = lax.broadcasted_iota(jnp.int32, (256, 768), 0)
    b = lax.broadcasted_iota(jnp.int32, (256, 768), 1)
    return jnp.where(b == (a // HD) * (3 * HD) + part * HD + lax.rem(a, HD), 1.0, 0.0).astype(bf16)


def adam(w, m, v, g, rate, decay):
    half = 0.5 * g
    m = 0.5 * m + half
    v = 0.5 * v + half * g
    scale = 1.0 / (1.0 - 0.5**STEP)
    w = w - ((rate * scale) * m / (jnp.sqrt(v * scale) + 1e-08) + (rate * decay) * w)
    return w, m, v


def adam_tile(w, m, v, g, rate, decay):
    half = 0.5 * g
    m = 0.5 * m + half
    v = 0.5 * v + half * g
    scale = 1.0 / (1.0 - 0.5**STEP)
    seen = v * scale
    below = seen * lax.rsqrt(seen) + 1e-08
    inverse = pl.reciprocal(below, approx=True)
    inverse = inverse * (2.0 - below * inverse)
    w = w - ((rate * scale) * m * inverse + (rate * decay) * w)
    return w, m, v


MATRICES = (
    (1024, 512, FF**-0.5, 4, 64),
    (512, 1024, D**-0.5, 4, 32),
    (256, 512, (D // HD) ** -0.5, 1, 64),
    (512, 768, D**-0.5, 4, 64),
)


def adam_kernel(*refs):
    full, small_sum, raw_out, raw_gin = refs[:4]
    mats = refs[4:16]
    smalls = refs[16:25]
    outs = refs[25:41]
    small_outs = refs[41:50]
    out, gin = refs[50:52]
    bufs = refs[52:64]
    lows = refs[64:68]
    g_vm, out_vm, gin_vm, in_sem, out_sem, more_sem = refs[68:]
    g_load = pltpu.make_async_copy(full, g_vm, more_sem.at[2])
    g_load.start()
    loads = {}
    for i, (rows, cols, rate, pieces, tile) in enumerate(MATRICES):
        size = rows // pieces
        for p in range(pieces):
            rs = pl.ds(p * size, size)
            for j in range(3):
                go = pltpu.make_async_copy(
                    mats[3 * i + j].at[rs, :], bufs[3 * i + j].at[rs, :], in_sem.at[i, p, j]
                )
                go.start()
                loads[i, p, j] = go
    passing = [
        pltpu.make_async_copy(raw_out, out_vm, more_sem.at[0]),
        pltpu.make_async_copy(raw_gin, gin_vm, more_sem.at[1]),
    ]
    moves = [
        pltpu.make_async_copy(out_vm, out, more_sem.at[3]),
        pltpu.make_async_copy(gin_vm, gin, more_sem.at[4]),
    ]
    for go in passing:
        go.start()
    stores = []
    g_load.wait()
    for i, (rows, cols, rate, pieces, tile) in enumerate(MATRICES):
        size = rows // pieces
        bw, bm, bv = bufs[3 * i : 3 * i + 3]
        low = lows[i]
        spreads = [spread(part) for part in range(3)] if i == 3 else None
        for p in range(pieces):
            for j in range(3):
                loads[i, p, j].wait()

            def body(first, tile, i=i, p=p, bw=bw, bm=bm, bv=bv, low=low, rate=rate, size=size, spreads=spreads):
                rs = pl.ds(p * size + first, tile)
                if i == 0:
                    g = [
                        g_vm[pl.ds(DOWN + (p // 2 * 2 + j) * 512 + p % 2 * size + first, tile), :]
                        for j in range(2)
                    ]
                elif i == 1:
                    g = [g_vm[pl.ds(UP + j * 512 + p * size + first, tile), :] for j in range(4)]
                elif i == 2:
                    g = [g_vm[pl.ds(OUT + j * 256 + p * size + first, tile), :] for j in range(2)]
                else:
                    g = None
                    for part in range(3):
                        own = g_vm[pl.ds(IN + part * 512 + p * size + first, tile), :]
                        term = nn(own, spreads[part])
                        g = term if g is None else g + term
                if i < 3:
                    g = jnp.concatenate(g, axis=1).astype(f32)
                w, m, v = adam_tile(bw[rs, :], bm[rs, :], bv[rs, :], g, rate, 0.05)
                bw[rs, :] = w
                bm[rs, :] = m
                bv[rs, :] = v
                low[rs, :] = w.astype(bf16)

            tile_loop(size, tile, body)
            rs = pl.ds(p * size, size)
            for j, src in enumerate((bw, bm, bv, low)):
                go = pltpu.make_async_copy(
                    src.at[rs, :], outs[4 * i + j].at[rs, :], out_sem.at[i, p, j]
                )
                go.start()
                stores.append(go)
        if i == 0:
            for come, go in zip(passing, moves):
                come.wait()
                go.start()
    x = lax.axis_index("tensor")
    mine = pl.ds(pl.multiple_of(x * 256, 256), 256)
    g_small = small_sum[:, mine]
    both = small_sum[16:20, :]
    first = jnp.where(x == 0, 1.0, 0.0)
    g_bias = jnp.concatenate(
        [
            (both[j : j + 1, :] * first + both[2 + j : 3 + j, :] * (1.0 - first))
            for j in range(2)
        ],
        axis=1,
    )
    for i, (g, rate, decay) in enumerate(
        ((g_small[0:9], 2.0, 0.05), (g_bias, 0.3, 0.0), (g_small[9:16], 0.3, 0.0))
    ):
        w = smalls[3 * i][...] if i < 2 else smalls[6][:, mine]
        new = adam(w, smalls[3 * i + 1][...], smalls[3 * i + 2][...], g, rate, decay)
        for j in range(3):
            small_outs[3 * i + j][...] = new[j]
    for go in stores + moves:
        go.wait()


def adam_step(full, small_sum, raw_out, raw_gin, mats, smalls):
    S = jax.ShapeDtypeStruct
    V = pltpu.VMEM
    mat_shapes = [shape[:2] for shape in MATRICES]
    any_spec = pl.BlockSpec(memory_space=pl.ANY)
    vmem_spec = pl.BlockSpec(memory_space=V)
    small_shapes = [(9, 256)] * 3 + [(1, 1024)] * 3 + [(7, 256)] * 3
    return pl.pallas_call(
        adam_kernel,
        out_shape=tuple(
            S(shape, kind) for shape in mat_shapes for kind in (f32, f32, f32, bf16)
        )
        + tuple(S(shape, f32) for shape in small_shapes)
        + (S(raw_out.shape, bf16), S(raw_gin.shape, f32)),
        in_specs=[any_spec, vmem_spec, any_spec, any_spec] + [any_spec] * 12 + [vmem_spec] * 9,
        out_specs=[any_spec] * 16 + [vmem_spec] * 9 + [any_spec] * 2,
        scratch_shapes=[V(shape, f32) for shape in mat_shapes for _ in range(3)]
        + [V(shape, bf16) for shape in mat_shapes]
        + [
            V((GROWS, 256), bf16),
            V(raw_out.shape, bf16),
            V(raw_gin.shape, f32),
            pltpu.SemaphoreType.DMA((4, 4, 3)),
            pltpu.SemaphoreType.DMA((4, 4, 4)),
            pltpu.SemaphoreType.DMA((5,)),
        ],
        compiler_params=pltpu.CompilerParams(vmem_limit_bytes=62 * 1024 * 1024),
    )(full, small_sum, raw_out, raw_gin, *mats, *smalls)


CHUNKS = (
    (0, 1024),
    (2048, 1024),
    (1024, 1024),
    (3072, 1024),
    (4096, 512),
    (5632, 512),
    (5120, 512),
    (4608, 512),
)
LATE = 5
SLOTS = 12
PLAN = {
    'U0': ((0, 0),),
    'f0': ((1, 0),),
    'f3': ((0, 1),),
    'D1': ((1, 1),),
    'U1': ((2, 0),),
    'd0': ((3, 0),),
    'd1': ((2, 1), (3, 1),),
    'd2': ((0, 2),),
    'r0': ((4, 0),),
    'r1': ((1, 2), (0, 3), (4, 1),),
    'r5': ((1, 3),),
    'r6': ((2, 2), (0, 4),),
    'A1': ((5, 0),),
    'A0': ((6, 0),),
    'r8': ((7, 0), (5, 1), (6, 1), (3, 2), (2, 3), (1, 4), (7, 1),),
    'r9': ((0, 5), (4, 2),),
    'r12': ((3, 3), (2, 4),),
    'r14': ((0, 6),),
    'r15': ((4, 3), (1, 5), (0, 7),),
    'B1': ((5, 2), (3, 4), (6, 2),),
    's0': ((7, 2), (5, 3), (6, 3),),
    's1': ((2, 5), (7, 3), (1, 6),),
    's2': ((4, 4),),
    's3': ((5, 4), (1, 7),),
    'N': ((6, 4), (3, 5),),
}
TAIL = (
    (4, 5), (2, 6), (5, 5), (2, 7), (7, 4), (6, 5),
    (3, 6), (5, 6), (3, 7), (4, 6), (7, 5), (4, 7),
    (6, 6), (5, 7), (5, 8), (7, 6), (6, 7), (6, 8),
    (7, 7), (7, 8),
)


ITEMS = ((0, 0, 64), (0, 64, 64), (1, 0, 64), (2, 0, 64), (2, 64, 64), (3, 0, 128), (3, 128, 128))


class Traffic:
    def __init__(self, images, refs):
        (self.tok, self.cot, self.w_in, self.w_out, self.w_up, self.w_down, self.taps, self.bias,
         self.out, self.gin, self.full, self.small_sum,
         self.gin_v, self.grads, self.gsmall, self.wi, self.wo, self.wu, self.wd, self.small,
         self.at_s, self.af_s, self.da_s, self.gp_s, self.mf_s, self.nb_s, self.lb_s, self.out_v,
         self.cores, self.xs, self.ys, self.zs, self.firsts,
         self.small_in, self.small_z, self.send, self.recv, self.ssend, self.srecv,
         self.wsend, self.wrecv, self.load, self.save) = refs
        self.images = images
        dp, x = lax.axis_index("dp"), lax.axis_index("tensor")
        core, y, z = lax.rem(dp, 2), lax.rem(dp // 2, 2), dp // 4

        def at(zz, yy, cc, xx):
            return ((zz * 2 + yy) * 2 + cc, xx)

        self.x, self.core, self.y, self.z = x, core, y, z
        self.core_mate = at(z, y, 1 - core, x)
        self.x_mate = at(z, y, core, 1 - x)
        self.y_mate = at(z, 1 - y, core, x)
        self.z_others = [lax.rem(z + k, 4) for k in range(1, 4)]
        self.z_mates = [at(o, y, core, x) for o in self.z_others]
        quarter = y * 2 + core
        self.quarter = quarter

        def load(i, src, dst):
            return pltpu.make_async_copy(src, dst, self.load.at[i])

        w_in, w_out, w_up, w_down = self.w_in, self.w_out, self.w_up, self.w_down
        at_s, af_s, da_s, mf_s, gin = self.at_s, self.af_s, self.da_s, self.mf_s, self.gin_v
        q_in, q_out = aligned(quarter * 128, 128), aligned(quarter * 64, 64)
        q_down = aligned(quarter * 256, 256)
        self.early = [
            load(0, w_in.at[q_in, 0:256], at_s.at[0:128, 0:256]),
            load(1, w_in.at[q_in, 256:512], at_s.at[0:128, 256:512]),
            load(2, w_in.at[q_in, 512:768], at_s.at[128:256, 0:256]),
            load(3, w_out.at[q_out, :], at_s.at[256:320, :]),
            load(4, w_up.at[q_in, 0:512], at_s.at[320:448, :]),
            load(5, w_up.at[q_in, 512:1024], at_s.at[448:576, :]),
            load(6, w_down.at[q_down, :], at_s.at[576:832, :]),
        ]
        self.own_in = [
            load(7, w_in.at[:, 0:256], mf_s.at[0, 0:512, :]),
            load(8, w_in.at[:, 256:512], mf_s.at[1, 0:512, :]),
            load(9, w_in.at[:, 512:768], gin.at[0:512, 0:256]),
        ]
        self.tok_load = load(10, self.tok, self.nb_s.at[0 : images * WIN, :])
        self.cot_load = load(11, self.cot, self.lb_s.at[0 : images * WIN, :])
        self.own_rest = [
            load(12, w_out.at[:, 0:256], gin.at[0:256, 256:512]),
            load(13, w_out.at[:, 256:512], gin.at[256:512, 256:512]),
            load(14, w_up.at[:, 0:512], da_s.at[0:512, :]),
            load(15, w_up.at[:, 512:1024], af_s.at[0:512, :]),
            load(16, w_down.at[0:256, :], da_s.at[512:768, :]),
            load(17, w_down.at[256:512, :], af_s.at[512:768, :]),
            load(18, w_down.at[512:768, :], gin.at[512:768, :]),
            load(19, w_down.at[768:896, :], da_s.at[768:896, :]),
            load(20, w_down.at[896:1024, :], af_s.at[768:896, :]),
        ]


    def weight_copy(self, src, dst, item, slot, mate):
        return pltpu.make_async_remote_copy(
            src_ref=src,
            dst_ref=dst,
            send_sem=self.wsend.at[item, slot],
            recv_sem=self.wrecv.at[item, slot],
            device_id=mate,
            device_id_type=MESH,
        )

    def view(self, item, half, yy, cc):
        kind, first, size = ITEMS[item]
        quarter = yy * 2 + cc
        if kind == 0:
            return self.wi.at[half, :, aligned(quarter * 128 + first, size), :]
        ref, rows = ((self.wo, 64), (self.wu, 128), (self.wd, 256))[kind - 1]
        return ref.at[half, aligned(quarter * rows + first, size), :]

    def crossing(self, item):
        if item == len(ITEMS):
            own = self.small.at[self.x]
        else:
            own = self.view(item, self.x, self.y, self.core)
        return self.weight_copy(own, own, item, 0, self.x_mate)

    def inward(self, item):
        got = self.view(item, 1 - self.x, self.y, self.core)
        return self.weight_copy(got, got, item, 1, self.core_mate)

    def aside(self, item):
        got = self.view(item, 1 - self.x, self.y, self.core)
        return self.weight_copy(got, got, item, 2, self.y_mate)

    def onward(self, item):
        got = self.view(item, 1 - self.x, 1 - self.y, self.core)
        return self.weight_copy(got, got, item, 3, self.core_mate)

    def permuted(self, pieces, rows):
        low = jnp.concatenate(pieces, axis=1).astype(bf16)
        for part in range(3):
            for j in range(2):
                four = nn(low[:, j * 384 : (j + 1) * 384], spread_four(part))
                self.wi[self.x, part, rows, j * 128 : (j + 1) * 128] = four.astype(bf16)

    def begin(self):
        for go in self.early[0:3]:
            go.start()
        barrier = pltpu.get_barrier_semaphore()
        for mate in (self.core_mate, self.x_mate, self.y_mate, *self.z_mates):
            pl.semaphore_signal(barrier, inc=1, device_id=mate, device_id_type=MESH)
        for go in self.early[3:]:
            go.start()
        self.tok_load.start()
        for go in self.own_in:
            go.start()
        x, quarter, at_s = self.x, self.quarter, self.at_s
        self.small[x, 0:9, :] = self.taps[...]
        for j in range(4):
            self.small[x, 9 + j : 10 + j, :] = self.bias[:, j * 256 : (j + 1) * 256]
        for go in self.early[0:3]:
            go.wait()
        self.permuted(
            [at_s[0:128, 0:256], at_s[0:128, 256:512], at_s[128:256, 0:256]],
            aligned(quarter * 128, 128),
        )
        pl.semaphore_wait(barrier, 6)
        self.crossing(0).start()
        self.crossing(1).start()
        self.crossing(len(ITEMS)).start()
        self.early[3].wait()
        self.wo[x, aligned(quarter * 64, 64), :] = at_s[256:320, :].astype(bf16)
        self.crossing(2).start()
        for go in self.early[4:6]:
            go.wait()
        rows = aligned(quarter * 128, 128)
        self.wu[x, rows, 0:512] = at_s[320:448, :].astype(bf16)
        self.wu[x, rows, 512:1024] = at_s[448:576, :].astype(bf16)
        self.crossing(3).start()
        self.crossing(4).start()
        self.early[6].wait()
        self.wd[x, aligned(quarter * 256, 256), :] = at_s[576:832, :].astype(bf16)
        self.crossing(5).start()
        self.crossing(6).start()
        self.cot_load.start()
        for go in self.own_rest:
            go.start()

    def tokens(self):
        self.tok_load.wait()

    def others(self, body):
        for j in range(4):

            @pl.when(self.quarter != j)
            def _(j=j):
                body(j)

    def weights(self):
        for go in self.own_in:
            go.wait()
        mf_s, gin = self.mf_s, self.gin_v

        def body(j):
            rows = slice(j * 128, (j + 1) * 128)
            self.permuted([mf_s[0, rows, :], mf_s[1, rows, :], gin[rows, 0:256]], rows)

        self.others(body)

    def passed(self, *items):
        for item in items:
            self.crossing(item).wait()
            self.inward(item).start()
            self.aside(item).start()

    def turned(self, *items):
        for item in items:
            self.aside(item).wait()
            self.onward(item).start()

    def done(self, *items):
        for item in items:
            self.inward(item).wait()
            self.onward(item).wait()

    def fore(self, i):
        last = self.images - 1
        for k, steps in {
            0: (("passed", 0), ("passed", 1)),
            1: (("turned", 0), ("passed", 2)),
            2: (("turned", 1),),
            last: (("done", 0), ("done", 1), ("passed", 3)),
            last + 1: (("turned", 2), ("passed", 4)),
            last + 2: (("turned", 3),),
            last + 3: (("passed", 5),),
            last + 4: (("turned", 4), ("passed", 6)),
        }.items():

            @pl.when(i == k)
            def _(k=k, steps=steps):
                for name, item in steps:
                    {"passed": self.passed, "turned": self.turned, "done": self.done}[name](item)
                if k == last:
                    self.crossing(len(ITEMS)).wait()

    def cotangent(self):
        self.done(2)
        for go in self.own_rest:
            go.wait()
        x, gin, da_s, af_s = self.x, self.gin_v, self.da_s, self.af_s

        def body(j):
            rows = slice(j * 64, (j + 1) * 64)
            self.wo[x, rows, 0:256] = gin[rows, 256:512].astype(bf16)
            self.wo[x, rows, 256:512] = gin[j * 64 + 256 : (j + 1) * 64 + 256, 256:512].astype(bf16)
            rows = slice(j * 128, (j + 1) * 128)
            self.wu[x, rows, 0:512] = da_s[rows, :].astype(bf16)
            self.wu[x, rows, 512:1024] = af_s[rows, :].astype(bf16)
            rows = slice(j * 256, (j + 1) * 256)
            if j < 3:
                self.wd[x, rows, :] = (da_s, af_s, gin)[j][512:768, :].astype(bf16)
            else:
                self.wd[x, 768:896, :] = da_s[768:896, :].astype(bf16)
                self.wd[x, 896:1024, :] = af_s[768:896, :].astype(bf16)

        self.others(body)
        self.cot_load.wait()

    def near(self):
        self.turned(5, 6)

    def arrived(self):
        self.done(3, 4, 5, 6)


    def output(self):
        self.out_v[...] = self.gin_v[...].astype(bf16)
        self.saving(0).start()

    def saving(self, i):
        src, dst = (
            (self.out_v, self.out),
            (self.gin_v, self.gin),
        )[i]
        return pltpu.make_async_copy(src, dst, self.save.at[i])

    def finished(self):
        self.saving(1).start()

    def keeping(self, c):
        base, R = CHUNKS[c]
        rows = pl.ds(base, R)
        return pltpu.make_async_copy(
            self.grads.at[0, rows, :], self.full.at[rows, :], self.save.at[2 + c]
        )


    def copy(self, src, dst, chunk, slot, mate):
        return pltpu.make_async_remote_copy(
            src_ref=src,
            dst_ref=dst,
            send_sem=self.send.at[chunk, slot],
            recv_sem=self.recv.at[chunk, slot],
            device_id=mate,
            device_id_type=MESH,
        )

    def flights(self, c, s):
        base, R = CHUNKS[c]
        half, quarter, piece = R // 2, R // 4, R // 16
        x, y, z, core, grads = self.x, self.y, self.z, self.core, self.grads
        mine = base + core * half
        theirs = aligned(base + (1 - core) * half, half)
        if c >= LATE:
            if s == 0:
                src = grads.at[1 - x, theirs, :]
                return [self.copy(src, self.firsts[c - LATE], c, 11, self.core_mate)]
            if s == 1:
                return [self.copy(self.firsts[c - LATE], self.xs[c], c, 1, self.x_mate)]
            if s == 2:
                return [self.copy(grads.at[x, theirs, :], self.cores[c], c, 0, self.core_mate)]
            s -= 1
        else:
            if s == 0:
                return [self.copy(grads.at[:, theirs, :], self.cores[c], c, 0, self.core_mate)]
            if s == 1:
                return [self.copy(self.cores[c].at[1 - x], self.xs[c], c, 1, self.x_mate)]
        if s == 2:
            src = self.xs[c].at[aligned((1 - y) * quarter, quarter), :]
            return [self.copy(src, self.ys[c], c, 2, self.y_mate)]
        if s == 3:
            return [
                self.copy(
                    self.ys[c].at[aligned(self.z_others[k] * piece, piece), :],
                    self.zs[c].at[k],
                    c,
                    3 + k,
                    self.z_mates[k],
                )
                for k in range(3)
            ]
        if s == 4:
            own = grads.at[0, aligned(mine + y * quarter + z * piece, piece), :]
            return [self.copy(own, own, c, 6 + k, self.z_mates[k]) for k in range(3)]
        if s == 5:
            own = grads.at[0, aligned(mine + y * quarter, quarter), :]
            return [self.copy(own, own, c, 9, self.y_mate)]
        if s == 6:
            own = grads.at[0, aligned(mine, half), :]
            return [self.copy(own, own, c, 10, self.core_mate)]
        return []

    def stage(self, c, s):
        base, R = CHUNKS[c]
        half, quarter, piece = R // 2, R // 4, R // 16
        x, y, z, core, grads = self.x, self.y, self.z, self.core, self.grads
        mine = base + core * half
        late = c >= LATE
        if s > 0 and not (late and s == 2):
            for flight in self.flights(c, s - 1):
                flight.wait()
        if late and s == 3:
            self.flights(c, 1)[0].wait()

        def total(*parts):
            out = None
            for part in parts:
                part = part.astype(f32)
                out = part if out is None else out + part
            return out.astype(bf16)

        cores, xs, ys, zs = self.cores[c], self.xs[c], self.ys[c], self.zs[c]
        step = s - 1 if late else s
        if late and s == 1:
            first = self.firsts[c - LATE]

            def body(i, size):
                rows, own = pl.ds(i, size), aligned(mine + i, size)
                first[rows, :] = total(grads[1 - x, own, :], first[rows, :])

            tile_loop(half, 128, body)
        elif late and s == 3:

            def body(i, size):
                rows, own = pl.ds(i, size), aligned(mine + i, size)
                xs[rows, :] = total(grads[x, own, :], cores[rows, :], xs[rows, :])

            tile_loop(half, 128, body)
        elif not late and s == 1:

            def body(i, size):
                rows, own = pl.ds(i, size), aligned(mine + i, size)
                for t in range(2):
                    cores[t, rows, :] = total(grads[t, own, :], cores[t, rows, :])

            tile_loop(half, 128, body)
        elif not late and s == 2:

            def body(i, size):
                rows = pl.ds(i, size)
                xs[rows, :] = total(cores[x, rows, :], xs[rows, :])

            tile_loop(half, 128, body)
        elif step == 3:

            def body(i, size):
                rows, own = pl.ds(i, size), aligned(y * quarter + i, size)
                ys[rows, :] = total(xs[own, :], ys[rows, :])

            tile_loop(quarter, 128, body)
        elif step == 4:
            own = aligned(z * piece, piece)
            grads[0, aligned(mine + y * quarter + z * piece, piece), :] = total(
                ys[own, :], zs[0], zs[1], zs[2]
            )
        if step == 7:
            self.keeping(c).start()
        for flight in self.flights(c, s):
            flight.start()

    def small_flights(self, s):
        def small_copy(src, dst, slot, mate):
            return pltpu.make_async_remote_copy(
                src_ref=src,
                dst_ref=dst,
                send_sem=self.ssend.at[slot],
                recv_sem=self.srecv.at[slot],
                device_id=mate,
                device_id_type=MESH,
            )

        if s < 3:
            mate = (self.core_mate, self.x_mate, self.y_mate)[s]
            return [small_copy(self.small_z.at[s], self.small_in.at[s], s, mate)]
        return [
            small_copy(self.small_z.at[3], self.small_z.at[4 + self.z], 3 + k, self.z_mates[k])
            for k in range(3)
        ]

    def small_stage(self, s):
        small_z = self.small_z
        if s > 0:
            for flight in self.small_flights(s - 1):
                flight.wait()
        if s == 0:
            small_z[0] = self.gsmall[...]
        elif s <= 3:
            small_z[s] = small_z[s - 1] + self.small_in[s - 1]
        else:
            self.small_sum[...] = (small_z[4] + small_z[5]) + (small_z[6] + small_z[7])
            return
        if s == 3:
            small_z[4 + self.z] = small_z[3]
        for flight in self.small_flights(s):
            flight.start()

    def point(self, name):
        for c, s in PLAN.get(name, ()):
            self.stage(c, s)

    def turn(self, name, i, count):
        for k in range(count):
            if name + str(k) in PLAN:

                @pl.when(i == k)
                def _(k=k):
                    self.point(name + str(k))

    def sums(self, k):
        self.small_stage(k)

    def end(self):
        self.small_stage(2)
        for k, (c, s) in enumerate(TAIL):
            self.stage(c, s)
            if k == len(TAIL) // 3:
                self.small_stage(3)
        self.small_stage(4)
        for i in range(2):
            self.saving(i).wait()
        for c in range(len(CHUNKS)):
            self.keeping(c).wait()


def main_kernel(images, counts, tok, cot, w_in, w_out, w_up, w_down, taps, bias, vecs,
                out, gin, full, small_sum, *scratch):
    n = len(block_scratch(images))
    inner, rest = scratch[:n], scratch[n:]
    gin_v, grads, gsmall, wi, wo, wu, wd, small = rest[:8]
    rest = rest[8:]
    count = len(CHUNKS)
    cores, xs, ys, zs = (rest[count * i : count * (i + 1)] for i in range(4))
    rest = rest[4 * count :]
    firsts, rest = rest[: count - LATE], rest[count - LATE :]
    x_s, co_s, at_s, af_s, da_s, gp_s, mf_s, na_s, nb_s, lb_s = inner[:10]
    traffic = Traffic(
        images,
        (tok, cot, w_in, w_out, w_up, w_down, taps, bias, out, gin, full, small_sum,
         gin_v, grads, gsmall, wi, wo, wu, wd, small,
         at_s, af_s, da_s, gp_s, mf_s, nb_s, lb_s, co_s.at[0 : images * WIN, :],
         cores, xs, ys, zs, firsts, *rest),
    )
    x = lax.axis_index("tensor")
    limit = counts[lax.axis_index("dp")] - x * images
    traffic.begin()
    block_body(
        images, limit, x, traffic, wi, wo, wu, wd, small, vecs, gin_v, grads, gsmall, *inner
    )
    traffic.end()


def main_call(counts, tok, cot, w_in, w_out, w_up, w_down, taps, bias, vecs):
    images = tok.shape[0] // WIN
    S = jax.ShapeDtypeStruct
    V = pltpu.VMEM
    away = pl.BlockSpec(memory_space=pl.ANY)
    here = pl.BlockSpec(memory_space=V)
    sizes = [R for _, R in CHUNKS]
    dma = pltpu.SemaphoreType.DMA
    return pl.pallas_call(
        functools.partial(main_kernel, images),
        out_shape=(
            S(tok.shape, bf16),
            S(tok.shape, f32),
            S((GROWS, 256), bf16),
            S((24, D), f32),
        ),
        in_specs=[pl.BlockSpec(memory_space=pltpu.SMEM)] + [away] * 6 + [here] * 3,
        out_specs=[away] * 3 + [here],
        scratch_shapes=block_scratch(images)
        + [
            V(tok.shape, f32),
            V((2, GROWS, 256), bf16),
            V((24, D), f32),
            V((2, 3, D, 256), bf16),
            V((2, 256, D), bf16),
            V((2, D, 1024), bf16),
            V((2, 1024, D), bf16),
            V((2, 16, 256), f32),
        ]
        + [V((2, R // 2, 256), bf16) for R in sizes[:LATE]]
        + [V((R // 2, 256), bf16) for R in sizes[LATE:]]
        + [V((R // 2, 256), bf16) for R in sizes]
        + [V((R // 4, 256), bf16) for R in sizes]
        + [V((3, R // 16, 256), bf16) for R in sizes]
        + [V((R // 2, 256), bf16) for R in sizes[LATE:]]
        + [
            V((3, 24, D), f32),
            V((8, 24, D), f32),
            dma((len(sizes), SLOTS)),
            dma((len(sizes), SLOTS)),
            dma((6,)),
            dma((6,)),
            dma((8, 4)),
            dma((8, 4)),
            dma((21,)),
            dma((2 + len(sizes),)),
        ],
        compiler_params=pltpu.CompilerParams(
            collective_id=1, has_side_effects=True, vmem_limit_bytes=63 * 1024 * 1024
        ),
    )(counts, tok, cot, w_in, w_out, w_up, w_down, taps, bias, vecs)


def local(
    tokens, cotangent, image_counts,
    w_in, m_in, v_in, w_out, m_out, v_out, w_up, m_up, v_up, w_down, m_down, v_down,
    kernel, m_kernel, v_kernel, up_bias, m_bias, v_bias, vectors, m_vectors, v_vectors,
):
    biases = tuple(a.reshape(1, -1) for a in (up_bias, m_bias, v_bias))
    raw_out, raw_gin, full, small_sum = main_call(
        image_counts, tokens, cotangent, w_in, w_out, w_up, w_down, kernel, biases[0], vectors
    )
    new = adam_step(
        full,
        small_sum,
        raw_out,
        raw_gin,
        (w_down, m_down, v_down, w_up, m_up, v_up, w_out, m_out, v_out, w_in, m_in, v_in),
        (kernel, m_kernel, v_kernel)
        + biases
        + (vectors, m_vectors, v_vectors),
    )
    down, up, mid, first = new[:4], new[4:8], new[8:12], new[12:16]
    bias = tuple(a.reshape(-1) for a in new[19:22])
    return (*new[25:27], *first, *mid, *up, *down, *new[16:19], *bias, *new[22:25])


def general(
    tokens, cotangent, image_counts,
    w_in, m_in, v_in, w_out, m_out, v_out, w_up, m_up, v_up, w_down, m_down, v_down,
    kernel, m_kernel, v_kernel, up_bias, m_bias, v_bias, vectors, m_vectors, v_vectors,
):
    images = tokens.shape[0] // WIN
    place = lax.axis_index("tensor")
    live = image_counts[lax.axis_index("dp")] - place * images

    def whole(a, axis):
        return lax.all_gather(a, "tensor", axis=axis, tiled=True)

    wi = whole(w_in.astype(bf16), 1).reshape(D, 2, 8, 3, HD).transpose(1, 3, 0, 2, 4)
    wi = wi.reshape(2, 3, D, 256)
    wo = whole(w_out.astype(bf16), 0).reshape(2, 256, D)
    wd = whole(w_down.astype(bf16), 0).reshape(2, 1024, D)
    wu = whole(w_up.astype(bf16), 1).reshape(D, 2, 1024).transpose(1, 0, 2)
    small = jnp.concatenate(
        [
            whole(kernel, 1).reshape(9, 2, 256).transpose(1, 0, 2),
            whole(up_bias, 0).reshape(2, 4, 256),
            jnp.zeros((2, 3, 256), f32),
        ],
        axis=1,
    )
    out, grad_in, grads, gs = block(
        live.reshape(1), tokens, cotangent, wi, wo, wu, wd, small, vectors
    )
    grads = grads.astype(f32)

    def columns(first, rows, count):
        part = grads[:, first : first + rows * count].reshape(2, count, rows, 256)
        return part

    g_down = grads[:, DOWN:UP].reshape(2, 2, 2, 512, 256).transpose(0, 1, 3, 2, 4).reshape(FF, D)
    g_up = columns(UP, 512, 4).transpose(2, 0, 1, 3).reshape(D, FF)
    g_out = columns(OUT, 256, 2).transpose(0, 2, 1, 3).reshape(D, D)
    g_in = columns(IN, 512, 3).reshape(2, 3, D, 8, HD).transpose(2, 0, 3, 1, 4).reshape(D, 3 * D)

    def owned(a, axis):
        return lax.psum(lax.psum_scatter(a, "tensor", scatter_dimension=axis, tiled=True), "dp")

    g_in, g_out, g_up, g_down = owned(g_in, 1), owned(g_out, 0), owned(g_up, 1), owned(g_down, 0)
    g_kernel, g_bias, g_vectors = owned(gs[0:9], 1), owned(gs[16:20].reshape(-1), 0), owned(gs[9:16], 1)
    vector_width = m_vectors.shape[1]
    own_vectors = lax.dynamic_slice_in_dim(vectors, place * vector_width, vector_width, 1)
    results = [out, grad_in]
    for w, m, v, g, rate in (
        (w_in, m_in, v_in, g_in, D**-0.5),
        (w_out, m_out, v_out, g_out, (D // HD) ** -0.5),
        (w_up, m_up, v_up, g_up, D**-0.5),
        (w_down, m_down, v_down, g_down, FF**-0.5),
    ):
        new = adam(w, m, v, g, rate, 0.05)
        results += [*new, new[0].astype(bf16)]
    results += adam(kernel, m_kernel, v_kernel, g_kernel, 2.0, 0.05)
    results += adam(up_bias, m_bias, v_bias, g_bias, 0.3, 0.0)
    results += adam(own_vectors, m_vectors, v_vectors, g_vectors, 0.3, 0.0)
    return tuple(results)


def solution(mesh):
    rows, columns = P("tensor", None), P(None, "tensor")
    tokens = P(("dp", "tensor"), None)
    mats = (columns,) * 3 + (rows,) * 3 + (columns,) * 3 + (rows,) * 3
    news = (columns,) * 4 + (rows,) * 4 + (columns,) * 4 + (rows,) * 4
    pairs = mesh.shape["dp"] == 16 and mesh.shape["tensor"] == 2
    return jax.shard_map(
        local if pairs else general,
        mesh=mesh,
        in_specs=(tokens, tokens, P(), *mats)
        + (columns,) * 3
        + (P("tensor"),) * 3
        + (P(), columns, columns),
        out_specs=(tokens, tokens, *news) + (columns,) * 3 + (P("tensor"),) * 3 + (columns,) * 3,
        check_vma=False,
    )
```

```python
import functools
import jax
import jax.numpy as jnp
from jax import lax
from jax.experimental import pallas as pl
from jax.experimental.pallas import tpu as pltpu
from jax.sharding import PartitionSpec as P

D = 512
HD = 32
FF = 2048
SIDE = 14
WIDE = 16
WIN = SIDE * SIDE
ROWS = SIDE * WIDE
KEYS = 256
GROUPS = D // 128
STEP = 5
DOWN, UP, OUT, IN, GROWS = 0, 2048, 4096, 4608, 6144
MESH = pl.DeviceIdType.MESH
eps = 1e-05
f32 = jnp.float32
bf16 = jnp.bfloat16
C0 = 0.7978845608028654
C1 = 0.044715


def nn(a, b):
    return lax.dot_general(a, b, (((1,), (0,)), ((), ())), preferred_element_type=f32)


def nt(a, b):
    return lax.dot_general(a, b, (((1,), (1,)), ((), ())), preferred_element_type=f32)


def tn(a, b):
    return lax.dot_general(a, b, (((0,), (0,)), ((), ())), preferred_element_type=f32)


def normed(x):
    c = x - jnp.mean(x, axis=-1, keepdims=True)
    r = lax.rsqrt(jnp.mean(c * c, axis=-1, keepdims=True) + eps)
    return c * r, r


def norm_back(u, xhat, r):
    return r * (
        u
        - jnp.mean(u, axis=-1, keepdims=True)
        - xhat * jnp.mean(u * xhat, axis=-1, keepdims=True)
    )


def gelu_pair(x):
    x2 = x * x
    t = 0.5 * jnp.tanh(x * (C0 + (C0 * C1) * x2))
    h = 0.5 + t
    value = x * h
    return value, h + value * ((0.5 - t) * (2.0 * C0 + (6.0 * C0 * C1) * x2))


def gelu(x):
    return x * (0.5 + 0.5 * jnp.tanh(x * (C0 + (C0 * C1) * (x * x))))


def row_sum(x):
    return jnp.sum(x, axis=0, keepdims=True)


def shift_rows(x, by):
    z = jnp.zeros((abs(by), x.shape[1]), x.dtype)
    if by > 0:
        return jnp.concatenate([z, x[:-by]], axis=0)
    return jnp.concatenate([x[-by:], z], axis=0)


def roll1(x, by):
    return pltpu.roll(x, by % x.shape[0], 0)


def pool(c):
    s = c + roll1(c, 1) + roll1(c, -1)
    return s + shift_rows(s, WIDE) + shift_rows(s, -WIDE)


def block_body(images, limit, first_half, hooks, wi, wo, wu, wd, small, vecs,
               gin, grads, gsmall,
               x_s, co_s, at_s, af_s, da_s, gp_s, mf_s, na_s, nb_s, lb_s, la_s, mx_s,
               q_s, k_s, v_s, dm_s, hd_s, dp_s, pj_s, p_s, taps_s, ds_s):
    gain_a, shift_a, gain_b, shift_b, scale_a, scale_f, bias_f = (
        vecs[i : i + 1, :] for i in range(7)
    )
    gsmall[...] = jnp.zeros_like(gsmall)
    gtaps = taps_s
    gtaps[...] = jnp.zeros_like(gtaps)
    blank = jnp.zeros((KEYS - ROWS, 256), bf16)
    for ref in (q_s, k_s, v_s, dm_s):
        for t in range(2):
            for n in range(images):
                ref[t, n * KEYS + ROWS : (n + 1) * KEYS, :] = blank

    cell = lax.broadcasted_iota(jnp.int32, (ROWS, 1), 0)
    inside = lax.rem(cell, WIDE) < SIDE
    lane = lax.broadcasted_iota(jnp.int32, (1, 128), 1)
    head_masks = [(lane // HD) == h for h in range(4)]
    key_row = lax.broadcasted_iota(jnp.int32, (KEYS, 128), 0)
    key_lane = lax.broadcasted_iota(jnp.int32, (KEYS, 128), 1)
    key_pad = (lax.rem(key_row, WIDE) >= SIDE) | (key_row >= ROWS)
    key_block = jnp.where(key_pad & (key_lane == 0), -1e30, 0.0).astype(bf16)
    one_block = jnp.where(key_lane == 0, 1.0, 0.0).astype(bf16)

    def padded(n):
        return pl.ds(pl.multiple_of(n * ROWS, WIDE), ROWS)

    def held(n):
        return pl.ds(pl.multiple_of(n * KEYS, WIDE), ROWS)

    def whole(n):
        return pl.ds(pl.multiple_of(n * KEYS, WIDE), KEYS)

    def masked(h, a):
        return jnp.where(head_masks[h], a, jnp.zeros_like(a))

    def prepare(n, carry):
        rows = padded(n)
        xhat, _ = normed(x_s[rows, :].astype(f32))
        na_s[rows, :] = (xhat * gain_a + shift_a).astype(bf16)
        return carry

    def tap(t, i, ls):
        return small[t, pl.ds(i, 1), ls]

    def attend(t, n):
        rows = padded(n)
        na = na_s[rows, :]
        k_s[t, held(n), :] = nn(na, wi[t, 1]).astype(bf16)
        v_s[t, held(n), :] = nn(na, wi[t, 2]).astype(bf16)
        for g in range(2):
            ls = slice(g * 128, (g + 1) * 128)
            gp = nn(na, wi[t, 0, :, ls])
            gp_s[t, rows, ls] = gp
            field = jnp.where(inside, gelu(gp), 0.0)
            back, ahead = roll1(field, 1), roll1(field, -1)
            conv = None
            for a in range(3):
                part = (
                    tap(t, 3 * a, ls) * back
                    + tap(t, 3 * a + 1, ls) * field
                    + tap(t, 3 * a + 2, ls) * ahead
                )
                if a != 1:
                    part = shift_rows(part, WIDE * (1 - a))
                conv = part if conv is None else conv + part
            pooled = pool(jnp.where(inside, conv, 0.0)) * (HD ** (-0.5) / 9.0)
            q_s[t, held(n), ls] = pooled.astype(bf16)
        for g in range(2):
            ls = slice(g * 128, (g + 1) * 128)
            qa = jnp.concatenate([q_s[t, whole(n), ls], one_block], axis=1)
            kg = k_s[t, whole(n), ls]
            vt = jnp.transpose(v_s[t, whole(n), ls])
            mixed = []
            keys = jnp.concatenate(
                [jnp.concatenate([masked(h, kg), key_block], axis=1) for h in range(4)], axis=0
            )
            scores = nt(keys, qa)
            for h in range(4):
                hs = slice(h * KEYS, (h + 1) * KEYS)
                s = scores[hs]
                e = jnp.exp(s - jnp.max(s, axis=0, keepdims=True))
                p_s[t, n * 2 + g, :, hs] = (e * (1.0 / jnp.sum(e, axis=0, keepdims=True))).astype(bf16)
            for h in range(4):
                p = p_s[t, n * 2 + g, :, h * KEYS : (h + 1) * KEYS]
                mixed.append(nn(vt[h * HD : (h + 1) * HD], p))
            mix = jnp.transpose(jnp.concatenate(mixed, axis=0))[:ROWS]
            mf_s[t, rows, ls] = mix
            mx_s[t, rows, ls] = mix.astype(bf16)

    def finish(n, carry):
        rows = padded(n)
        attn = nn(mx_s[0, rows, :], wo[0]) + nn(mx_s[1, rows, :], wo[1])
        at_s[rows, :] = attn
        after = x_s[rows, :].astype(f32) + scale_a * attn
        af_s[rows, :] = after
        xhat, _ = normed(after)
        nb_s[rows, :] = (xhat * gain_b + shift_b).astype(bf16)
        lb_s[rows, :] = (scale_f * co_s[rows, :].astype(f32)).astype(bf16)
        return carry

    def feed(t, u, n):
        rows = padded(n)
        us = slice(u * 512, (u + 1) * 512)
        cs = pl.ds(pl.multiple_of(t * 1024 + u * 512, 512), 512)
        unit_bias = jnp.concatenate(
            [small[t, 9 + 2 * u + j : 10 + 2 * u + j, :] for j in range(2)], axis=1
        )
        value, slope = gelu_pair(nn(nb_s[rows, :], wu[t, :, us]) + unit_bias)
        hd_s[rows, cs] = value.astype(bf16)
        d_pre = slope * nt(lb_s[rows, :], wd[t, us, :])
        gsmall[pl.ds(16 + 2 * t + u, 1), :] += row_sum(d_pre)
        dp_s[rows, cs] = d_pre.astype(bf16)

    def digest(n, carry):
        rows = padded(n)
        branch = nn(hd_s[rows, 0:1024], wd[0]) + nn(hd_s[rows, 1024:2048], wd[1])
        d_nb = nt(dp_s[rows, 0:1024], wu[0]) + nt(dp_s[rows, 1024:2048], wu[1])
        co = co_s[rows, :].astype(f32)
        after = af_s[rows, :]
        xhat, r = normed(after)
        moved = branch + bias_f
        live = (n < limit).astype(f32)
        af_s[rows, :] = (after + scale_f * moved) * live
        gsmall[14:15, :] += row_sum(co * moved)
        gsmall[15:16, :] += scale_f * row_sum(co)
        gsmall[11:12, :] += row_sum(d_nb * xhat)
        gsmall[12:13, :] += row_sum(d_nb)
        d_after = co + norm_back(gain_b * d_nb, xhat, r)
        da_s[rows, :] = d_after
        gsmall[13:14, :] += row_sum(d_after * at_s[rows, :])
        la = (scale_a * d_after).astype(bf16)
        la_s[rows, :] = la
        for t in range(2):
            dm_s[t, held(n), :] = nt(la, wo[t]).astype(bf16)
        hooks.turn("d", n)
        return carry

    pick_row = lax.broadcasted_iota(jnp.int32, (256, 128), 0)
    pick_lane = lax.broadcasted_iota(jnp.int32, (256, 128), 1)
    pick = jnp.where(
        (lax.rem(pick_row, 128) // HD == lax.rem(pick_lane, 4)) & (pick_lane < 8), 1.0, 0.0
    ).astype(bf16)

    def split(a):
        high = a.astype(bf16)
        return high, (a - high.astype(f32)).astype(bf16)

    def inner_block(a):
        sums = nn(jnp.concatenate(split(a), axis=1), pick)
        high, low = split(sums)
        return jnp.where(lane < 4, high, low)

    blank_rows = jnp.zeros((KEYS - ROWS, 128), bf16)

    minus = [
        jnp.where((lane == h) | (lane == h + 4), -1.0, 0.0).astype(bf16) for h in range(4)
    ]

    def recede(t, n, turn):
        rows = padded(n)
        for g in range(2):
            ls = slice(g * 128, (g + 1) * 128)
            inner = inner_block(dm_s[t, held(n), ls].astype(f32) * mf_s[t, rows, ls])
            dmg = dm_s[t, whole(n), ls]
            left = jnp.concatenate(
                [dmg, jnp.concatenate([inner, blank_rows], axis=0)], axis=1
            )
            qg = q_s[t, whole(n), ls]
            kg = k_s[t, whole(n), ls]
            vg = v_s[t, whole(n), ls]
            kt = jnp.transpose(kg)
            dqs = []
            right = jnp.concatenate(
                [
                    jnp.concatenate([masked(h, vg), jnp.broadcast_to(minus[h], (KEYS, 128))], axis=1)
                    for h in range(4)
                ],
                axis=0,
            )
            d_probs = nt(right, left)
            for h in range(4):
                hs = slice(h * KEYS, (h + 1) * KEYS)
                e = p_s[t, n * 2 + g, :, hs]
                ds_s[:, hs] = (e.astype(f32) * d_probs[hs]).astype(bf16)
            dv = nn(
                p_s[t, n * 2 + g], jnp.concatenate([masked(h, dmg) for h in range(4)], axis=0)
            )
            dk = nn(ds_s[...], jnp.concatenate([masked(h, qg) for h in range(4)], axis=0))
            for h in range(4):
                dqs.append(nn(kt[h * HD : (h + 1) * HD], ds_s[:, h * KEYS : (h + 1) * KEYS]))
            dq = jnp.transpose(jnp.concatenate(dqs, axis=0))[:ROWS]
            pj_s[t, 1, rows, ls] = dk[:ROWS].astype(bf16)
            pj_s[t, 2, rows, ls] = dv[:ROWS].astype(bf16)
            value, slope = gelu_pair(gp_s[t, rows, ls])
            field = jnp.where(inside, value, 0.0)
            d_conv = jnp.where(inside, pool(dq * (HD ** (-0.5) / 9.0)), 0.0)
            shifted = (roll1(field, 1), field, roll1(field, -1))
            d_cols = [None, None, None]
            for a in range(3):
                moved = d_conv if a == 1 else shift_rows(d_conv, WIDE * (a - 1))
                for b in range(3):
                    i = 3 * a + b
                    gtaps[t, i : i + 1, ls] += row_sum(moved * shifted[b])
                    term = tap(t, i, ls) * moved
                    d_cols[b] = term if d_cols[b] is None else d_cols[b] + term
            d_field = roll1(d_cols[0], -1) + d_cols[1] + roll1(d_cols[2], 1)
            pj_s[t, 0, rows, ls] = jnp.where(inside, slope * d_field, 0.0).astype(bf16)
            hooks.turn("r", n, 2, turn + g)

    def rise(n, carry):
        rows = padded(n)
        d_na = None
        for t in range(2):
            for part in range(3):
                term = nt(pj_s[t, part, rows, :], wi[t, part])
                d_na = term if d_na is None else d_na + term
        xhat, r = normed(x_s[rows, :].astype(f32))
        gsmall[9:10, :] += row_sum(d_na * xhat)
        gsmall[10:11, :] += row_sum(d_na)
        da_s[rows, :] += norm_back(gain_a * d_na, xhat, r)
        hooks.turn("s", n)
        return carry

    def narrow_rows(target, source):
        for i in range(images * SIDE):
            target[i * SIDE : (i + 1) * SIDE, :] = source[i * WIDE : i * WIDE + SIDE, :]

    def store_down(u):
        for t in range(2):
            cs = slice((2 * t + u) * 512, (2 * t + u + 1) * 512)
            down = tn(hd_s[:, cs], lb_s[...]).astype(bf16)
            for j in range(2):
                first = DOWN + (2 * u + j) * 512
                grads[t, first : first + 512, :] = down[:, j * 256 : (j + 1) * 256]

    def store_up(u):
        for t in range(2):
            cs = slice((2 * t + u) * 512, (2 * t + u + 1) * 512)
            up = tn(nb_s[...], dp_s[:, cs]).astype(bf16)
            for j in range(2):
                first = UP + (2 * u + j) * 512
                grads[t, first : first + 512, :] = up[:, j * 256 : (j + 1) * 256]

    def store_out():
        for t in range(2):
            g_out = tn(mx_s[t], la_s[...]).astype(bf16)
            for j in range(2):
                first = OUT + j * 256
                grads[t, first : first + 256, :] = g_out[:, j * 256 : (j + 1) * 256]

    def store_in(t, part):
        first = IN + part * 512
        grads[t, first : first + 512, :] = tn(na_s[...], pj_s[t, part]).astype(bf16)

    def widen(source, spares, target, scaled):
        temp = at_s
        temp[0 : images * WIN, :] = source[0 : images * WIN, :].astype(f32)
        for first, width, spare in spares:
            cs = slice(first, first + width)
            pad = jnp.zeros((WIDE - SIDE, width), f32)
            for n in range(images):
                for i in range(n * SIDE, (n + 1) * SIDE):
                    cells = temp[i * SIDE : (i + 1) * SIDE, cs]
                    if scaled:
                        cells = cells * (n < limit).astype(f32)
                    spare[i * WIDE : i * WIDE + SIDE, :] = cells
                    spare[i * WIDE + SIDE : (i + 1) * WIDE, :] = pad
            target[:, cs] = spare[...].astype(bf16)

    loop = lax.fori_loop
    hooks.tokens()
    widen(nb_s, [(t * 256, 256, gp_s.at[t]) for t in range(2)], x_s, False)
    loop(0, images, prepare, 0)
    hooks.weights()
    other_half = 1 - first_half

    def fore(i, carry):
        later = i // images
        attend(first_half + (other_half - first_half) * later, lax.rem(i, images))
        hooks.fore(i)
        return carry

    loop(0, 2 * images, fore, 0)
    hooks.cotangent()
    widen(lb_s, [(0, D, da_s)], co_s, True)
    loop(0, images, finish, 0)
    hooks.near()

    def feed_own(n, carry):
        for u in range(2):
            feed(first_half, u, n)
        return carry

    def feed_first(n, carry):
        feed(other_half, 0, n)
        return carry

    def feed_second(n, carry):
        feed(other_half, 1, n)
        hooks.turn("f", n)
        return carry

    loop(0, images, feed_own, 0)
    hooks.arrived()
    loop(0, images, feed_first, 0)
    store_down(0)
    hooks.point("D0")
    store_up(0)
    hooks.point("U0")
    loop(0, images, feed_second, 0)
    store_down(1)
    hooks.point("D1")
    store_up(1)
    hooks.point("U1")
    loop(0, images, digest, 0)
    store_out()
    hooks.point("O")

    def aft(n, carry):
        recede(other_half, n, 0)
        return carry

    loop(0, images, aft, 0)
    for part in (2, 1, 0):
        store_in(other_half, part)
        hooks.point("A%d" % part)

    def aft2(n, carry):
        recede(first_half, n, 2 * images)
        return carry

    loop(0, images, aft2, 0)
    for part in (2, 1, 0):
        store_in(first_half, part)
        hooks.point("B%d" % part)
    loop(0, images, rise, 0)
    for t in range(2):
        gsmall[0:9, t * 256 : (t + 1) * 256] = gtaps[t, 0:9, :]
    hooks.sums(0)
    narrow_rows(gin, af_s)
    hooks.output()
    hooks.sums(1)
    hooks.point("N")
    narrow_rows(gin, da_s)
    hooks.finished()
    hooks.point("R")


class Quiet:
    def __init__(self, tok, cot, nb_s, lb_s, out, gin):
        self.refs = tok, cot, nb_s, lb_s, out, gin

    def tokens(self):
        tok, cot, nb_s, lb_s, _, _ = self.refs
        rows = tok.shape[0]
        nb_s[0:rows, :] = tok[...]
        lb_s[0:rows, :] = cot[...]

    def output(self):
        _, _, _, _, out, gin = self.refs
        out[...] = gin[...].astype(bf16)

    def point(self, name):
        pass

    def turn(self, name, n, stride=1, offset=0):
        pass

    sums = fore = point

    def weights(self):
        pass

    cotangent = near = arrived = finished = weights


def block_kernel(images, lim, tok, cot, wi, wo, wu, wd, small, vecs, out, gin, grads, gsmall, *scratch):
    quiet = Quiet(tok, cot, scratch[8], scratch[9], out, gin)
    block_body(images, lim[0], 0, quiet, wi, wo, wu, wd, small, vecs, gin, grads, gsmall, *scratch)


def block_scratch(images):
    R = images * ROWS
    K = images * KEYS
    V = pltpu.VMEM
    return (
        [V((R, D), bf16)] * 2
        + [V((R, D), f32)] * 3
        + [V((2, R, 256), f32)] * 2
        + [V((R, D), bf16)] * 4
        + [V((2, R, 256), bf16)]
        + [V((2, K, 256), bf16)] * 4
        + [V((R, FF), bf16)] * 2
        + [
            V((2, 3, R, 256), bf16),
            V((2, images * 2, KEYS, 4 * KEYS), bf16),
            V((2, 16, 256), f32),
            V((KEYS, 4 * KEYS), bf16),
        ]
    )


def block(lim, tok, cot, wi, wo, wu, wd, small, vecs):
    images = tok.shape[0] // WIN
    S = jax.ShapeDtypeStruct
    V = pltpu.VMEM
    return pl.pallas_call(
        functools.partial(block_kernel, images),
        out_shape=(
            S(tok.shape, bf16),
            S(tok.shape, f32),
            S((2, GROWS, 256), bf16),
            S((24, D), f32),
        ),
        in_specs=[pl.BlockSpec(memory_space=pltpu.SMEM)] + [pl.BlockSpec(memory_space=V)] * 8,
        out_specs=[pl.BlockSpec(memory_space=V)] * 4,
        scratch_shapes=block_scratch(images),
        compiler_params=pltpu.CompilerParams(vmem_limit_bytes=62 * 1024 * 1024),
    )(lim, tok, cot, wi, wo, wu, wd, small, vecs)


def tile_loop(rows, size, body):
    if rows <= size:
        body(0, rows)
        return

    def step(i, carry):
        body(pl.multiple_of(i * size, size), size)
        return carry

    lax.fori_loop(0, rows // size, step, 0)


def aligned(first, size):
    return pl.ds(pl.multiple_of(first, 16), size)


def spread_four(part):
    a = lax.broadcasted_iota(jnp.int32, (384, 128), 1)
    b = lax.broadcasted_iota(jnp.int32, (384, 128), 0)
    return jnp.where(b == (a // HD) * (3 * HD) + part * HD + lax.rem(a, HD), 1.0, 0.0).astype(bf16)


def spread(part):
    a = lax.broadcasted_iota(jnp.int32, (256, 768), 0)
    b = lax.broadcasted_iota(jnp.int32, (256, 768), 1)
    return jnp.where(b == (a // HD) * (3 * HD) + part * HD + lax.rem(a, HD), 1.0, 0.0).astype(bf16)


def adam(w, m, v, g, rate, decay):
    half = 0.5 * g
    m = 0.5 * m + half
    v = 0.5 * v + half * g
    scale = 1.0 / (1.0 - 0.5**STEP)
    w = w - ((rate * scale) * m / (jnp.sqrt(v * scale) + 1e-08) + (rate * decay) * w)
    return w, m, v


def adam_tile(w, m, v, g, rate, decay):
    half = 0.5 * g
    m = 0.5 * m + half
    v = 0.5 * v + half * g
    scale = 1.0 / (1.0 - 0.5**STEP)
    seen = v * scale
    below = seen * lax.rsqrt(seen) + 1e-08
    inverse = pl.reciprocal(below, approx=True)
    inverse = inverse * (2.0 - below * inverse)
    w = w - ((rate * scale) * m * inverse + (rate * decay) * w)
    return w, m, v


MATRICES = (
    (1024, 512, FF**-0.5, 4, 64),
    (512, 1024, D**-0.5, 4, 32),
    (256, 512, (D // HD) ** -0.5, 1, 64),
    (512, 768, D**-0.5, 4, 64),
)


def adam_kernel(*refs):
    full, small_sum, raw_out, raw_gin = refs[:4]
    mats = refs[4:16]
    smalls = refs[16:25]
    outs = refs[25:41]
    small_outs = refs[41:50]
    out, gin = refs[50:52]
    bufs = refs[52:64]
    lows = refs[64:68]
    g_vm, out_vm, gin_vm, in_sem, out_sem, more_sem = refs[68:]
    g_load = pltpu.make_async_copy(full, g_vm, more_sem.at[2])
    g_load.start()
    loads = {}
    for i, (rows, cols, rate, pieces, tile) in enumerate(MATRICES):
        size = rows // pieces
        for p in range(pieces):
            rs = pl.ds(p * size, size)
            for j in range(3):
                go = pltpu.make_async_copy(
                    mats[3 * i + j].at[rs, :], bufs[3 * i + j].at[rs, :], in_sem.at[i, p, j]
                )
                go.start()
                loads[i, p, j] = go
    passing = [
        pltpu.make_async_copy(raw_out, out_vm, more_sem.at[0]),
        pltpu.make_async_copy(raw_gin, gin_vm, more_sem.at[1]),
    ]
    moves = [
        pltpu.make_async_copy(out_vm, out, more_sem.at[3]),
        pltpu.make_async_copy(gin_vm, gin, more_sem.at[4]),
    ]
    for go in passing:
        go.start()
    stores = []
    g_load.wait()
    for i, (rows, cols, rate, pieces, tile) in enumerate(MATRICES):
        size = rows // pieces
        bw, bm, bv = bufs[3 * i : 3 * i + 3]
        low = lows[i]
        spreads = [spread(part) for part in range(3)] if i == 3 else None
        for p in range(pieces):
            for j in range(3):
                loads[i, p, j].wait()

            def body(first, tile, i=i, p=p, bw=bw, bm=bm, bv=bv, low=low, rate=rate, size=size, spreads=spreads):
                rs = pl.ds(p * size + first, tile)
                if i == 0:
                    g = [
                        g_vm[pl.ds(DOWN + (p // 2 * 2 + j) * 512 + p % 2 * size + first, tile), :]
                        for j in range(2)
                    ]
                elif i == 1:
                    g = [g_vm[pl.ds(UP + j * 512 + p * size + first, tile), :] for j in range(4)]
                elif i == 2:
                    g = [g_vm[pl.ds(OUT + j * 256 + p * size + first, tile), :] for j in range(2)]
                else:
                    g = None
                    for part in range(3):
                        own = g_vm[pl.ds(IN + part * 512 + p * size + first, tile), :]
                        term = nn(own, spreads[part])
                        g = term if g is None else g + term
                if i < 3:
                    g = jnp.concatenate(g, axis=1).astype(f32)
                w, m, v = adam_tile(bw[rs, :], bm[rs, :], bv[rs, :], g, rate, 0.05)
                bw[rs, :] = w
                bm[rs, :] = m
                bv[rs, :] = v
                low[rs, :] = w.astype(bf16)

            tile_loop(size, tile, body)
            rs = pl.ds(p * size, size)
            for j, src in enumerate((bw, bm, bv, low)):
                go = pltpu.make_async_copy(
                    src.at[rs, :], outs[4 * i + j].at[rs, :], out_sem.at[i, p, j]
                )
                go.start()
                stores.append(go)
        if i == 0:
            for come, go in zip(passing, moves):
                come.wait()
                go.start()
    x = lax.axis_index("tensor")
    mine = pl.ds(pl.multiple_of(x * 256, 256), 256)
    g_small = small_sum[:, mine]
    both = small_sum[16:20, :]
    first = jnp.where(x == 0, 1.0, 0.0)
    g_bias = jnp.concatenate(
        [
            (both[j : j + 1, :] * first + both[2 + j : 3 + j, :] * (1.0 - first))
            for j in range(2)
        ],
        axis=1,
    )
    for i, (g, rate, decay) in enumerate(
        ((g_small[0:9], 2.0, 0.05), (g_bias, 0.3, 0.0), (g_small[9:16], 0.3, 0.0))
    ):
        w = smalls[3 * i][...] if i < 2 else smalls[6][:, mine]
        new = adam(w, smalls[3 * i + 1][...], smalls[3 * i + 2][...], g, rate, decay)
        for j in range(3):
            small_outs[3 * i + j][...] = new[j]
    for go in stores + moves:
        go.wait()


def adam_step(full, small_sum, raw_out, raw_gin, mats, smalls):
    S = jax.ShapeDtypeStruct
    V = pltpu.VMEM
    mat_shapes = [shape[:2] for shape in MATRICES]
    any_spec = pl.BlockSpec(memory_space=pl.ANY)
    vmem_spec = pl.BlockSpec(memory_space=V)
    small_shapes = [(9, 256)] * 3 + [(1, 1024)] * 3 + [(7, 256)] * 3
    return pl.pallas_call(
        adam_kernel,
        out_shape=tuple(
            S(shape, kind) for shape in mat_shapes for kind in (f32, f32, f32, bf16)
        )
        + tuple(S(shape, f32) for shape in small_shapes)
        + (S(raw_out.shape, bf16), S(raw_gin.shape, f32)),
        in_specs=[any_spec, vmem_spec, any_spec, any_spec] + [any_spec] * 12 + [vmem_spec] * 9,
        out_specs=[any_spec] * 16 + [vmem_spec] * 9 + [any_spec] * 2,
        scratch_shapes=[V(shape, f32) for shape in mat_shapes for _ in range(3)]
        + [V(shape, bf16) for shape in mat_shapes]
        + [
            V((GROWS, 256), bf16),
            V(raw_out.shape, bf16),
            V(raw_gin.shape, f32),
            pltpu.SemaphoreType.DMA((4, 4, 3)),
            pltpu.SemaphoreType.DMA((4, 4, 4)),
            pltpu.SemaphoreType.DMA((5,)),
        ],
        compiler_params=pltpu.CompilerParams(vmem_limit_bytes=62 * 1024 * 1024),
    )(full, small_sum, raw_out, raw_gin, *mats, *smalls)


CHUNKS = (
    (0, 1024),
    (2048, 1024),
    (1024, 1024),
    (3072, 1024),
    (4096, 512),
    (5632, 512),
    (5120, 512),
    (4608, 512),
)
LATE = 5
SLOTS = 12
PLAN = {
    'U0': ((0, 0),),
    'f0': ((1, 0),),
    'f3': ((0, 1),),
    'D1': ((1, 1), (2, 0),),
    'd0': ((3, 0), (2, 1),),
    'd1': ((3, 1),),
    'd2': ((0, 2),),
    'r0': ((4, 0),),
    'r1': ((1, 2), (0, 3), (4, 1),),
    'r6': ((2, 2), (1, 3), (0, 4),),
    'A1': ((5, 0),),
    'A0': ((6, 0),),
    'r8': ((7, 0), (5, 1), (6, 1), (3, 2), (2, 3),),
    'r9': ((7, 1), (4, 2), (1, 4),),
    'r10': ((0, 5),),
    'r12': ((3, 3),),
    'r13': ((4, 3), (2, 4),),
    'r15': ((1, 5), (0, 6),),
    'B1': ((5, 2),),
    'B0': ((6, 2), (3, 4), (7, 2), (5, 3), (4, 4), (0, 7), (6, 3),),
    's0': ((7, 3), (1, 6),),
    's1': ((2, 5), (5, 4), (1, 7),),
    's2': ((6, 4),),
    's3': ((3, 5), (7, 4),),
    'N': ((4, 5),),
    'R': ((5, 5),),
}
TAIL = (
    (2, 6), (6, 5), (2, 7), (7, 5), (3, 6), (4, 6),
    (3, 7), (5, 6), (4, 7), (6, 6), (7, 6), (5, 7),
    (5, 8), (6, 7), (6, 8), (7, 7), (7, 8),
)


ITEMS = ((0, 0, 64), (0, 64, 64), (1, 0, 64), (2, 0, 64), (2, 64, 64), (3, 0, 128), (3, 128, 128))


class Traffic:
    def __init__(self, images, refs):
        (self.tok, self.cot, self.w_in, self.w_out, self.w_up, self.w_down, self.taps, self.bias,
         self.out, self.gin, self.full, self.small_sum,
         self.gin_v, self.grads, self.gsmall, self.wi, self.wo, self.wu, self.wd, self.small,
         self.at_s, self.af_s, self.da_s, self.gp_s, self.mf_s, self.nb_s, self.lb_s, self.out_v,
         self.cores, self.xs, self.ys, self.zs, self.firsts,
         self.small_in, self.small_z, self.send, self.recv, self.ssend, self.srecv,
         self.wsend, self.wrecv, self.load, self.save) = refs
        self.images = images
        dp, x = lax.axis_index("dp"), lax.axis_index("tensor")
        core, y, z = lax.rem(dp, 2), lax.rem(dp // 2, 2), dp // 4

        def at(zz, yy, cc, xx):
            return ((zz * 2 + yy) * 2 + cc, xx)

        self.x, self.core, self.y, self.z = x, core, y, z
        self.core_mate = at(z, y, 1 - core, x)
        self.x_mate = at(z, y, core, 1 - x)
        self.y_mate = at(z, 1 - y, core, x)
        self.z_others = [lax.rem(z + k, 4) for k in range(1, 4)]
        self.z_mates = [at(o, y, core, x) for o in self.z_others]
        quarter = y * 2 + core
        self.quarter = quarter

        def load(i, src, dst):
            return pltpu.make_async_copy(src, dst, self.load.at[i])

        w_in, w_out, w_up, w_down = self.w_in, self.w_out, self.w_up, self.w_down
        at_s, af_s, da_s, mf_s, gin = self.at_s, self.af_s, self.da_s, self.mf_s, self.gin_v
        q_in, q_out = aligned(quarter * 128, 128), aligned(quarter * 64, 64)
        q_down = aligned(quarter * 256, 256)
        self.early = [
            load(0, w_in.at[q_in, 0:256], at_s.at[0:128, 0:256]),
            load(1, w_in.at[q_in, 256:512], at_s.at[0:128, 256:512]),
            load(2, w_in.at[q_in, 512:768], at_s.at[128:256, 0:256]),
            load(3, w_out.at[q_out, :], at_s.at[256:320, :]),
            load(4, w_up.at[q_in, 0:512], at_s.at[320:448, :]),
            load(5, w_up.at[q_in, 512:1024], at_s.at[448:576, :]),
            load(6, w_down.at[q_down, :], at_s.at[576:832, :]),
        ]
        self.own_in = [
            load(7, w_in.at[:, 0:256], mf_s.at[0, 0:512, :]),
            load(8, w_in.at[:, 256:512], mf_s.at[1, 0:512, :]),
            load(9, w_in.at[:, 512:768], gin.at[0:512, 0:256]),
        ]
        self.tok_load = load(10, self.tok, self.nb_s.at[0 : images * WIN, :])
        self.cot_load = load(11, self.cot, self.lb_s.at[0 : images * WIN, :])
        self.own_rest = [
            load(12, w_out.at[:, 0:256], gin.at[0:256, 256:512]),
            load(13, w_out.at[:, 256:512], gin.at[256:512, 256:512]),
            load(14, w_up.at[:, 0:512], da_s.at[0:512, :]),
            load(15, w_up.at[:, 512:1024], af_s.at[0:512, :]),
            load(16, w_down.at[0:256, :], da_s.at[512:768, :]),
            load(17, w_down.at[256:512, :], af_s.at[512:768, :]),
            load(18, w_down.at[512:768, :], gin.at[512:768, :]),
            load(19, w_down.at[768:896, :], da_s.at[768:896, :]),
            load(20, w_down.at[896:1024, :], af_s.at[768:896, :]),
        ]


    def weight_copy(self, src, dst, item, slot, mate):
        return pltpu.make_async_remote_copy(
            src_ref=src,
            dst_ref=dst,
            send_sem=self.wsend.at[item, slot],
            recv_sem=self.wrecv.at[item, slot],
            device_id=mate,
            device_id_type=MESH,
        )

    def view(self, item, half, yy, cc):
        kind, first, size = ITEMS[item]
        quarter = yy * 2 + cc
        if kind == 0:
            return self.wi.at[half, :, aligned(quarter * 128 + first, size), :]
        ref, rows = ((self.wo, 64), (self.wu, 128), (self.wd, 256))[kind - 1]
        return ref.at[half, aligned(quarter * rows + first, size), :]

    def crossing(self, item):
        if item == len(ITEMS):
            own = self.small.at[self.x]
        else:
            own = self.view(item, self.x, self.y, self.core)
        return self.weight_copy(own, own, item, 0, self.x_mate)

    def inward(self, item):
        got = self.view(item, 1 - self.x, self.y, self.core)
        return self.weight_copy(got, got, item, 1, self.core_mate)

    def aside(self, item):
        got = self.view(item, 1 - self.x, self.y, self.core)
        return self.weight_copy(got, got, item, 2, self.y_mate)

    def onward(self, item):
        got = self.view(item, 1 - self.x, 1 - self.y, self.core)
        return self.weight_copy(got, got, item, 3, self.core_mate)

    def permuted(self, pieces, rows):
        low = jnp.concatenate(pieces, axis=1).astype(bf16)
        for part in range(3):
            for j in range(2):
                four = nn(low[:, j * 384 : (j + 1) * 384], spread_four(part))
                self.wi[self.x, part, rows, j * 128 : (j + 1) * 128] = four.astype(bf16)

    def begin(self):
        for go in self.early[0:3]:
            go.start()
        barrier = pltpu.get_barrier_semaphore()
        for mate in (self.core_mate, self.x_mate, self.y_mate, *self.z_mates):
            pl.semaphore_signal(barrier, inc=1, device_id=mate, device_id_type=MESH)
        for go in self.early[3:]:
            go.start()
        self.tok_load.start()
        for go in self.own_in:
            go.start()
        x, quarter, at_s = self.x, self.quarter, self.at_s
        self.small[x, 0:9, :] = self.taps[...]
        for j in range(4):
            self.small[x, 9 + j : 10 + j, :] = self.bias[:, j * 256 : (j + 1) * 256]
        for go in self.early[0:3]:
            go.wait()
        self.permuted(
            [at_s[0:128, 0:256], at_s[0:128, 256:512], at_s[128:256, 0:256]],
            aligned(quarter * 128, 128),
        )
        pl.semaphore_wait(barrier, 6)
        self.crossing(0).start()
        self.crossing(1).start()
        self.crossing(len(ITEMS)).start()
        self.early[3].wait()
        self.wo[x, aligned(quarter * 64, 64), :] = at_s[256:320, :].astype(bf16)
        self.crossing(2).start()
        for go in self.early[4:6]:
            go.wait()
        rows = aligned(quarter * 128, 128)
        self.wu[x, rows, 0:512] = at_s[320:448, :].astype(bf16)
        self.wu[x, rows, 512:1024] = at_s[448:576, :].astype(bf16)
        self.crossing(3).start()
        self.crossing(4).start()
        self.early[6].wait()
        self.wd[x, aligned(quarter * 256, 256), :] = at_s[576:832, :].astype(bf16)
        self.crossing(5).start()
        self.crossing(6).start()
        self.cot_load.start()
        for go in self.own_rest:
            go.start()

    def tokens(self):
        self.tok_load.wait()

    def others(self, body):
        for j in range(4):

            @pl.when(self.quarter != j)
            def _(j=j):
                body(j)

    def weights(self):
        for go in self.own_in:
            go.wait()
        mf_s, gin = self.mf_s, self.gin_v

        def body(j):
            rows = slice(j * 128, (j + 1) * 128)
            self.permuted([mf_s[0, rows, :], mf_s[1, rows, :], gin[rows, 0:256]], rows)

        self.others(body)

    def passed(self, *items):
        for item in items:
            self.crossing(item).wait()
            self.inward(item).start()
            self.aside(item).start()

    def turned(self, *items):
        for item in items:
            self.aside(item).wait()
            self.onward(item).start()

    def done(self, *items):
        for item in items:
            self.inward(item).wait()
            self.onward(item).wait()

    def fore(self, i):
        last = self.images - 1
        for k, steps in {
            0: (("passed", 0), ("passed", 1)),
            1: (("turned", 0), ("passed", 2)),
            2: (("turned", 1),),
            last: (("done", 0), ("done", 1), ("passed", 3)),
            last + 1: (("turned", 2), ("passed", 4)),
            last + 2: (("turned", 3),),
            last + 3: (("passed", 5),),
            last + 4: (("turned", 4), ("passed", 6)),
        }.items():

            @pl.when(i == k)
            def _(k=k, steps=steps):
                for name, item in steps:
                    {"passed": self.passed, "turned": self.turned, "done": self.done}[name](item)
                if k == last:
                    self.crossing(len(ITEMS)).wait()

    def cotangent(self):
        self.done(2)
        for go in self.own_rest:
            go.wait()
        x, gin, da_s, af_s = self.x, self.gin_v, self.da_s, self.af_s

        def body(j):
            rows = slice(j * 64, (j + 1) * 64)
            self.wo[x, rows, 0:256] = gin[rows, 256:512].astype(bf16)
            self.wo[x, rows, 256:512] = gin[j * 64 + 256 : (j + 1) * 64 + 256, 256:512].astype(bf16)
            rows = slice(j * 128, (j + 1) * 128)
            self.wu[x, rows, 0:512] = da_s[rows, :].astype(bf16)
            self.wu[x, rows, 512:1024] = af_s[rows, :].astype(bf16)
            rows = slice(j * 256, (j + 1) * 256)
            if j < 3:
                self.wd[x, rows, :] = (da_s, af_s, gin)[j][512:768, :].astype(bf16)
            else:
                self.wd[x, 768:896, :] = da_s[768:896, :].astype(bf16)
                self.wd[x, 896:1024, :] = af_s[768:896, :].astype(bf16)

        self.others(body)
        self.cot_load.wait()

    def near(self):
        self.turned(5, 6)

    def arrived(self):
        self.done(3, 4, 5, 6)


    def output(self):
        self.out_v[...] = self.gin_v[...].astype(bf16)
        self.saving(0).start()

    def saving(self, i):
        src, dst = (
            (self.out_v, self.out),
            (self.gin_v, self.gin),
        )[i]
        return pltpu.make_async_copy(src, dst, self.save.at[i])

    def finished(self):
        self.saving(1).start()

    def keeping(self, c):
        base, R = CHUNKS[c]
        rows = pl.ds(base, R)
        return pltpu.make_async_copy(
            self.grads.at[0, rows, :], self.full.at[rows, :], self.save.at[2 + c]
        )


    def copy(self, src, dst, chunk, slot, mate):
        return pltpu.make_async_remote_copy(
            src_ref=src,
            dst_ref=dst,
            send_sem=self.send.at[chunk, slot],
            recv_sem=self.recv.at[chunk, slot],
            device_id=mate,
            device_id_type=MESH,
        )

    def flights(self, c, s):
        base, R = CHUNKS[c]
        half, quarter, piece = R // 2, R // 4, R // 16
        x, y, z, core, grads = self.x, self.y, self.z, self.core, self.grads
        mine = base + core * half
        theirs = aligned(base + (1 - core) * half, half)
        if c >= LATE:
            if s == 0:
                src = grads.at[1 - x, theirs, :]
                return [self.copy(src, self.firsts[c - LATE], c, 11, self.core_mate)]
            if s == 1:
                return [self.copy(self.firsts[c - LATE], self.xs[c], c, 1, self.x_mate)]
            if s == 2:
                return [self.copy(grads.at[x, theirs, :], self.cores[c], c, 0, self.core_mate)]
            s -= 1
        else:
            if s == 0:
                return [self.copy(grads.at[:, theirs, :], self.cores[c], c, 0, self.core_mate)]
            if s == 1:
                return [self.copy(self.cores[c].at[1 - x], self.xs[c], c, 1, self.x_mate)]
        if s == 2:
            src = self.xs[c].at[aligned((1 - y) * quarter, quarter), :]
            return [self.copy(src, self.ys[c], c, 2, self.y_mate)]
        if s == 3:
            return [
                self.copy(
                    self.ys[c].at[aligned(self.z_others[k] * piece, piece), :],
                    self.zs[c].at[k],
                    c,
                    3 + k,
                    self.z_mates[k],
                )
                for k in range(3)
            ]
        if s == 4:
            own = grads.at[0, aligned(mine + y * quarter + z * piece, piece), :]
            return [self.copy(own, own, c, 6 + k, self.z_mates[k]) for k in range(3)]
        if s == 5:
            own = grads.at[0, aligned(mine + y * quarter, quarter), :]
            return [self.copy(own, own, c, 9, self.y_mate)]
        if s == 6:
            own = grads.at[0, aligned(mine, half), :]
            return [self.copy(own, own, c, 10, self.core_mate)]
        return []

    def stage(self, c, s):
        base, R = CHUNKS[c]
        half, quarter, piece = R // 2, R // 4, R // 16
        x, y, z, core, grads = self.x, self.y, self.z, self.core, self.grads
        mine = base + core * half
        late = c >= LATE
        if s > 0 and not (late and s == 2):
            for flight in self.flights(c, s - 1):
                flight.wait()
        if late and s == 3:
            self.flights(c, 1)[0].wait()

        def total(*parts):
            out = None
            for part in parts:
                part = part.astype(f32)
                out = part if out is None else out + part
            return out.astype(bf16)

        cores, xs, ys, zs = self.cores[c], self.xs[c], self.ys[c], self.zs[c]
        step = s - 1 if late else s
        if late and s == 1:
            first = self.firsts[c - LATE]

            def body(i, size):
                rows, own = pl.ds(i, size), aligned(mine + i, size)
                first[rows, :] = total(grads[1 - x, own, :], first[rows, :])

            tile_loop(half, 128, body)
        elif late and s == 3:

            def body(i, size):
                rows, own = pl.ds(i, size), aligned(mine + i, size)
                xs[rows, :] = total(grads[x, own, :], cores[rows, :], xs[rows, :])

            tile_loop(half, 128, body)
        elif not late and s == 1:

            def body(i, size):
                rows, own = pl.ds(i, size), aligned(mine + i, size)
                for t in range(2):
                    cores[t, rows, :] = total(grads[t, own, :], cores[t, rows, :])

            tile_loop(half, 128, body)
        elif not late and s == 2:

            def body(i, size):
                rows = pl.ds(i, size)
                xs[rows, :] = total(cores[x, rows, :], xs[rows, :])

            tile_loop(half, 128, body)
        elif step == 3:

            def body(i, size):
                rows, own = pl.ds(i, size), aligned(y * quarter + i, size)
                ys[rows, :] = total(xs[own, :], ys[rows, :])

            tile_loop(quarter, 128, body)
        elif step == 4:
            own = aligned(z * piece, piece)
            grads[0, aligned(mine + y * quarter + z * piece, piece), :] = total(
                ys[own, :], zs[0], zs[1], zs[2]
            )
        if step == 7:
            self.keeping(c).start()
        for flight in self.flights(c, s):
            flight.start()

    def small_flights(self, s):
        def small_copy(src, dst, slot, mate):
            return pltpu.make_async_remote_copy(
                src_ref=src,
                dst_ref=dst,
                send_sem=self.ssend.at[slot],
                recv_sem=self.srecv.at[slot],
                device_id=mate,
                device_id_type=MESH,
            )

        if s < 3:
            mate = (self.core_mate, self.x_mate, self.y_mate)[s]
            return [small_copy(self.small_z.at[s], self.small_in.at[s], s, mate)]
        return [
            small_copy(self.small_z.at[3], self.small_z.at[4 + self.z], 3 + k, self.z_mates[k])
            for k in range(3)
        ]

    def small_stage(self, s):
        small_z = self.small_z
        if s > 0:
            for flight in self.small_flights(s - 1):
                flight.wait()
        if s == 0:
            small_z[0] = self.gsmall[...]
        elif s <= 3:
            small_z[s] = small_z[s - 1] + self.small_in[s - 1]
        else:
            self.small_sum[...] = (small_z[4] + small_z[5]) + (small_z[6] + small_z[7])
            return
        if s == 3:
            small_z[4 + self.z] = small_z[3]
        for flight in self.small_flights(s):
            flight.start()

    def point(self, name):
        for c, s in PLAN.get(name, ()):
            self.stage(c, s)

    def turn(self, name, n, stride=1, offset=0):
        for j in range(self.images):
            key = name + str(j * stride + offset)
            if key in PLAN:

                @pl.when(n == j)
                def _(key=key):
                    self.point(key)

    def sums(self, k):
        self.small_stage(k)

    def end(self):
        self.small_stage(2)
        for k, (c, s) in enumerate(TAIL):
            self.stage(c, s)
            if k == len(TAIL) // 3:
                self.small_stage(3)
        self.small_stage(4)
        for i in range(2):
            self.saving(i).wait()
        for c in range(len(CHUNKS)):
            self.keeping(c).wait()


def main_kernel(images, counts, tok, cot, w_in, w_out, w_up, w_down, taps, bias, vecs,
                out, gin, full, small_sum, *scratch):
    n = len(block_scratch(images))
    inner, rest = scratch[:n], scratch[n:]
    gin_v, grads, gsmall, wi, wo, wu, wd, small = rest[:8]
    rest = rest[8:]
    count = len(CHUNKS)
    cores, xs, ys, zs = (rest[count * i : count * (i + 1)] for i in range(4))
    rest = rest[4 * count :]
    firsts, rest = rest[: count - LATE], rest[count - LATE :]
    x_s, co_s, at_s, af_s, da_s, gp_s, mf_s, na_s, nb_s, lb_s = inner[:10]
    traffic = Traffic(
        images,
        (tok, cot, w_in, w_out, w_up, w_down, taps, bias, out, gin, full, small_sum,
         gin_v, grads, gsmall, wi, wo, wu, wd, small,
         at_s, af_s, da_s, gp_s, mf_s, nb_s, lb_s, co_s.at[0 : images * WIN, :],
         cores, xs, ys, zs, firsts, *rest),
    )
    x = lax.axis_index("tensor")
    limit = counts[lax.axis_index("dp")] - x * images
    traffic.begin()
    block_body(
        images, limit, x, traffic, wi, wo, wu, wd, small, vecs, gin_v, grads, gsmall, *inner
    )
    traffic.end()


def main_call(counts, tok, cot, w_in, w_out, w_up, w_down, taps, bias, vecs):
    images = tok.shape[0] // WIN
    S = jax.ShapeDtypeStruct
    V = pltpu.VMEM
    away = pl.BlockSpec(memory_space=pl.ANY)
    here = pl.BlockSpec(memory_space=V)
    sizes = [R for _, R in CHUNKS]
    dma = pltpu.SemaphoreType.DMA
    return pl.pallas_call(
        functools.partial(main_kernel, images),
        out_shape=(
            S(tok.shape, bf16),
            S(tok.shape, f32),
            S((GROWS, 256), bf16),
            S((24, D), f32),
        ),
        in_specs=[pl.BlockSpec(memory_space=pltpu.SMEM)] + [away] * 6 + [here] * 3,
        out_specs=[away] * 3 + [here],
        scratch_shapes=block_scratch(images)
        + [
            V(tok.shape, f32),
            V((2, GROWS, 256), bf16),
            V((24, D), f32),
            V((2, 3, D, 256), bf16),
            V((2, 256, D), bf16),
            V((2, D, 1024), bf16),
            V((2, 1024, D), bf16),
            V((2, 16, 256), f32),
        ]
        + [V((2, R // 2, 256), bf16) for R in sizes[:LATE]]
        + [V((R // 2, 256), bf16) for R in sizes[LATE:]]
        + [V((R // 2, 256), bf16) for R in sizes]
        + [V((R // 4, 256), bf16) for R in sizes]
        + [V((3, R // 16, 256), bf16) for R in sizes]
        + [V((R // 2, 256), bf16) for R in sizes[LATE:]]
        + [
            V((3, 24, D), f32),
            V((8, 24, D), f32),
            dma((len(sizes), SLOTS)),
            dma((len(sizes), SLOTS)),
            dma((6,)),
            dma((6,)),
            dma((8, 4)),
            dma((8, 4)),
            dma((21,)),
            dma((2 + len(sizes),)),
        ],
        compiler_params=pltpu.CompilerParams(
            collective_id=1, has_side_effects=True, vmem_limit_bytes=63 * 1024 * 1024
        ),
    )(counts, tok, cot, w_in, w_out, w_up, w_down, taps, bias, vecs)


def local(
    tokens, cotangent, image_counts,
    w_in, m_in, v_in, w_out, m_out, v_out, w_up, m_up, v_up, w_down, m_down, v_down,
    kernel, m_kernel, v_kernel, up_bias, m_bias, v_bias, vectors, m_vectors, v_vectors,
):
    biases = tuple(a.reshape(1, -1) for a in (up_bias, m_bias, v_bias))
    raw_out, raw_gin, full, small_sum = main_call(
        image_counts, tokens, cotangent, w_in, w_out, w_up, w_down, kernel, biases[0], vectors
    )
    new = adam_step(
        full,
        small_sum,
        raw_out,
        raw_gin,
        (w_down, m_down, v_down, w_up, m_up, v_up, w_out, m_out, v_out, w_in, m_in, v_in),
        (kernel, m_kernel, v_kernel)
        + biases
        + (vectors, m_vectors, v_vectors),
    )
    down, up, mid, first = new[:4], new[4:8], new[8:12], new[12:16]
    bias = tuple(a.reshape(-1) for a in new[19:22])
    return (*new[25:27], *first, *mid, *up, *down, *new[16:19], *bias, *new[22:25])


def general(
    tokens, cotangent, image_counts,
    w_in, m_in, v_in, w_out, m_out, v_out, w_up, m_up, v_up, w_down, m_down, v_down,
    kernel, m_kernel, v_kernel, up_bias, m_bias, v_bias, vectors, m_vectors, v_vectors,
):
    images = tokens.shape[0] // WIN
    place = lax.axis_index("tensor")
    live = image_counts[lax.axis_index("dp")] - place * images

    def whole(a, axis):
        return lax.all_gather(a, "tensor", axis=axis, tiled=True)

    wi = whole(w_in.astype(bf16), 1).reshape(D, 2, 8, 3, HD).transpose(1, 3, 0, 2, 4)
    wi = wi.reshape(2, 3, D, 256)
    wo = whole(w_out.astype(bf16), 0).reshape(2, 256, D)
    wd = whole(w_down.astype(bf16), 0).reshape(2, 1024, D)
    wu = whole(w_up.astype(bf16), 1).reshape(D, 2, 1024).transpose(1, 0, 2)
    small = jnp.concatenate(
        [
            whole(kernel, 1).reshape(9, 2, 256).transpose(1, 0, 2),
            whole(up_bias, 0).reshape(2, 4, 256),
            jnp.zeros((2, 3, 256), f32),
        ],
        axis=1,
    )
    out, grad_in, grads, gs = block(
        live.reshape(1), tokens, cotangent, wi, wo, wu, wd, small, vectors
    )
    grads = grads.astype(f32)

    def columns(first, rows, count):
        part = grads[:, first : first + rows * count].reshape(2, count, rows, 256)
        return part

    g_down = grads[:, DOWN:UP].reshape(2, 2, 2, 512, 256).transpose(0, 1, 3, 2, 4).reshape(FF, D)
    g_up = columns(UP, 512, 4).transpose(2, 0, 1, 3).reshape(D, FF)
    g_out = columns(OUT, 256, 2).transpose(0, 2, 1, 3).reshape(D, D)
    g_in = columns(IN, 512, 3).reshape(2, 3, D, 8, HD).transpose(2, 0, 3, 1, 4).reshape(D, 3 * D)

    def owned(a, axis):
        return lax.psum(lax.psum_scatter(a, "tensor", scatter_dimension=axis, tiled=True), "dp")

    g_in, g_out, g_up, g_down = owned(g_in, 1), owned(g_out, 0), owned(g_up, 1), owned(g_down, 0)
    g_kernel, g_bias, g_vectors = owned(gs[0:9], 1), owned(gs[16:20].reshape(-1), 0), owned(gs[9:16], 1)
    vector_width = m_vectors.shape[1]
    own_vectors = lax.dynamic_slice_in_dim(vectors, place * vector_width, vector_width, 1)
    results = [out, grad_in]
    for w, m, v, g, rate in (
        (w_in, m_in, v_in, g_in, D**-0.5),
        (w_out, m_out, v_out, g_out, (D // HD) ** -0.5),
        (w_up, m_up, v_up, g_up, D**-0.5),
        (w_down, m_down, v_down, g_down, FF**-0.5),
    ):
        new = adam(w, m, v, g, rate, 0.05)
        results += [*new, new[0].astype(bf16)]
    results += adam(kernel, m_kernel, v_kernel, g_kernel, 2.0, 0.05)
    results += adam(up_bias, m_bias, v_bias, g_bias, 0.3, 0.0)
    results += adam(own_vectors, m_vectors, v_vectors, g_vectors, 0.3, 0.0)
    return tuple(results)


def solution(mesh):
    rows, columns = P("tensor", None), P(None, "tensor")
    tokens = P(("dp", "tensor"), None)
    mats = (columns,) * 3 + (rows,) * 3 + (columns,) * 3 + (rows,) * 3
    news = (columns,) * 4 + (rows,) * 4 + (columns,) * 4 + (rows,) * 4
    pairs = mesh.shape["dp"] == 16 and mesh.shape["tensor"] == 2
    return jax.shard_map(
        local if pairs else general,
        mesh=mesh,
        in_specs=(tokens, tokens, P(), *mats)
        + (columns,) * 3
        + (P("tensor"),) * 3
        + (P(), columns, columns),
        out_specs=(tokens, tokens, *news) + (columns,) * 3 + (P("tensor"),) * 3 + (columns,) * 3,
        check_vma=False,
    )
```

```python
import functools
import jax
import jax.numpy as jnp
from jax import lax
from jax.experimental import pallas as pl
from jax.experimental.pallas import tpu as pltpu
from jax.sharding import PartitionSpec as P

D = 512
HD = 32
FF = 2048
SIDE = 14
WIDE = 16
WIN = SIDE * SIDE
ROWS = SIDE * WIDE
KEYS = 256
GROUPS = D // 128
STEP = 5
DOWN, UP, OUT, IN, GROWS = 0, 2048, 4096, 4608, 6144
MESH = pl.DeviceIdType.MESH
eps = 1e-05
f32 = jnp.float32
bf16 = jnp.bfloat16
C0 = 0.7978845608028654
C1 = 0.044715


def nn(a, b):
    return lax.dot_general(a, b, (((1,), (0,)), ((), ())), preferred_element_type=f32)


def nt(a, b):
    return lax.dot_general(a, b, (((1,), (1,)), ((), ())), preferred_element_type=f32)


def tn(a, b):
    return lax.dot_general(a, b, (((0,), (0,)), ((), ())), preferred_element_type=f32)


def normed(x):
    c = x - jnp.mean(x, axis=-1, keepdims=True)
    r = lax.rsqrt(jnp.mean(c * c, axis=-1, keepdims=True) + eps)
    return c * r, r


def norm_back(u, xhat, r):
    return r * (
        u
        - jnp.mean(u, axis=-1, keepdims=True)
        - xhat * jnp.mean(u * xhat, axis=-1, keepdims=True)
    )


def gelu_pair(x):
    x2 = x * x
    t = 0.5 * jnp.tanh(x * (C0 + (C0 * C1) * x2))
    h = 0.5 + t
    value = x * h
    return value, h + value * ((0.5 - t) * (2.0 * C0 + (6.0 * C0 * C1) * x2))


def gelu(x):
    return x * (0.5 + 0.5 * jnp.tanh(x * (C0 + (C0 * C1) * (x * x))))


def row_sum(x):
    return jnp.sum(x, axis=0, keepdims=True)


def shift_rows(x, by):
    z = jnp.zeros((abs(by), x.shape[1]), x.dtype)
    if by > 0:
        return jnp.concatenate([z, x[:-by]], axis=0)
    return jnp.concatenate([x[-by:], z], axis=0)


def roll1(x, by):
    return pltpu.roll(x, by % x.shape[0], 0)


def pool(c):
    s = c + roll1(c, 1) + roll1(c, -1)
    return s + shift_rows(s, WIDE) + shift_rows(s, -WIDE)


def block_body(images, limit, first_half, hooks, wi, wo, wu, wd, small, vecs,
               gin, grads, gsmall,
               x_s, co_s, at_s, af_s, da_s, gp_s, mf_s, na_s, nb_s, lb_s, la_s, mx_s,
               q_s, k_s, v_s, dm_s, hd_s, dp_s, pj_s, p_s, taps_s, ds_s):
    gain_a, shift_a, gain_b, shift_b, scale_a, scale_f, bias_f = (
        vecs[i : i + 1, :] for i in range(7)
    )
    gsmall[...] = jnp.zeros_like(gsmall)
    gtaps = taps_s
    gtaps[...] = jnp.zeros_like(gtaps)
    blank = jnp.zeros((KEYS - ROWS, 256), bf16)
    for ref in (q_s, k_s, v_s, dm_s):
        for t in range(2):
            for n in range(images):
                ref[t, n * KEYS + ROWS : (n + 1) * KEYS, :] = blank

    cell = lax.broadcasted_iota(jnp.int32, (ROWS, 1), 0)
    inside = lax.rem(cell, WIDE) < SIDE
    lane = lax.broadcasted_iota(jnp.int32, (1, 128), 1)
    head_masks = [(lane // HD) == h for h in range(4)]
    key_row = lax.broadcasted_iota(jnp.int32, (KEYS, 128), 0)
    key_lane = lax.broadcasted_iota(jnp.int32, (KEYS, 128), 1)
    key_pad = (lax.rem(key_row, WIDE) >= SIDE) | (key_row >= ROWS)
    key_block = jnp.where(key_pad & (key_lane == 0), -1e30, 0.0).astype(bf16)
    one_block = jnp.where(key_lane == 0, 1.0, 0.0).astype(bf16)

    def padded(n):
        return pl.ds(pl.multiple_of(n * ROWS, WIDE), ROWS)

    def held(n):
        return pl.ds(pl.multiple_of(n * KEYS, WIDE), ROWS)

    def whole(n):
        return pl.ds(pl.multiple_of(n * KEYS, WIDE), KEYS)

    def masked(h, a):
        return jnp.where(head_masks[h], a, jnp.zeros_like(a))

    def prepare(n, carry):
        rows = padded(n)
        xhat, _ = normed(x_s[rows, :].astype(f32))
        na_s[rows, :] = (xhat * gain_a + shift_a).astype(bf16)
        return carry

    def tap(t, i, ls):
        return small[t, pl.ds(i, 1), ls]

    def attend(t, n):
        rows = padded(n)
        na = na_s[rows, :]
        k_s[t, held(n), :] = nn(na, wi[t, 1]).astype(bf16)
        v_s[t, held(n), :] = nn(na, wi[t, 2]).astype(bf16)
        for g in range(2):
            ls = slice(g * 128, (g + 1) * 128)
            gp = nn(na, wi[t, 0, :, ls])
            gp_s[t, rows, ls] = gp
            field = jnp.where(inside, gelu(gp), 0.0)
            back, ahead = roll1(field, 1), roll1(field, -1)
            conv = None
            for a in range(3):
                part = (
                    tap(t, 3 * a, ls) * back
                    + tap(t, 3 * a + 1, ls) * field
                    + tap(t, 3 * a + 2, ls) * ahead
                )
                if a != 1:
                    part = shift_rows(part, WIDE * (1 - a))
                conv = part if conv is None else conv + part
            pooled = pool(jnp.where(inside, conv, 0.0)) * (HD ** (-0.5) / 9.0)
            q_s[t, held(n), ls] = pooled.astype(bf16)
        for g in range(2):
            ls = slice(g * 128, (g + 1) * 128)
            qa = jnp.concatenate([q_s[t, whole(n), ls], one_block], axis=1)
            kg = k_s[t, whole(n), ls]
            vt = jnp.transpose(v_s[t, whole(n), ls])
            mixed = []
            keys = jnp.concatenate(
                [jnp.concatenate([masked(h, kg), key_block], axis=1) for h in range(4)], axis=0
            )
            scores = nt(keys, qa)
            for h in range(4):
                hs = slice(h * KEYS, (h + 1) * KEYS)
                s = scores[hs]
                e = jnp.exp(s - jnp.max(s, axis=0, keepdims=True))
                p_s[t, n * 2 + g, :, hs] = (e * (1.0 / jnp.sum(e, axis=0, keepdims=True))).astype(bf16)
            for h in range(4):
                p = p_s[t, n * 2 + g, :, h * KEYS : (h + 1) * KEYS]
                mixed.append(nn(vt[h * HD : (h + 1) * HD], p))
            mix = jnp.transpose(jnp.concatenate(mixed, axis=0))[:ROWS]
            mf_s[t, rows, ls] = mix
            mx_s[t, rows, ls] = mix.astype(bf16)

    def finish(n, carry):
        rows = padded(n)
        attn = nn(mx_s[0, rows, :], wo[0]) + nn(mx_s[1, rows, :], wo[1])
        at_s[rows, :] = attn
        after = x_s[rows, :].astype(f32) + scale_a * attn
        af_s[rows, :] = after
        xhat, _ = normed(after)
        nb_s[rows, :] = (xhat * gain_b + shift_b).astype(bf16)
        lb_s[rows, :] = (scale_f * co_s[rows, :].astype(f32)).astype(bf16)
        return carry

    def feed(t, u, n):
        rows = padded(n)
        us = slice(u * 512, (u + 1) * 512)
        cs = pl.ds(pl.multiple_of(t * 1024 + u * 512, 512), 512)
        unit_bias = jnp.concatenate(
            [small[t, 9 + 2 * u + j : 10 + 2 * u + j, :] for j in range(2)], axis=1
        )
        value, slope = gelu_pair(nn(nb_s[rows, :], wu[t, :, us]) + unit_bias)
        hd_s[rows, cs] = value.astype(bf16)
        d_pre = slope * nt(lb_s[rows, :], wd[t, us, :])
        gsmall[pl.ds(16 + 2 * t + u, 1), :] += row_sum(d_pre)
        dp_s[rows, cs] = d_pre.astype(bf16)

    def digest(n, carry):
        rows = padded(n)
        branch = nn(hd_s[rows, 0:1024], wd[0]) + nn(hd_s[rows, 1024:2048], wd[1])
        d_nb = nt(dp_s[rows, 0:1024], wu[0]) + nt(dp_s[rows, 1024:2048], wu[1])
        co = co_s[rows, :].astype(f32)
        after = af_s[rows, :]
        xhat, r = normed(after)
        moved = branch + bias_f
        live = (n < limit).astype(f32)
        af_s[rows, :] = (after + scale_f * moved) * live
        gsmall[14:15, :] += row_sum(co * moved)
        gsmall[15:16, :] += scale_f * row_sum(co)
        gsmall[11:12, :] += row_sum(d_nb * xhat)
        gsmall[12:13, :] += row_sum(d_nb)
        d_after = co + norm_back(gain_b * d_nb, xhat, r)
        da_s[rows, :] = d_after
        gsmall[13:14, :] += row_sum(d_after * at_s[rows, :])
        la = (scale_a * d_after).astype(bf16)
        la_s[rows, :] = la
        for t in range(2):
            dm_s[t, held(n), :] = nt(la, wo[t]).astype(bf16)
        hooks.turn("d", n)
        return carry

    pick_row = lax.broadcasted_iota(jnp.int32, (256, 128), 0)
    pick_lane = lax.broadcasted_iota(jnp.int32, (256, 128), 1)
    pick = jnp.where(
        (lax.rem(pick_row, 128) // HD == lax.rem(pick_lane, 4)) & (pick_lane < 8), 1.0, 0.0
    ).astype(bf16)

    def split(a):
        high = a.astype(bf16)
        return high, (a - high.astype(f32)).astype(bf16)

    def inner_block(a):
        sums = nn(jnp.concatenate(split(a), axis=1), pick)
        high, low = split(sums)
        return jnp.where(lane < 4, high, low)

    blank_rows = jnp.zeros((KEYS - ROWS, 128), bf16)

    minus = [
        jnp.where((lane == h) | (lane == h + 4), -1.0, 0.0).astype(bf16) for h in range(4)
    ]

    def recede(t, n, turn):
        rows = padded(n)
        for g in range(2):
            ls = slice(g * 128, (g + 1) * 128)
            inner = inner_block(dm_s[t, held(n), ls].astype(f32) * mf_s[t, rows, ls])
            dmg = dm_s[t, whole(n), ls]
            left = jnp.concatenate(
                [dmg, jnp.concatenate([inner, blank_rows], axis=0)], axis=1
            )
            qg = q_s[t, whole(n), ls]
            kg = k_s[t, whole(n), ls]
            vg = v_s[t, whole(n), ls]
            kt = jnp.transpose(kg)
            dqs = []
            right = jnp.concatenate(
                [
                    jnp.concatenate([masked(h, vg), jnp.broadcast_to(minus[h], (KEYS, 128))], axis=1)
                    for h in range(4)
                ],
                axis=0,
            )
            d_probs = nt(right, left)
            for h in range(4):
                hs = slice(h * KEYS, (h + 1) * KEYS)
                e = p_s[t, n * 2 + g, :, hs]
                ds_s[:, hs] = (e.astype(f32) * d_probs[hs]).astype(bf16)
            dv = nn(
                p_s[t, n * 2 + g], jnp.concatenate([masked(h, dmg) for h in range(4)], axis=0)
            )
            dk = nn(ds_s[...], jnp.concatenate([masked(h, qg) for h in range(4)], axis=0))
            for h in range(4):
                dqs.append(nn(kt[h * HD : (h + 1) * HD], ds_s[:, h * KEYS : (h + 1) * KEYS]))
            dq = jnp.transpose(jnp.concatenate(dqs, axis=0))[:ROWS]
            pj_s[t, 1, rows, ls] = dk[:ROWS].astype(bf16)
            pj_s[t, 2, rows, ls] = dv[:ROWS].astype(bf16)
            value, slope = gelu_pair(gp_s[t, rows, ls])
            field = jnp.where(inside, value, 0.0)
            d_conv = jnp.where(inside, pool(dq * (HD ** (-0.5) / 9.0)), 0.0)
            shifted = (roll1(field, 1), field, roll1(field, -1))
            d_cols = [None, None, None]
            for a in range(3):
                moved = d_conv if a == 1 else shift_rows(d_conv, WIDE * (a - 1))
                for b in range(3):
                    i = 3 * a + b
                    gtaps[t, i : i + 1, ls] += row_sum(moved * shifted[b])
                    term = tap(t, i, ls) * moved
                    d_cols[b] = term if d_cols[b] is None else d_cols[b] + term
            d_field = roll1(d_cols[0], -1) + d_cols[1] + roll1(d_cols[2], 1)
            pj_s[t, 0, rows, ls] = jnp.where(inside, slope * d_field, 0.0).astype(bf16)
            hooks.turn("r", n, 2, turn + g)

    def rise(n, carry):
        rows = padded(n)
        d_na = None
        for t in range(2):
            for part in range(3):
                term = nt(pj_s[t, part, rows, :], wi[t, part])
                d_na = term if d_na is None else d_na + term
        xhat, r = normed(x_s[rows, :].astype(f32))
        gsmall[9:10, :] += row_sum(d_na * xhat)
        gsmall[10:11, :] += row_sum(d_na)
        da_s[rows, :] += norm_back(gain_a * d_na, xhat, r)
        hooks.turn("s", n)
        return carry

    def narrow_rows(target, source):
        for i in range(images * SIDE):
            target[i * SIDE : (i + 1) * SIDE, :] = source[i * WIDE : i * WIDE + SIDE, :]

    def store_down(u):
        for t in range(2):
            cs = slice((2 * t + u) * 512, (2 * t + u + 1) * 512)
            down = tn(hd_s[:, cs], lb_s[...]).astype(bf16)
            for j in range(2):
                first = DOWN + (2 * u + j) * 512
                grads[t, first : first + 512, :] = down[:, j * 256 : (j + 1) * 256]

    def store_up(u):
        for t in range(2):
            cs = slice((2 * t + u) * 512, (2 * t + u + 1) * 512)
            up = tn(nb_s[...], dp_s[:, cs]).astype(bf16)
            for j in range(2):
                first = UP + (2 * u + j) * 512
                grads[t, first : first + 512, :] = up[:, j * 256 : (j + 1) * 256]

    def store_out():
        for t in range(2):
            g_out = tn(mx_s[t], la_s[...]).astype(bf16)
            for j in range(2):
                first = OUT + j * 256
                grads[t, first : first + 256, :] = g_out[:, j * 256 : (j + 1) * 256]

    def store_in(t, part):
        first = IN + part * 512
        grads[t, first : first + 512, :] = tn(na_s[...], pj_s[t, part]).astype(bf16)

    def widen(source, spares, target, scaled):
        temp = at_s
        temp[0 : images * WIN, :] = source[0 : images * WIN, :].astype(f32)
        for first, width, spare in spares:
            cs = slice(first, first + width)
            pad = jnp.zeros((WIDE - SIDE, width), f32)
            for n in range(images):
                for i in range(n * SIDE, (n + 1) * SIDE):
                    cells = temp[i * SIDE : (i + 1) * SIDE, cs]
                    if scaled:
                        cells = cells * (n < limit).astype(f32)
                    spare[i * WIDE : i * WIDE + SIDE, :] = cells
                    spare[i * WIDE + SIDE : (i + 1) * WIDE, :] = pad
            target[:, cs] = spare[...].astype(bf16)

    loop = lax.fori_loop
    hooks.tokens()
    widen(nb_s, [(t * 256, 256, gp_s.at[t]) for t in range(2)], x_s, False)
    loop(0, images, prepare, 0)
    hooks.weights()
    other_half = 1 - first_half

    def fore(i, carry):
        later = i // images
        attend(first_half + (other_half - first_half) * later, lax.rem(i, images))
        hooks.fore(i)
        return carry

    loop(0, 2 * images, fore, 0)
    hooks.cotangent()
    widen(lb_s, [(0, D, da_s)], co_s, True)
    loop(0, images, finish, 0)
    hooks.near()

    def feed_own(n, carry):
        for u in range(2):
            feed(first_half, u, n)
        return carry

    def feed_first(n, carry):
        feed(other_half, 0, n)
        return carry

    def feed_second(n, carry):
        feed(other_half, 1, n)
        hooks.turn("f", n)
        return carry

    loop(0, images, feed_own, 0)
    hooks.arrived()
    loop(0, images, feed_first, 0)
    store_down(0)
    hooks.point("D0")
    store_up(0)
    hooks.point("U0")
    loop(0, images, feed_second, 0)
    store_down(1)
    hooks.point("D1")
    store_up(1)
    hooks.point("U1")
    loop(0, images, digest, 0)
    store_out()
    hooks.point("O")

    def aft(n, carry):
        recede(other_half, n, 0)
        return carry

    loop(0, images, aft, 0)
    for part in (2, 1, 0):
        store_in(other_half, part)
        hooks.point("A%d" % part)

    def aft2(n, carry):
        recede(first_half, n, 2 * images)
        return carry

    loop(0, images, aft2, 0)
    for part in (2, 1, 0):
        store_in(first_half, part)
        hooks.point("B%d" % part)
    loop(0, images, rise, 0)
    for t in range(2):
        gsmall[0:9, t * 256 : (t + 1) * 256] = gtaps[t, 0:9, :]
    hooks.sums(0)
    narrow_rows(gin, af_s)
    hooks.output()
    hooks.sums(1)
    hooks.point("N")
    narrow_rows(gin, da_s)
    hooks.finished()
    hooks.point("R")


class Quiet:
    def __init__(self, tok, cot, nb_s, lb_s, out, gin):
        self.refs = tok, cot, nb_s, lb_s, out, gin

    def tokens(self):
        tok, cot, nb_s, lb_s, _, _ = self.refs
        rows = tok.shape[0]
        nb_s[0:rows, :] = tok[...]
        lb_s[0:rows, :] = cot[...]

    def output(self):
        _, _, _, _, out, gin = self.refs
        out[...] = gin[...].astype(bf16)

    def point(self, name):
        pass

    def turn(self, name, n, stride=1, offset=0):
        pass

    sums = fore = point

    def weights(self):
        pass

    cotangent = near = arrived = finished = weights


def block_kernel(images, lim, tok, cot, wi, wo, wu, wd, small, vecs, out, gin, grads, gsmall, *scratch):
    quiet = Quiet(tok, cot, scratch[8], scratch[9], out, gin)
    block_body(images, lim[0], 0, quiet, wi, wo, wu, wd, small, vecs, gin, grads, gsmall, *scratch)


def block_scratch(images):
    R = images * ROWS
    K = images * KEYS
    V = pltpu.VMEM
    return (
        [V((R, D), bf16)] * 2
        + [V((R, D), f32)] * 3
        + [V((2, R, 256), f32)] * 2
        + [V((R, D), bf16)] * 4
        + [V((2, R, 256), bf16)]
        + [V((2, K, 256), bf16)] * 4
        + [V((R, FF), bf16)] * 2
        + [
            V((2, 3, R, 256), bf16),
            V((2, images * 2, KEYS, 4 * KEYS), bf16),
            V((2, 16, 256), f32),
            V((KEYS, 4 * KEYS), bf16),
        ]
    )


def block(lim, tok, cot, wi, wo, wu, wd, small, vecs):
    images = tok.shape[0] // WIN
    S = jax.ShapeDtypeStruct
    V = pltpu.VMEM
    return pl.pallas_call(
        functools.partial(block_kernel, images),
        out_shape=(
            S(tok.shape, bf16),
            S(tok.shape, f32),
            S((2, GROWS, 256), bf16),
            S((24, D), f32),
        ),
        in_specs=[pl.BlockSpec(memory_space=pltpu.SMEM)] + [pl.BlockSpec(memory_space=V)] * 8,
        out_specs=[pl.BlockSpec(memory_space=V)] * 4,
        scratch_shapes=block_scratch(images),
        compiler_params=pltpu.CompilerParams(vmem_limit_bytes=62 * 1024 * 1024),
    )(lim, tok, cot, wi, wo, wu, wd, small, vecs)


def tile_loop(rows, size, body):
    if rows <= size:
        body(0, rows)
        return

    def step(i, carry):
        body(pl.multiple_of(i * size, size), size)
        return carry

    lax.fori_loop(0, rows // size, step, 0)


def aligned(first, size):
    return pl.ds(pl.multiple_of(first, 16), size)


def spread_four(part):
    a = lax.broadcasted_iota(jnp.int32, (384, 128), 1)
    b = lax.broadcasted_iota(jnp.int32, (384, 128), 0)
    return jnp.where(b == (a // HD) * (3 * HD) + part * HD + lax.rem(a, HD), 1.0, 0.0).astype(bf16)


def spread(part):
    a = lax.broadcasted_iota(jnp.int32, (256, 768), 0)
    b = lax.broadcasted_iota(jnp.int32, (256, 768), 1)
    return jnp.where(b == (a // HD) * (3 * HD) + part * HD + lax.rem(a, HD), 1.0, 0.0).astype(bf16)


def adam(w, m, v, g, rate, decay):
    half = 0.5 * g
    m = 0.5 * m + half
    v = 0.5 * v + half * g
    scale = 1.0 / (1.0 - 0.5**STEP)
    w = w - ((rate * scale) * m / (jnp.sqrt(v * scale) + 1e-08) + (rate * decay) * w)
    return w, m, v


def adam_tile(w, m, v, g, rate, decay):
    half = 0.5 * g
    m = 0.5 * m + half
    v = 0.5 * v + half * g
    scale = 1.0 / (1.0 - 0.5**STEP)
    seen = v * scale
    below = seen * lax.rsqrt(seen) + 1e-08
    inverse = pl.reciprocal(below, approx=True)
    inverse = inverse * (2.0 - below * inverse)
    w = w - ((rate * scale) * m * inverse + (rate * decay) * w)
    return w, m, v


MATRICES = (
    (1024, 512, FF**-0.5, 4, 64),
    (512, 1024, D**-0.5, 4, 32),
    (256, 512, (D // HD) ** -0.5, 1, 64),
    (512, 768, D**-0.5, 4, 64),
)


def adam_kernel(*refs):
    full, small_sum, raw_out, raw_gin = refs[:4]
    mats = refs[4:16]
    smalls = refs[16:25]
    outs = refs[25:41]
    small_outs = refs[41:50]
    out, gin = refs[50:52]
    bufs = refs[52:64]
    lows = refs[64:68]
    g_vm, out_vm, gin_vm, in_sem, out_sem, more_sem = refs[68:]
    g_load = pltpu.make_async_copy(full, g_vm, more_sem.at[2])
    g_load.start()
    loads = {}
    for i, (rows, cols, rate, pieces, tile) in enumerate(MATRICES):
        size = rows // pieces
        for p in range(pieces):
            rs = pl.ds(p * size, size)
            for j in range(3):
                go = pltpu.make_async_copy(
                    mats[3 * i + j].at[rs, :], bufs[3 * i + j].at[rs, :], in_sem.at[i, p, j]
                )
                go.start()
                loads[i, p, j] = go
    passing = [
        pltpu.make_async_copy(raw_out, out_vm, more_sem.at[0]),
        pltpu.make_async_copy(raw_gin, gin_vm, more_sem.at[1]),
    ]
    moves = [
        pltpu.make_async_copy(out_vm, out, more_sem.at[3]),
        pltpu.make_async_copy(gin_vm, gin, more_sem.at[4]),
    ]
    for go in passing:
        go.start()
    stores = []
    g_load.wait()
    for i, (rows, cols, rate, pieces, tile) in enumerate(MATRICES):
        size = rows // pieces
        bw, bm, bv = bufs[3 * i : 3 * i + 3]
        low = lows[i]
        spreads = [spread(part) for part in range(3)] if i == 3 else None
        for p in range(pieces):
            for j in range(3):
                loads[i, p, j].wait()

            def body(first, tile, i=i, p=p, bw=bw, bm=bm, bv=bv, low=low, rate=rate, size=size, spreads=spreads):
                rs = pl.ds(p * size + first, tile)
                if i == 0:
                    g = [
                        g_vm[pl.ds(DOWN + (p // 2 * 2 + j) * 512 + p % 2 * size + first, tile), :]
                        for j in range(2)
                    ]
                elif i == 1:
                    g = [g_vm[pl.ds(UP + j * 512 + p * size + first, tile), :] for j in range(4)]
                elif i == 2:
                    g = [g_vm[pl.ds(OUT + j * 256 + p * size + first, tile), :] for j in range(2)]
                else:
                    g = None
                    for part in range(3):
                        own = g_vm[pl.ds(IN + part * 512 + p * size + first, tile), :]
                        term = nn(own, spreads[part])
                        g = term if g is None else g + term
                if i < 3:
                    g = jnp.concatenate(g, axis=1).astype(f32)
                w, m, v = adam_tile(bw[rs, :], bm[rs, :], bv[rs, :], g, rate, 0.05)
                bw[rs, :] = w
                bm[rs, :] = m
                bv[rs, :] = v
                low[rs, :] = w.astype(bf16)

            tile_loop(size, tile, body)
            rs = pl.ds(p * size, size)
            for j, src in enumerate((bw, bm, bv, low)):
                go = pltpu.make_async_copy(
                    src.at[rs, :], outs[4 * i + j].at[rs, :], out_sem.at[i, p, j]
                )
                go.start()
                stores.append(go)
        if i == 0:
            for come, go in zip(passing, moves):
                come.wait()
                go.start()
    x = lax.axis_index("tensor")
    mine = pl.ds(pl.multiple_of(x * 256, 256), 256)
    g_small = small_sum[:, mine]
    both = small_sum[16:20, :]
    first = jnp.where(x == 0, 1.0, 0.0)
    g_bias = jnp.concatenate(
        [
            (both[j : j + 1, :] * first + both[2 + j : 3 + j, :] * (1.0 - first))
            for j in range(2)
        ],
        axis=1,
    )
    for i, (g, rate, decay) in enumerate(
        ((g_small[0:9], 2.0, 0.05), (g_bias, 0.3, 0.0), (g_small[9:16], 0.3, 0.0))
    ):
        w = smalls[3 * i][...] if i < 2 else smalls[6][:, mine]
        new = adam(w, smalls[3 * i + 1][...], smalls[3 * i + 2][...], g, rate, decay)
        for j in range(3):
            small_outs[3 * i + j][...] = new[j]
    for go in stores + moves:
        go.wait()


def adam_step(full, small_sum, raw_out, raw_gin, mats, smalls):
    S = jax.ShapeDtypeStruct
    V = pltpu.VMEM
    mat_shapes = [shape[:2] for shape in MATRICES]
    any_spec = pl.BlockSpec(memory_space=pl.ANY)
    vmem_spec = pl.BlockSpec(memory_space=V)
    small_shapes = [(9, 256)] * 3 + [(1, 1024)] * 3 + [(7, 256)] * 3
    return pl.pallas_call(
        adam_kernel,
        out_shape=tuple(
            S(shape, kind) for shape in mat_shapes for kind in (f32, f32, f32, bf16)
        )
        + tuple(S(shape, f32) for shape in small_shapes)
        + (S(raw_out.shape, bf16), S(raw_gin.shape, f32)),
        in_specs=[any_spec, vmem_spec, any_spec, any_spec] + [any_spec] * 12 + [vmem_spec] * 9,
        out_specs=[any_spec] * 16 + [vmem_spec] * 9 + [any_spec] * 2,
        scratch_shapes=[V(shape, f32) for shape in mat_shapes for _ in range(3)]
        + [V(shape, bf16) for shape in mat_shapes]
        + [
            V((GROWS, 256), bf16),
            V(raw_out.shape, bf16),
            V(raw_gin.shape, f32),
            pltpu.SemaphoreType.DMA((4, 4, 3)),
            pltpu.SemaphoreType.DMA((4, 4, 4)),
            pltpu.SemaphoreType.DMA((5,)),
        ],
        compiler_params=pltpu.CompilerParams(vmem_limit_bytes=62 * 1024 * 1024),
    )(full, small_sum, raw_out, raw_gin, *mats, *smalls)


CHUNKS = (
    (0, 1024),
    (2048, 1024),
    (1024, 1024),
    (3072, 1024),
    (4096, 512),
    (5632, 512),
    (5120, 512),
    (4608, 512),
)
LATE = 5
SLOTS = 12
PLAN = {
    'U0': ((0, 0),),
    'f0': ((1, 0),),
    'f3': ((0, 1),),
    'D1': ((1, 1),),
    'U1': ((2, 0),),
    'd0': ((3, 0),),
    'd1': ((2, 1),),
    'd2': ((3, 1), (0, 2),),
    'r0': ((4, 0),),
    'r1': ((1, 2),),
    'r2': ((4, 1), (0, 3),),
    'r6': ((2, 2), (1, 3),),
    'A2': ((0, 4),),
    'A1': ((5, 0),),
    'A0': ((6, 0),),
    'r8': ((7, 0), (5, 1), (3, 2), (6, 1), (2, 3),),
    'r9': ((7, 1), (1, 4),),
    'r10': ((4, 2),),
    'r11': ((0, 5),),
    'r12': ((3, 3),),
    'r13': ((4, 3), (2, 4),),
    'r15': ((1, 5), (0, 6),),
    'B1': ((5, 2),),
    'B0': ((6, 2), (3, 4), (7, 2), (0, 7), (5, 3),),
    's0': ((6, 3), (4, 4), (7, 3), (1, 6),),
    's2': ((5, 4), (2, 5), (1, 7),),
    's3': ((6, 4),),
    'N': ((3, 5), (7, 4),),
    'R': ((4, 5),),
}
TAIL = (
    (5, 5), (2, 6), (6, 5), (2, 7), (7, 5), (3, 6),
    (4, 6), (5, 6), (3, 7), (4, 7), (6, 6), (7, 6),
    (5, 7), (5, 8), (6, 7), (6, 8), (7, 7), (7, 8),
)


ITEMS = ((0, 0, 64), (0, 64, 64), (1, 0, 64), (2, 0, 64), (2, 64, 64), (3, 0, 128), (3, 128, 128))


class Traffic:
    def __init__(self, images, refs):
        (self.tok, self.cot, self.w_in, self.w_out, self.w_up, self.w_down, self.taps, self.bias,
         self.out, self.gin, self.full, self.small_sum,
         self.gin_v, self.grads, self.gsmall, self.wi, self.wo, self.wu, self.wd, self.small,
         self.at_s, self.af_s, self.da_s, self.gp_s, self.mf_s, self.nb_s, self.lb_s, self.out_v,
         self.cores, self.xs, self.ys, self.zs, self.firsts,
         self.small_in, self.small_z, self.send, self.recv, self.ssend, self.srecv,
         self.wsend, self.wrecv, self.load, self.save) = refs
        self.images = images
        dp, x = lax.axis_index("dp"), lax.axis_index("tensor")
        core, y, z = lax.rem(dp, 2), lax.rem(dp // 2, 2), dp // 4

        def at(zz, yy, cc, xx):
            return ((zz * 2 + yy) * 2 + cc, xx)

        self.x, self.core, self.y, self.z = x, core, y, z
        self.core_mate = at(z, y, 1 - core, x)
        self.x_mate = at(z, y, core, 1 - x)
        self.y_mate = at(z, 1 - y, core, x)
        self.z_others = [lax.rem(z + k, 4) for k in range(1, 4)]
        self.z_mates = [at(o, y, core, x) for o in self.z_others]
        quarter = y * 2 + core
        self.quarter = quarter

        def load(i, src, dst):
            return pltpu.make_async_copy(src, dst, self.load.at[i])

        w_in, w_out, w_up, w_down = self.w_in, self.w_out, self.w_up, self.w_down
        at_s, af_s, da_s, mf_s, gin = self.at_s, self.af_s, self.da_s, self.mf_s, self.gin_v
        q_in, q_out = aligned(quarter * 128, 128), aligned(quarter * 64, 64)
        q_down = aligned(quarter * 256, 256)
        self.early = [
            load(0, w_in.at[q_in, 0:256], at_s.at[0:128, 0:256]),
            load(1, w_in.at[q_in, 256:512], at_s.at[0:128, 256:512]),
            load(2, w_in.at[q_in, 512:768], at_s.at[128:256, 0:256]),
            load(3, w_out.at[q_out, :], at_s.at[256:320, :]),
            load(4, w_up.at[q_in, 0:512], at_s.at[320:448, :]),
            load(5, w_up.at[q_in, 512:1024], at_s.at[448:576, :]),
            load(6, w_down.at[q_down, :], at_s.at[576:832, :]),
        ]
        self.own_in = [
            load(7, w_in.at[:, 0:256], mf_s.at[0, 0:512, :]),
            load(8, w_in.at[:, 256:512], mf_s.at[1, 0:512, :]),
            load(9, w_in.at[:, 512:768], gin.at[0:512, 0:256]),
        ]
        self.tok_load = load(10, self.tok, self.nb_s.at[0 : images * WIN, :])
        self.cot_load = load(11, self.cot, self.lb_s.at[0 : images * WIN, :])
        self.own_rest = [
            load(12, w_out.at[:, 0:256], gin.at[0:256, 256:512]),
            load(13, w_out.at[:, 256:512], gin.at[256:512, 256:512]),
            load(14, w_up.at[:, 0:512], da_s.at[0:512, :]),
            load(15, w_up.at[:, 512:1024], af_s.at[0:512, :]),
            load(16, w_down.at[0:256, :], da_s.at[512:768, :]),
            load(17, w_down.at[256:512, :], af_s.at[512:768, :]),
            load(18, w_down.at[512:768, :], gin.at[512:768, :]),
            load(19, w_down.at[768:896, :], da_s.at[768:896, :]),
            load(20, w_down.at[896:1024, :], af_s.at[768:896, :]),
        ]


    def weight_copy(self, src, dst, item, slot, mate):
        return pltpu.make_async_remote_copy(
            src_ref=src,
            dst_ref=dst,
            send_sem=self.wsend.at[item, slot],
            recv_sem=self.wrecv.at[item, slot],
            device_id=mate,
            device_id_type=MESH,
        )

    def view(self, item, half, yy, cc):
        kind, first, size = ITEMS[item]
        quarter = yy * 2 + cc
        if kind == 0:
            return self.wi.at[half, :, aligned(quarter * 128 + first, size), :]
        ref, rows = ((self.wo, 64), (self.wu, 128), (self.wd, 256))[kind - 1]
        return ref.at[half, aligned(quarter * rows + first, size), :]

    def crossing(self, item):
        if item == len(ITEMS):
            own = self.small.at[self.x]
        else:
            own = self.view(item, self.x, self.y, self.core)
        return self.weight_copy(own, own, item, 0, self.x_mate)

    def inward(self, item):
        got = self.view(item, 1 - self.x, self.y, self.core)
        return self.weight_copy(got, got, item, 1, self.core_mate)

    def aside(self, item):
        got = self.view(item, 1 - self.x, self.y, self.core)
        return self.weight_copy(got, got, item, 2, self.y_mate)

    def onward(self, item):
        got = self.view(item, 1 - self.x, 1 - self.y, self.core)
        return self.weight_copy(got, got, item, 3, self.core_mate)

    def permuted(self, pieces, rows):
        low = jnp.concatenate(pieces, axis=1).astype(bf16)
        for part in range(3):
            for j in range(2):
                four = nn(low[:, j * 384 : (j + 1) * 384], spread_four(part))
                self.wi[self.x, part, rows, j * 128 : (j + 1) * 128] = four.astype(bf16)

    def begin(self):
        for go in self.early[0:3]:
            go.start()
        barrier = pltpu.get_barrier_semaphore()
        for mate in (self.core_mate, self.x_mate, self.y_mate, *self.z_mates):
            pl.semaphore_signal(barrier, inc=1, device_id=mate, device_id_type=MESH)
        for go in self.early[3:]:
            go.start()
        self.tok_load.start()
        for go in self.own_in:
            go.start()
        x, quarter, at_s = self.x, self.quarter, self.at_s
        self.small[x, 0:9, :] = self.taps[...]
        for j in range(4):
            self.small[x, 9 + j : 10 + j, :] = self.bias[:, j * 256 : (j + 1) * 256]
        for go in self.early[0:3]:
            go.wait()
        self.permuted(
            [at_s[0:128, 0:256], at_s[0:128, 256:512], at_s[128:256, 0:256]],
            aligned(quarter * 128, 128),
        )
        pl.semaphore_wait(barrier, 6)
        self.crossing(0).start()
        self.crossing(1).start()
        self.crossing(len(ITEMS)).start()
        self.early[3].wait()
        self.wo[x, aligned(quarter * 64, 64), :] = at_s[256:320, :].astype(bf16)
        self.crossing(2).start()
        for go in self.early[4:6]:
            go.wait()
        rows = aligned(quarter * 128, 128)
        self.wu[x, rows, 0:512] = at_s[320:448, :].astype(bf16)
        self.wu[x, rows, 512:1024] = at_s[448:576, :].astype(bf16)
        self.crossing(3).start()
        self.crossing(4).start()
        self.early[6].wait()
        self.wd[x, aligned(quarter * 256, 256), :] = at_s[576:832, :].astype(bf16)
        self.crossing(5).start()
        self.crossing(6).start()
        self.cot_load.start()
        for go in self.own_rest:
            go.start()

    def tokens(self):
        self.tok_load.wait()

    def others(self, body):
        for j in range(4):

            @pl.when(self.quarter != j)
            def _(j=j):
                body(j)

    def weights(self):
        for go in self.own_in:
            go.wait()
        mf_s, gin = self.mf_s, self.gin_v

        def body(j):
            rows = slice(j * 128, (j + 1) * 128)
            self.permuted([mf_s[0, rows, :], mf_s[1, rows, :], gin[rows, 0:256]], rows)

        self.others(body)

    def passed(self, *items):
        for item in items:
            self.crossing(item).wait()
            self.inward(item).start()
            self.aside(item).start()

    def turned(self, *items):
        for item in items:
            self.aside(item).wait()
            self.onward(item).start()

    def done(self, *items):
        for item in items:
            self.inward(item).wait()
            self.onward(item).wait()

    def fore(self, i):
        last = self.images - 1
        for k, steps in {
            0: (("passed", 0), ("passed", 1)),
            1: (("turned", 0), ("passed", 2)),
            2: (("turned", 1),),
            last: (("done", 0), ("done", 1), ("passed", 3)),
            last + 1: (("turned", 2), ("passed", 4)),
            last + 2: (("turned", 3),),
            last + 3: (("passed", 5),),
            last + 4: (("turned", 4), ("passed", 6)),
        }.items():

            @pl.when(i == k)
            def _(k=k, steps=steps):
                for name, item in steps:
                    {"passed": self.passed, "turned": self.turned, "done": self.done}[name](item)
                if k == last:
                    self.crossing(len(ITEMS)).wait()

    def cotangent(self):
        self.done(2)
        for go in self.own_rest:
            go.wait()
        x, gin, da_s, af_s = self.x, self.gin_v, self.da_s, self.af_s

        def body(j):
            rows = slice(j * 64, (j + 1) * 64)
            self.wo[x, rows, 0:256] = gin[rows, 256:512].astype(bf16)
            self.wo[x, rows, 256:512] = gin[j * 64 + 256 : (j + 1) * 64 + 256, 256:512].astype(bf16)
            rows = slice(j * 128, (j + 1) * 128)
            self.wu[x, rows, 0:512] = da_s[rows, :].astype(bf16)
            self.wu[x, rows, 512:1024] = af_s[rows, :].astype(bf16)
            rows = slice(j * 256, (j + 1) * 256)
            if j < 3:
                self.wd[x, rows, :] = (da_s, af_s, gin)[j][512:768, :].astype(bf16)
            else:
                self.wd[x, 768:896, :] = da_s[768:896, :].astype(bf16)
                self.wd[x, 896:1024, :] = af_s[768:896, :].astype(bf16)

        self.others(body)
        self.cot_load.wait()

    def near(self):
        self.turned(5, 6)

    def arrived(self):
        self.done(3, 4, 5, 6)


    def output(self):
        self.out_v[...] = self.gin_v[...].astype(bf16)
        self.saving(0).start()

    def saving(self, i):
        src, dst = (
            (self.out_v, self.out),
            (self.gin_v, self.gin),
        )[i]
        return pltpu.make_async_copy(src, dst, self.save.at[i])

    def finished(self):
        self.saving(1).start()

    def keeping(self, c):
        base, R = CHUNKS[c]
        rows = pl.ds(base, R)
        return pltpu.make_async_copy(
            self.grads.at[0, rows, :], self.full.at[rows, :], self.save.at[2 + c]
        )


    def copy(self, src, dst, chunk, slot, mate):
        return pltpu.make_async_remote_copy(
            src_ref=src,
            dst_ref=dst,
            send_sem=self.send.at[chunk, slot],
            recv_sem=self.recv.at[chunk, slot],
            device_id=mate,
            device_id_type=MESH,
        )

    def flights(self, c, s):
        base, R = CHUNKS[c]
        half, quarter, piece = R // 2, R // 4, R // 16
        x, y, z, core, grads = self.x, self.y, self.z, self.core, self.grads
        mine = base + core * half
        theirs = aligned(base + (1 - core) * half, half)
        if c >= LATE:
            if s == 0:
                src = grads.at[1 - x, theirs, :]
                return [self.copy(src, self.firsts[c - LATE], c, 11, self.core_mate)]
            if s == 1:
                return [self.copy(self.firsts[c - LATE], self.xs[c], c, 1, self.x_mate)]
            if s == 2:
                return [self.copy(grads.at[x, theirs, :], self.cores[c], c, 0, self.core_mate)]
            s -= 1
        else:
            if s == 0:
                return [self.copy(grads.at[:, theirs, :], self.cores[c], c, 0, self.core_mate)]
            if s == 1:
                return [self.copy(self.cores[c].at[1 - x], self.xs[c], c, 1, self.x_mate)]
        if s == 2:
            src = self.xs[c].at[aligned((1 - y) * quarter, quarter), :]
            return [self.copy(src, self.ys[c], c, 2, self.y_mate)]
        if s == 3:
            return [
                self.copy(
                    self.ys[c].at[aligned(self.z_others[k] * piece, piece), :],
                    self.zs[c].at[k],
                    c,
                    3 + k,
                    self.z_mates[k],
                )
                for k in range(3)
            ]
        if s == 4:
            own = grads.at[0, aligned(mine + y * quarter + z * piece, piece), :]
            return [self.copy(own, own, c, 6 + k, self.z_mates[k]) for k in range(3)]
        if s == 5:
            own = grads.at[0, aligned(mine + y * quarter, quarter), :]
            return [self.copy(own, own, c, 9, self.y_mate)]
        if s == 6:
            own = grads.at[0, aligned(mine, half), :]
            return [self.copy(own, own, c, 10, self.core_mate)]
        return []

    def stage(self, c, s):
        base, R = CHUNKS[c]
        half, quarter, piece = R // 2, R // 4, R // 16
        x, y, z, core, grads = self.x, self.y, self.z, self.core, self.grads
        mine = base + core * half
        late = c >= LATE
        if s > 0 and not (late and s == 2):
            for flight in self.flights(c, s - 1):
                flight.wait()
        if late and s == 3:
            self.flights(c, 1)[0].wait()

        def total(*parts):
            out = None
            for part in parts:
                part = part.astype(f32)
                out = part if out is None else out + part
            return out.astype(bf16)

        cores, xs, ys, zs = self.cores[c], self.xs[c], self.ys[c], self.zs[c]
        step = s - 1 if late else s
        if late and s == 1:
            first = self.firsts[c - LATE]

            def body(i, size):
                rows, own = pl.ds(i, size), aligned(mine + i, size)
                first[rows, :] = total(grads[1 - x, own, :], first[rows, :])

            tile_loop(half, 128, body)
        elif late and s == 3:

            def body(i, size):
                rows, own = pl.ds(i, size), aligned(mine + i, size)
                xs[rows, :] = total(grads[x, own, :], cores[rows, :], xs[rows, :])

            tile_loop(half, 128, body)
        elif not late and s == 1:

            def body(i, size):
                rows, own = pl.ds(i, size), aligned(mine + i, size)
                for t in range(2):
                    cores[t, rows, :] = total(grads[t, own, :], cores[t, rows, :])

            tile_loop(half, 128, body)
        elif not late and s == 2:

            def body(i, size):
                rows = pl.ds(i, size)
                xs[rows, :] = total(cores[x, rows, :], xs[rows, :])

            tile_loop(half, 128, body)
        elif step == 3:

            def body(i, size):
                rows, own = pl.ds(i, size), aligned(y * quarter + i, size)
                ys[rows, :] = total(xs[own, :], ys[rows, :])

            tile_loop(quarter, 128, body)
        elif step == 4:
            own = aligned(z * piece, piece)
            grads[0, aligned(mine + y * quarter + z * piece, piece), :] = total(
                ys[own, :], zs[0], zs[1], zs[2]
            )
        if step == 7:
            self.keeping(c).start()
        for flight in self.flights(c, s):
            flight.start()

    def small_flights(self, s):
        def small_copy(src, dst, slot, mate):
            return pltpu.make_async_remote_copy(
                src_ref=src,
                dst_ref=dst,
                send_sem=self.ssend.at[slot],
                recv_sem=self.srecv.at[slot],
                device_id=mate,
                device_id_type=MESH,
            )

        if s < 3:
            mate = (self.core_mate, self.x_mate, self.y_mate)[s]
            return [small_copy(self.small_z.at[s], self.small_in.at[s], s, mate)]
        return [
            small_copy(self.small_z.at[3], self.small_z.at[4 + self.z], 3 + k, self.z_mates[k])
            for k in range(3)
        ]

    def small_stage(self, s):
        small_z = self.small_z
        if s > 0:
            for flight in self.small_flights(s - 1):
                flight.wait()
        if s == 0:
            small_z[0] = self.gsmall[...]
        elif s <= 3:
            small_z[s] = small_z[s - 1] + self.small_in[s - 1]
        else:
            self.small_sum[...] = (small_z[4] + small_z[5]) + (small_z[6] + small_z[7])
            return
        if s == 3:
            small_z[4 + self.z] = small_z[3]
        for flight in self.small_flights(s):
            flight.start()

    def point(self, name):
        for c, s in PLAN.get(name, ()):
            self.stage(c, s)

    def turn(self, name, n, stride=1, offset=0):
        for j in range(self.images):
            key = name + str(j * stride + offset)
            if key in PLAN:

                @pl.when(n == j)
                def _(key=key):
                    self.point(key)

    def sums(self, k):
        self.small_stage(k)

    def end(self):
        self.small_stage(2)
        for k, (c, s) in enumerate(TAIL):
            self.stage(c, s)
            if k == len(TAIL) // 3:
                self.small_stage(3)
        self.small_stage(4)
        for i in range(2):
            self.saving(i).wait()
        for c in range(len(CHUNKS)):
            self.keeping(c).wait()


def main_kernel(images, counts, tok, cot, w_in, w_out, w_up, w_down, taps, bias, vecs,
                out, gin, full, small_sum, *scratch):
    n = len(block_scratch(images))
    inner, rest = scratch[:n], scratch[n:]
    gin_v, grads, gsmall, wi, wo, wu, wd, small = rest[:8]
    rest = rest[8:]
    count = len(CHUNKS)
    cores, xs, ys, zs = (rest[count * i : count * (i + 1)] for i in range(4))
    rest = rest[4 * count :]
    firsts, rest = rest[: count - LATE], rest[count - LATE :]
    x_s, co_s, at_s, af_s, da_s, gp_s, mf_s, na_s, nb_s, lb_s = inner[:10]
    traffic = Traffic(
        images,
        (tok, cot, w_in, w_out, w_up, w_down, taps, bias, out, gin, full, small_sum,
         gin_v, grads, gsmall, wi, wo, wu, wd, small,
         at_s, af_s, da_s, gp_s, mf_s, nb_s, lb_s, co_s.at[0 : images * WIN, :],
         cores, xs, ys, zs, firsts, *rest),
    )
    x = lax.axis_index("tensor")
    limit = counts[lax.axis_index("dp")] - x * images
    traffic.begin()
    block_body(
        images, limit, x, traffic, wi, wo, wu, wd, small, vecs, gin_v, grads, gsmall, *inner
    )
    traffic.end()


def main_call(counts, tok, cot, w_in, w_out, w_up, w_down, taps, bias, vecs):
    images = tok.shape[0] // WIN
    S = jax.ShapeDtypeStruct
    V = pltpu.VMEM
    away = pl.BlockSpec(memory_space=pl.ANY)
    here = pl.BlockSpec(memory_space=V)
    sizes = [R for _, R in CHUNKS]
    dma = pltpu.SemaphoreType.DMA
    return pl.pallas_call(
        functools.partial(main_kernel, images),
        out_shape=(
            S(tok.shape, bf16),
            S(tok.shape, f32),
            S((GROWS, 256), bf16),
            S((24, D), f32),
        ),
        in_specs=[pl.BlockSpec(memory_space=pltpu.SMEM)] + [away] * 6 + [here] * 3,
        out_specs=[away] * 3 + [here],
        scratch_shapes=block_scratch(images)
        + [
            V(tok.shape, f32),
            V((2, GROWS, 256), bf16),
            V((24, D), f32),
            V((2, 3, D, 256), bf16),
            V((2, 256, D), bf16),
            V((2, D, 1024), bf16),
            V((2, 1024, D), bf16),
            V((2, 16, 256), f32),
        ]
        + [V((2, R // 2, 256), bf16) for R in sizes[:LATE]]
        + [V((R // 2, 256), bf16) for R in sizes[LATE:]]
        + [V((R // 2, 256), bf16) for R in sizes]
        + [V((R // 4, 256), bf16) for R in sizes]
        + [V((3, R // 16, 256), bf16) for R in sizes]
        + [V((R // 2, 256), bf16) for R in sizes[LATE:]]
        + [
            V((3, 24, D), f32),
            V((8, 24, D), f32),
            dma((len(sizes), SLOTS)),
            dma((len(sizes), SLOTS)),
            dma((6,)),
            dma((6,)),
            dma((8, 4)),
            dma((8, 4)),
            dma((21,)),
            dma((2 + len(sizes),)),
        ],
        compiler_params=pltpu.CompilerParams(
            collective_id=1, has_side_effects=True, vmem_limit_bytes=63 * 1024 * 1024
        ),
    )(counts, tok, cot, w_in, w_out, w_up, w_down, taps, bias, vecs)


def local(
    tokens, cotangent, image_counts,
    w_in, m_in, v_in, w_out, m_out, v_out, w_up, m_up, v_up, w_down, m_down, v_down,
    kernel, m_kernel, v_kernel, up_bias, m_bias, v_bias, vectors, m_vectors, v_vectors,
):
    biases = tuple(a.reshape(1, -1) for a in (up_bias, m_bias, v_bias))
    raw_out, raw_gin, full, small_sum = main_call(
        image_counts, tokens, cotangent, w_in, w_out, w_up, w_down, kernel, biases[0], vectors
    )
    new = adam_step(
        full,
        small_sum,
        raw_out,
        raw_gin,
        (w_down, m_down, v_down, w_up, m_up, v_up, w_out, m_out, v_out, w_in, m_in, v_in),
        (kernel, m_kernel, v_kernel)
        + biases
        + (vectors, m_vectors, v_vectors),
    )
    down, up, mid, first = new[:4], new[4:8], new[8:12], new[12:16]
    bias = tuple(a.reshape(-1) for a in new[19:22])
    return (*new[25:27], *first, *mid, *up, *down, *new[16:19], *bias, *new[22:25])


def general(
    tokens, cotangent, image_counts,
    w_in, m_in, v_in, w_out, m_out, v_out, w_up, m_up, v_up, w_down, m_down, v_down,
    kernel, m_kernel, v_kernel, up_bias, m_bias, v_bias, vectors, m_vectors, v_vectors,
):
    images = tokens.shape[0] // WIN
    place = lax.axis_index("tensor")
    live = image_counts[lax.axis_index("dp")] - place * images

    def whole(a, axis):
        return lax.all_gather(a, "tensor", axis=axis, tiled=True)

    wi = whole(w_in.astype(bf16), 1).reshape(D, 2, 8, 3, HD).transpose(1, 3, 0, 2, 4)
    wi = wi.reshape(2, 3, D, 256)
    wo = whole(w_out.astype(bf16), 0).reshape(2, 256, D)
    wd = whole(w_down.astype(bf16), 0).reshape(2, 1024, D)
    wu = whole(w_up.astype(bf16), 1).reshape(D, 2, 1024).transpose(1, 0, 2)
    small = jnp.concatenate(
        [
            whole(kernel, 1).reshape(9, 2, 256).transpose(1, 0, 2),
            whole(up_bias, 0).reshape(2, 4, 256),
            jnp.zeros((2, 3, 256), f32),
        ],
        axis=1,
    )
    out, grad_in, grads, gs = block(
        live.reshape(1), tokens, cotangent, wi, wo, wu, wd, small, vectors
    )
    grads = grads.astype(f32)

    def columns(first, rows, count):
        part = grads[:, first : first + rows * count].reshape(2, count, rows, 256)
        return part

    g_down = grads[:, DOWN:UP].reshape(2, 2, 2, 512, 256).transpose(0, 1, 3, 2, 4).reshape(FF, D)
    g_up = columns(UP, 512, 4).transpose(2, 0, 1, 3).reshape(D, FF)
    g_out = columns(OUT, 256, 2).transpose(0, 2, 1, 3).reshape(D, D)
    g_in = columns(IN, 512, 3).reshape(2, 3, D, 8, HD).transpose(2, 0, 3, 1, 4).reshape(D, 3 * D)

    def owned(a, axis):
        return lax.psum(lax.psum_scatter(a, "tensor", scatter_dimension=axis, tiled=True), "dp")

    g_in, g_out, g_up, g_down = owned(g_in, 1), owned(g_out, 0), owned(g_up, 1), owned(g_down, 0)
    g_kernel, g_bias, g_vectors = owned(gs[0:9], 1), owned(gs[16:20].reshape(-1), 0), owned(gs[9:16], 1)
    vector_width = m_vectors.shape[1]
    own_vectors = lax.dynamic_slice_in_dim(vectors, place * vector_width, vector_width, 1)
    results = [out, grad_in]
    for w, m, v, g, rate in (
        (w_in, m_in, v_in, g_in, D**-0.5),
        (w_out, m_out, v_out, g_out, (D // HD) ** -0.5),
        (w_up, m_up, v_up, g_up, D**-0.5),
        (w_down, m_down, v_down, g_down, FF**-0.5),
    ):
        new = adam(w, m, v, g, rate, 0.05)
        results += [*new, new[0].astype(bf16)]
    results += adam(kernel, m_kernel, v_kernel, g_kernel, 2.0, 0.05)
    results += adam(up_bias, m_bias, v_bias, g_bias, 0.3, 0.0)
    results += adam(own_vectors, m_vectors, v_vectors, g_vectors, 0.3, 0.0)
    return tuple(results)


def solution(mesh):
    rows, columns = P("tensor", None), P(None, "tensor")
    tokens = P(("dp", "tensor"), None)
    mats = (columns,) * 3 + (rows,) * 3 + (columns,) * 3 + (rows,) * 3
    news = (columns,) * 4 + (rows,) * 4 + (columns,) * 4 + (rows,) * 4
    pairs = mesh.shape["dp"] == 16 and mesh.shape["tensor"] == 2
    return jax.shard_map(
        local if pairs else general,
        mesh=mesh,
        in_specs=(tokens, tokens, P(), *mats)
        + (columns,) * 3
        + (P("tensor"),) * 3
        + (P(), columns, columns),
        out_specs=(tokens, tokens, *news) + (columns,) * 3 + (P("tensor"),) * 3 + (columns,) * 3,
        check_vma=False,
    )
```
